32 devices in a mesh: dp: 2 (over x), expert: 4 (over z), head: 4 (over y, core).
Axes of the slice: x: 2, y: 2, z: 4, core: 2. Of those that a mesh axis runs over, the one named last changes fastest.
Arguments:
- inputs: bfloat16 [16, 784, 768], P(('dp', 'expert')), may hold values from -6 to 6
- w_qkv: bfloat16 [768, 3, 768], P(('dp', 'expert'), None, 'head'), may hold values from -0.21875 to 0.21875
- w_out: bfloat16 [768, 768], P('head', ('dp', 'expert')), may hold values from -0.875 to 0.875
- w_router: bfloat16 [768, 4], P(('dp', 'expert')), may hold values from -0.109375 to 0.109375
- gain_one: float32 [768], P(('dp', 'expert')), may hold values from 0.1 to 1.9
- gain_two: float32 [768], P(('dp', 'expert')), may hold values from 0.1 to 1.9
- w_in: bfloat16 [4, 768, 3072], P('expert', 'dp', 'head'), may hold values from -0.21875 to 0.21875
- w_back: bfloat16 [4, 3072, 768], P('expert', 'head', 'dp'), may hold values from -0.4375 to 0.4375
- experts: int32 [16, 784, 2], P(('dp', 'expert')), may hold values from 0 to 3, all different within a row
- priority: int32 [16, 784], P(('dp', 'expert')), may hold values from 0 to 783, each once within a row
- cotangent: bfloat16 [16, 784, 768], P(('dp', 'expert')), may hold values from -6 to 6
Outputs:
- mixed: bfloat16 [16, 784, 768], P(('dp', 'expert'), 'head')
- grad_inputs: bfloat16 [16, 784, 768], P(('dp', 'expert'))
- grad_qkv: float32 [768, 3, 768], P(('dp', 'expert'), None, 'head')
- grad_w_out: float32 [768, 768], P('head', ('dp', 'expert'))
- grad_router: float32 [768, 4], P(('dp', 'expert'))
- grad_gain_one: float32 [768], P(('dp', 'expert'))
- grad_gain_two: float32 [768], P(('dp', 'expert'))
- grad_w_in: float32 [4, 768, 3072], P('expert', 'dp', 'head')
- grad_w_back: float32 [4, 3072, 768], P('expert', 'head', 'dp')
The draws below stay inside these ranges and needn't reach their ends.
Inputs may be any that keep to these rules, and one draw needn't show every extreme that they name: Each token names two different experts; every expert is named by some token. Each row of priority holds every one of the 784 ranks once.
All inputs are finite; a program needn't handle non-finite values.
Results may differ from the reference program's by a relative error of at most 0.038.
Values may be sent and summed in bfloat16 or wider, within the bound.
A program may use at most 192 MiB of HBM per device.

```python
import jax
import jax.numpy as jnp
from jax import lax

D = 768
HEADS = 12
HD = 64
FF = 3072
SEQ = 196
E = 4
M = 784
CAP = 196
NBLK = 16
N_HEAD = 4


def block_levels(own_key, extent, cuts, least, largest):
    gain, own = 1.0, jax.random.fold_in(own_key, 6)
    for dim, parts in cuts:
        heights = jnp.exp(jax.random.uniform(jax.random.fold_in(own, dim), (parts,), jnp.float32, least / len(cuts), largest / len(cuts)))
        gain = gain * jnp.repeat(heights, extent[dim] // parts).reshape([-1 if axis == dim else 1 for axis in range(len(extent))])
    return gain


def picks_of(key, rows, amount, top, lift):
    sequence = jax.random.permutation(jax.random.fold_in(key, 1), amount)
    boost = sequence
    for power in range(3):
        boost = boost * boost // amount
    boost = boost * lift // amount
    lots = jax.random.randint(jax.random.fold_in(key, 2), (rows, amount), 0, 4096) + boost
    sure = jax.random.permutation(jax.random.fold_in(key, 3), rows)[jnp.arange(amount) % rows]
    lots = jnp.where(jnp.arange(rows)[:, None] == sure[None, :], 1 << 14, lots)
    score = lots * amount + jnp.arange(amount)
    return lax.top_k(score.astype(jnp.int32), top)[1].astype(jnp.int32)


def normal_values(stream_key, dims, spread, limit, cuts=(), kind=jnp.bfloat16):
    drawn = spread * jax.random.normal(stream_key, dims, jnp.float32)
    if cuts:
        drawn = drawn * block_levels(stream_key, dims, cuts, -0.22, 0.18)
    return jnp.clip(drawn, -limit, limit).astype(kind)


def setup_inputs(seed: int = 0) -> dict:
    splits = jax.random.split(jax.random.key(seed), 12)
    inputs = normal_values(splits[0], (NBLK, M, D), 1.0, 6.0, ((0, 8),))
    w_qkv = normal_values(splits[1], (D, 3, D), D ** -0.5, 0.21875, ((0, 8), (2, 4)))
    w_out = normal_values(splits[2], (D, D), (D // 16) ** -0.5, 0.875, ((0, 4), (1, 8)))
    w_router = normal_values(splits[3], (D, E), (4 * D) ** -0.5, 0.109375, ((0, 8),))
    gain_one = jnp.clip(1.0 + 0.18 * jax.random.normal(splits[4], (D,), jnp.float32), 0.1, 1.9)
    gain_two = jnp.clip(1.0 + 0.18 * jax.random.normal(splits[5], (D,), jnp.float32), 0.1, 1.9)
    w_in = normal_values(splits[6], (E, D, FF), D ** -0.5, 0.21875, ((0, 4), (1, 2), (2, 4)))
    w_back = normal_values(splits[7], (E, FF, D), (max(1, FF // (E * E))) ** -0.5, 0.4375, ((0, 4), (1, 4), (2, 2)))
    experts = picks_of(splits[8], NBLK * M, E, 2, 4096).reshape((NBLK, M, 2))
    priority = jax.vmap(lambda own: jax.random.permutation(own, M))(jax.random.split(splits[9], NBLK)).reshape((NBLK, M)).astype(jnp.int32)
    cotangent = normal_values(splits[10], (NBLK, M, D), 1.0, 6.0, ((0, 8),))
    return dict(inputs=inputs, w_qkv=w_qkv, w_out=w_out, w_router=w_router, gain_one=gain_one, gain_two=gain_two, w_in=w_in, w_back=w_back, experts=experts, priority=priority, cotangent=cotangent)


@jax.custom_vjp
def low(v):
    return lax.optimization_barrier(v.astype(jnp.bfloat16)).astype(jnp.float32)

@jax.custom_vjp
def low_back(v):
    return v

def low_keep(v):
    return (low(v), None)

def low_pass(kept, grad):
    return (grad,)

def back_keep(v):
    return (v, None)

def back_low(kept, grad):
    return (low(grad),)
low.defvjp(low_keep, low_pass)
low_back.defvjp(back_keep, back_low)

def normalize(values):
    centered = values - lax.optimization_barrier(jnp.mean(values, axis=1, keepdims=True))
    inverse = lax.rsqrt(lax.optimization_barrier(jnp.mean(centered * centered, axis=1, keepdims=True)) + 1e-06)
    return centered * inverse

def route_slots(chosen, ranks, expert_count, capacity):
    total_rows = ranks.shape[0]
    positions = jnp.arange(total_rows, dtype=jnp.int32)
    by_rank = jnp.zeros((total_rows,), jnp.int32).at[ranks].set(positions)
    ordered = jnp.concatenate([chosen[by_rank, 0], chosen[by_rank, 1]])
    onehot = (ordered[:, None] == jnp.arange(expert_count, dtype=jnp.int32)[None, :]).astype(jnp.int32)
    earlier = jnp.cumsum(onehot, axis=0) - onehot
    seq_slot = lax.optimization_barrier(jnp.sum(earlier * onehot, axis=1))
    slot_pos = jnp.stack([seq_slot[ranks], seq_slot[total_rows + ranks]], axis=1)
    kept_mask = slot_pos < capacity
    target = jnp.where(kept_mask, chosen * capacity + slot_pos, expert_count * capacity).astype(jnp.int32)
    return (kept_mask, target)

def block_forward(weights, pieces):
    w_qkv, w_out, w_router, gain_one, gain_two, w_in, w_back = weights
    tokens, chosen, ranks = pieces
    highest = lax.Precision.HIGHEST
    row_count = tokens.shape[0]
    images = row_count // SEQ
    score_scale = HD ** (-0.5)
    act_one = low(normalize(tokens) * gain_one)
    projected = jnp.einsum('md,dsh->msh', act_one, w_qkv, precision=highest)
    query = low_back(low(projected[:, 0] * score_scale)).reshape(images, SEQ, HEADS, HD)
    key_part = low_back(low(projected[:, 1])).reshape(images, SEQ, HEADS, HD)
    value_part = low_back(low(projected[:, 2])).reshape(images, SEQ, HEADS, HD)
    scores = low_back(jnp.einsum('ishd,ithd->ihst', query, key_part, precision=highest))
    probs_low = low(jax.nn.softmax(scores, axis=-1))
    attended = jnp.einsum('ihst,ithd->ishd', probs_low, value_part, precision=highest).reshape(row_count, D)
    attended = low_back(low(attended))
    attn_out = low_back(jnp.dot(attended, w_out, precision=highest))
    hidden = tokens + attn_out
    act_two = low(normalize(hidden) * gain_two)
    logits = low_back(jnp.dot(act_two, w_router, precision=highest))
    router_probs = jax.nn.softmax(logits, axis=1)
    kept_mask, target = route_slots(chosen, ranks, E, CAP)
    choice_hot = (chosen[:, :, None] == jnp.arange(E, dtype=jnp.int32)[None, None, :]).astype(jnp.float32)
    live_gates = lax.optimization_barrier(jnp.sum(choice_hot * router_probs[:, None, :], axis=2)) * kept_mask.astype(jnp.float32)
    slots_total = E * CAP
    packed = jnp.zeros((slots_total + 1, D), jnp.float32).at[target[:, 0]].set(act_two).at[target[:, 1]].set(act_two)
    dispatched = packed[:slots_total].reshape(E, CAP, D)
    part_width = FF // N_HEAD
    mixed = hidden
    for quarter in range(N_HEAD):
        in_part = lax.slice_in_dim(w_in, quarter * part_width, (quarter + 1) * part_width, axis=2)
        back_part = lax.slice_in_dim(w_back, quarter * part_width, (quarter + 1) * part_width, axis=1)
        pre_act = low_back(jnp.einsum('ecd,edf->ecf', low_back(dispatched), in_part, precision=highest))
        act_part = low(jax.nn.gelu(pre_act, approximate=True))
        part_out = low_back(low(jnp.einsum('ecf,efd->ecd', act_part, back_part, precision=highest)))
        extended = jnp.concatenate([part_out.reshape(slots_total, D), jnp.zeros((1, D), jnp.float32)], axis=0)
        mixed = mixed + lax.optimization_barrier(jnp.sum(live_gates[:, :, None] * extended[target], axis=1))
    return mixed

def reference(inputs, w_qkv, w_out, w_router, gain_one, gain_two, w_in, w_back, experts, priority, cotangent):
    weights = (w_qkv.astype(jnp.float32), w_out.astype(jnp.float32), w_router.astype(jnp.float32), gain_one.astype(jnp.float32), gain_two.astype(jnp.float32), w_in.astype(jnp.float32), w_back.astype(jnp.float32))
    tokens_all = inputs.astype(jnp.float32)
    saved_block = jax.checkpoint(block_forward)

    def forward(weight_set, token_set):

        def one_block(pieces):
            return saved_block(weight_set, pieces)
        return lax.map(one_block, (token_set, experts, priority))
    mixed, pullback = jax.vjp(forward, weights, tokens_all)
    grad_weights, grad_tokens = pullback(cotangent.astype(jnp.float32))
    return (mixed.astype(jnp.bfloat16), grad_tokens.astype(jnp.bfloat16), grad_weights[0], grad_weights[1], grad_weights[2], grad_weights[3], grad_weights[4], grad_weights[5], grad_weights[6])
```

```python
import functools
import types

import jax
import jax.numpy as jnp
from jax import lax
from jax.experimental import pallas as pl
from jax.experimental.pallas import tpu as pltpu
from jax.sharding import PartitionSpec as P

HD = 64
SEQ = 196
MESH = pl.DeviceIdType.MESH
F32, BF16 = jnp.float32, jnp.bfloat16
LIMIT = 62 * 2**20


def up16(n):
    return -(-n // 16) * 16


def nn(a, b):
    return lax.dot_general(a, b, (((1,), (0,)), ((), ())), preferred_element_type=F32)


def nt(a, b):
    return lax.dot_general(a, b, (((1,), (1,)), ((), ())), preferred_element_type=F32)


def tn(a, b):
    return lax.dot_general(a, b, (((0,), (0,)), ((), ())), preferred_element_type=F32)


def loop(count, body):
    def step(i, carry):
        body(i)
        return carry

    lax.fori_loop(0, count, step, 0)


def iota(shape, dim):
    return lax.broadcasted_iota(jnp.int32, shape, dim)


def fiota(shape, dim):
    return iota(shape, dim).astype(F32)


def normalize(v):
    centered = v - jnp.mean(v, axis=1, keepdims=True)
    inverse = lax.rsqrt(jnp.mean(centered * centered, axis=1, keepdims=True) + 1e-06)
    return centered * inverse, inverse


def norm_backward(upstream, normed, inverse, gain):
    scaled = upstream * gain
    return inverse * (
        scaled
        - jnp.mean(scaled, axis=1, keepdims=True)
        - normed * jnp.mean(scaled * normed, axis=1, keepdims=True)
    )


class Sizes:
    def __init__(self, mesh, model, rows, hidden):
        self.nd, self.ne, self.nh = mesh.shape["dp"], mesh.shape["expert"], mesh.shape["head"]
        self.D, self.DH = model, model // 2
        self.M = rows
        self.CAP = rows // self.ne
        self.CP = up16(self.CAP + 2)
        self.IP = up16(SEQ)
        self.NI = rows // SEQ
        self.TP = self.NI * self.IP
        self.SL = self.ne * self.CP
        self.F = hidden
        self.PR = model // (self.nd * self.ne)
        self.aligned = self.PR % 16 == 0
        self.SG = 1
        while self.SG * 2 * self.CP <= self.IP and self.ne % (self.SG * 2) == 0:
            self.SG *= 2
        self.R = self.SG * 2 * self.CP
        self.LW = model // self.nh
        assert self.nd == 2 and self.nh == 4 and self.NI == 4 and self.LW == 3 * HD
        assert self.ne <= 64 and 0 <= self.CAP - (self.CP - 16) <= 14


class Place:
    def __init__(self, g):
        self.ne = g.ne
        self.d = lax.axis_index("dp")
        self.e = lax.axis_index("expert")
        self.h = lax.axis_index("head")
        self.y = lax.div(self.h, 2)
        self.c = lax.rem(self.h, 2)
        self.oy, self.oc, self.od = 1 - self.y, 1 - self.c, 1 - self.d
        self.hcore = 2 * self.y + self.oc
        self.hy = 2 * self.oy + self.c
        self.hdiag = 2 * self.oy + self.oc
        self.core = (self.d, self.e, self.hcore)
        self.across = (self.d, self.e, self.hy)
        self.diag = (self.d, self.e, self.hdiag)
        self.twin = (self.od, self.e, self.h)

    def other(self, k):
        return lax.rem(self.e + k, self.ne)

    def along(self, e2):
        return (self.d, e2, self.h)

    def enter(self):
        barrier = pltpu.get_barrier_semaphore()

        def tell(device):
            pl.semaphore_signal(barrier, inc=1, device_id=device, device_id_type=MESH)

        for device in (self.core, self.across, self.diag, self.twin):
            tell(device)
        loop(self.ne - 1, lambda k: tell(self.along(self.other(k + 1))))
        pl.semaphore_wait(barrier, 4 + self.ne - 1)


def copy(b, name, src, dst, si, ri, device):
    return pltpu.make_async_remote_copy(
        src_ref=src,
        dst_ref=dst,
        send_sem=getattr(b, name + "_s").at[si],
        recv_sem=getattr(b, name + "_r").at[ri],
        device_id=device,
        device_id_type=MESH,
    )


def send(b, name, src, dst, si, ri, device):
    copy(b, name, src, dst, si, ri, device).start()


def arrived(b, p, name, ref, ri):
    copy(b, name, ref, ref, 0, ri, p.core).wait_recv()


def left(b, p, name, ref, si):
    copy(b, name, ref, ref, si, 0, p.core).wait_send()


def route(g, p, b):
    c = p.c
    pr_row, e0r, e1r = b.mr[c, 2:3, :], b.mr[c, 0:1, :], b.mr[c, 1:2, :]
    lane = fiota((g.IP, 128), 1)
    base = jnp.zeros((1, 128), F32)
    for i in range(g.NI):
        rows = slice(i * g.IP, (i + 1) * g.IP)
        col = b.mc[c, rows, :]
        e0c, e1c, prc = col[:, 0:1], col[:, 1:2], col[:, 2:3]
        b.L[rows, :] = jnp.where(pr_row < prc, 1.0, 0.0).astype(BF16)
        b.O[rows, :] = jnp.where((lane == e0c) | (lane == e1c + 64.0), 1.0, 0.0).astype(BF16)
        base = base + jnp.sum(jnp.where(lane == e0c + 64.0, 1.0, 0.0), axis=0, keepdims=True)
    slot_lane = fiota((g.IP, g.SL), 1)
    for i in range(g.NI):
        rows = slice(i * g.IP, (i + 1) * g.IP)
        col = b.mc[c, rows, :]
        e0c, e1c = col[:, 0:1], col[:, 1:2]
        own = b.O[rows, :].astype(F32)
        earlier = nn(b.L[rows, :], b.O[...])
        s0 = jnp.sum(jnp.where(lane < 64.0, earlier * own, 0.0), axis=1, keepdims=True)
        s1 = jnp.sum(jnp.where(lane < 64.0, 0.0, (earlier + base) * own), axis=1, keepdims=True)
        t0 = jnp.where(s0 < g.CAP, e0c * g.CP + s0, -1.0)
        t1 = jnp.where(s1 < g.CAP, e1c * g.CP + s1, -1.0)
        b.PT[rows, :] = jnp.where((slot_lane == t0) | (slot_lane == t1), 1.0, 0.0).astype(BF16)
    sub = fiota((128, g.TP), 0)
    own = jnp.where((sub == e0r) | (sub == e1r + 64.0), 1.0, 0.0)
    base = jnp.sum(jnp.where(sub == e0r + 64.0, 1.0, 0.0), axis=1, keepdims=True)
    earlier = nt(own.astype(BF16), b.L[...])
    s0 = jnp.sum(jnp.where(sub < 64.0, earlier * own, 0.0), axis=0, keepdims=True)
    s1 = jnp.sum(jnp.where(sub < 64.0, 0.0, (earlier + base) * own), axis=0, keepdims=True)
    t0 = jnp.where(s0 < g.CAP, e0r * g.CP + s0, -1.0)
    t1 = jnp.where(s1 < g.CAP, e1r * g.CP + s1, -1.0)
    slot_sub = fiota((g.CP, g.TP), 0)

    def fill(e2):
        at = slot_sub + (e2 * g.CP).astype(F32)
        b.P[pl.ds(pl.multiple_of(e2 * g.CP, 16), g.CP), :] = jnp.where(
            (at == t0) | (at == t1), 1.0, 0.0
        ).astype(BF16)

    loop(g.ne, fill)


def pack_rows(g, e2):
    return pl.ds(pl.multiple_of(e2 * g.CP, 16), g.CP)


def piece_rows(g, d, e2):
    return pl.ds(pl.multiple_of((d * g.ne + e2) * g.PR, 16), g.PR)


def weights_out(g, p, b):
    own = piece_rows(g, p.d, p.e)
    if g.aligned:
        mine = p.d * g.ne + p.e

        def to_expert(k):
            device = p.along(p.other(k + 1))
            send(b, "wz", b.wp, b.W.at[p.h, own, :], k, p.e, device)
            send(b, "mz", b.mp, b.MI.at[own, :], k, p.e, device)

        loop(g.ne - 1, to_expert)
        send(b, "wx", b.wp, b.W.at[p.h, own, :], p.e, p.e, p.twin)
        send(b, "mx", b.mp, b.MI.at[own, :], p.e, p.e, p.twin)
        send(b, "wy", b.wp, b.W.at[p.h, own, :], mine, mine, p.across)
        send(b, "wc", b.wp, b.W.at[p.h, own, :], mine, mine, p.core)
        b.W[p.h, own, :] = b.wp[...]
        b.MI[own, :] = b.mp[...]
    else:
        send(b, "wy", b.wp, b.W.at[p.h], 0, 0, p.across)
        send(b, "wc", b.wp, b.W.at[p.h], 0, 0, p.core)
        b.W[p.h] = b.wp[...]
        b.MI[...] = b.mp[...]


def weights_on(g, p, b):
    if not g.aligned:
        return

    def relay(k):
        e2 = p.other(k + 1)
        rows = piece_rows(g, p.d, e2)
        at = p.d * g.ne + e2
        part = b.W.at[p.h, rows, :]
        arrived(b, p, "wz", part, e2)
        send(b, "wx", part, part, e2, e2, p.twin)
        send(b, "wy", part, part, at, at, p.across)
        send(b, "wc", part, part, at, at, p.core)
        part = b.MI.at[rows, :]
        arrived(b, p, "mz", part, e2)
        send(b, "mx", part, part, e2, e2, p.twin)

    loop(g.ne - 1, relay)


def weights_end(g, p, b):
    if not g.aligned:
        return

    def relay(k):
        e2 = p.other(k)
        rows = piece_rows(g, p.od, e2)
        at = p.od * g.ne + e2
        part = b.W.at[p.h, rows, :]
        arrived(b, p, "wx", part, e2)
        send(b, "wy", part, part, at, at, p.across)
        send(b, "wc", part, part, at, at, p.core)
        arrived(b, p, "mx", b.MI.at[rows, :], e2)

    loop(g.ne, relay)


def pieces(g):
    return g.nd * g.ne if g.aligned else 1


def piece_of(g, ref, group, i):
    if not g.aligned:
        return ref.at[group]
    return ref.at[group, pl.ds(pl.multiple_of(i * g.PR, 16), g.PR), :]


def group_in(g, p, b, k):
    @pl.when(k == 1)
    def _():
        loop(pieces(g), lambda i: arrived(b, p, "wc", piece_of(g, b.W, p.hcore, i), i))

    @pl.when(k == 2)
    def _():
        def on(i):
            part = piece_of(g, b.W, p.hy, i)
            arrived(b, p, "wy", part, i)
            send(b, "wd", part, part, i, i, p.core)

        loop(pieces(g), on)

    @pl.when(k == 3)
    def _():
        loop(pieces(g), lambda i: arrived(b, p, "wd", piece_of(g, b.W, p.hdiag, i), i))


def masks(rows):
    lane = iota((rows, 128), 1)
    return lane < 64, lane >= 64


def attention(g, p, b):
    low, high = masks(g.IP)
    live = iota((g.IP, g.IP), 1) < SEQ
    zero = jnp.zeros((g.IP, 128), BF16)

    def group(k):
        group_in(g, p, b, k)
        gi = 2 * lax.rem(p.y + lax.div(k, 2), 2) + lax.rem(p.c + k, 2)
        for blk in range(2):
            rows = slice(blk * g.IP, (blk + 1) * g.IP)
            b.QKV[gi, rows, :] = nn(b.ACT1[rows, :], b.W[gi, :, 0:640]).astype(BF16)
        for blk in range(2):
            rows = slice(blk * g.IP, (blk + 1) * g.IP)
            outs = []
            for j in range(3):
                qt = b.QKV[gi, rows, (j // 2) * 128 : (j // 2) * 128 + 128]
                kt = b.QKV[gi, rows, 384 + (j // 2) * 128 : 384 + (j // 2) * 128 + 128]
                vt = b.QKV[gi, rows, 128 + ((j + 1) // 2) * 128 : 256 + ((j + 1) // 2) * 128]
                scores = nt(jnp.where(high if j == 1 else low, qt, zero), kt) * (HD**-0.5)
                scores = jnp.where(live, scores, -1e30)
                scores = jnp.exp(scores - jnp.max(scores, axis=1, keepdims=True))
                probs = (scores / jnp.sum(scores, axis=1, keepdims=True)).astype(BF16)
                b.PB[gi, blk * 3 + j] = probs
                outs.append(nn(probs, vt))
            b.ATT[gi, rows, 0:128] = jnp.where(high, outs[0], 0.0).astype(BF16)
            b.ATT[gi, rows, 128:256] = jnp.where(low, outs[1], outs[2]).astype(BF16)
        for blk in range(2):
            rows = slice(blk * g.IP, (blk + 1) * g.IP)
            b.HID[rows, :] += nt(b.ATT[gi, rows, :], b.W[gi, :, 512:768])

    loop(4, group)


def first_norm(g, b):
    def rows16(i):
        rows = pl.ds(pl.multiple_of(i * 16, 16), 16)
        x = b.x[rows, :].astype(F32)
        normed, _ = normalize(x)
        b.ACT1[rows, :] = (normed * b.GN[0:1, :]).astype(BF16)
        b.HID[rows, :] = x

    loop(2 * g.IP // 16, rows16)


def second_norm(g, b):
    def rows16(i):
        rows = pl.ds(pl.multiple_of(i * 16, 16), 16)
        normed, _ = normalize(b.HID[rows, :])
        b.ACT2[rows, :] = (normed * b.GN[1:2, :]).astype(BF16)

    loop(2 * g.IP // 16, rows16)
    lane = iota((g.IP, 128), 1)
    for blk in range(2):
        rows = slice(blk * g.IP, (blk + 1) * g.IP)
        logits = jnp.where(lane < g.ne, nn(b.ACT2[rows, :], b.RW[...]), -1e30)
        weight = jnp.exp(logits - jnp.max(logits, axis=1, keepdims=True))
        probs = weight / jnp.sum(weight, axis=1, keepdims=True)
        b.PRB[rows, :] = probs
        top = probs.astype(BF16).astype(F32)
        rest = probs - top
        b.PRH[rows, :] = (top + pltpu.roll(rest, 64, 1)).astype(BF16)


def small_weights(g, b):
    lane = iota((g.D, 128), 1)
    small = b.MI[...].astype(F32)
    b.RW[...] = jnp.where(lane < g.ne, small, 0.0).astype(BF16)
    gains = jnp.transpose(small)[120:128, :]
    b.GN[0:1, :] = gains[0:1, :] + gains[1:2, :]
    b.GN[1:2, :] = gains[2:3, :] + gains[3:4, :]


def half_of(g, i):
    return pl.ds(pl.multiple_of(i * g.DH, 128), g.DH)


def tokens_of(g, blk):
    return pl.ds(pl.multiple_of(blk * g.IP, 16), g.IP)


def tokens_out(g, p, b):
    for at, (device, yy, cc) in enumerate(
        ((p.across, p.oy, p.c), (p.diag, p.oy, p.oc), (p.core, p.y, p.oc))
    ):
        send(b, "ta", b.ACT2.at[tokens_of(g, cc), half_of(g, yy)], b.TA.at[p.h], at, p.h, device)
        send(b, "tp", b.PRH.at[tokens_of(g, cc), :], b.TG.at[p.h], at, p.h, device)
    b.TA[p.h] = b.ACT2[tokens_of(g, p.c), half_of(g, p.y)]
    b.TG[p.h] = b.PRH[tokens_of(g, p.c), :]


def tokens_in(g, p, b):
    for src in (p.hcore, p.hy, p.hdiag):
        arrived(b, p, "ta", b.TA.at[src], src)
        arrived(b, p, "tp", b.TG.at[src], src)


def cotangent_out(g, p, b):
    def pack(k):
        e2 = p.other(k + 1)
        rows = nn(b.P[pack_rows(g, e2), :], b.up[p.c]).astype(BF16)
        b.PKU[e2] = rows
        b.UPK[e2] = b.PKU[e2, :, half_of(g, p.y)]

        @pl.when(k < g.ne - 1)
        def _():
            send(b, "uz", b.PKU.at[e2], b.US.at[p.e, p.c], k, p.e, p.along(e2))

        @pl.when(k == g.ne - 1)
        def _():
            b.US[p.e, p.c] = rows
            send(b, "uc", b.US.at[p.e, p.c], b.US.at[p.e, p.c], p.e, p.e, p.core)

    loop(g.ne, pack)


def cotangent_on(g, p, b):
    def relay(k):
        e2 = p.other(k + 1)
        part = b.US.at[e2, p.c]
        arrived(b, p, "uz", part, e2)
        send(b, "uc", part, part, e2, e2, p.core)

    loop(g.ne - 1, relay)


def slots_out(g, p, b):
    row = iota((g.CP, g.DH), 0)
    eye = row == iota((g.CP, g.DH), 1)
    lane = iota((g.CP, 128), 1)

    def pack(k):
        e2 = p.other(k + 1)
        hot = b.P[pack_rows(g, e2), :]
        tok = nn(hot, b.TA[...].reshape(g.TP, g.DH))
        gates = nn(hot, b.TG[...].reshape(g.TP, 128))
        gate = jnp.sum(
            jnp.where((lane == e2) | (lane == e2 + 64), gates, 0.0), axis=1, keepdims=True
        )
        b.GC[e2] = jnp.broadcast_to(gate, (g.CP, 128))
        across = jnp.sum(jnp.where(eye, gate, 0.0), axis=0, keepdims=True)
        top = across.astype(BF16).astype(F32)
        rows = jnp.where(row == g.CAP, top, jnp.where(row == g.CAP + 1, across - top, tok))
        rows = rows.astype(BF16)

        @pl.when(k < g.ne - 1)
        def _():
            b.PKA[e2] = rows
            send(b, "xz", b.PKA.at[e2], b.XS.at[p.e, p.c, p.y], k, p.e, p.along(e2))

        @pl.when(k == g.ne - 1)
        def _():
            part = b.XS.at[p.e, p.c, p.y]
            b.XS[p.e, p.c, p.y] = rows
            send(b, "xy", part, part, p.e, p.e, p.across)
            send(b, "xc", part, part, p.e, p.e, p.core)

    loop(g.ne, pack)


def slots_on(g, p, b):
    def relay(k):
        e2 = p.other(k + 1)
        part = b.XS.at[e2, p.c, p.y]
        arrived(b, p, "xz", part, e2)
        send(b, "xy", part, part, e2, e2, p.across)
        send(b, "xc", part, part, e2, e2, p.core)

    loop(g.ne - 1, relay)


def slots_in(g, p, b):
    def relay(k):
        e2 = p.other(k)
        part = b.XS.at[e2, p.c, p.oy]
        arrived(b, p, "xy", part, e2)
        send(b, "xd", part, part, e2, e2, p.core)

    loop(g.ne, relay)

    def rest(k):
        e2 = p.other(k)
        arrived(b, p, "xc", b.XS.at[e2, p.oc, p.y], e2)
        arrived(b, p, "xd", b.XS.at[e2, p.oc, p.oy], e2)
        arrived(b, p, "uc", b.US.at[e2, p.oc], e2)

    loop(g.ne, rest)


def experts_out(g, p, b):
    b.WI[p.d] = b.wi[...]
    b.WB[p.d] = b.wb[...]
    send(b, "ei", b.wi, b.WI.at[p.d], 0, 0, p.twin)
    send(b, "eb", b.wb, b.WB.at[p.d], 0, 0, p.twin)


def gelu_parts(u):
    inner = 0.7978845608028654 * (u + 0.044715 * u * u * u)
    tangent = jnp.tanh(inner)
    value = 0.5 * u * (1.0 + tangent)
    slope = 0.5 * (1.0 + tangent) + 0.5 * u * (1.0 - tangent * tangent) * 0.7978845608028654 * (
        1.0 + 3.0 * 0.044715 * u * u
    )
    return value, slope


def expert(g, b):
    base = g.CP - 16
    eye = iota((g.CP, g.DH), 0) == iota((g.CP, g.DH), 1)

    def sources(t):
        first = t * g.SG
        for i in range(g.SG):
            for blk in range(2):
                tail = b.XS[first + i, blk, 0, base:, :].astype(F32)
                row = tail[g.CAP - base : g.CAP - base + 1] + tail[g.CAP - base + 1 : g.CAP - base + 2]
                gate = jnp.sum(jnp.where(eye, row, 0.0), axis=1, keepdims=True)
                at = (i * 2 + blk) * g.CP
                b.GP[at : at + g.CP, :] = (b.US[first + i, blk].astype(F32) * gate).astype(BF16)
        x = [b.XS[pl.ds(first, g.SG), :, q].reshape(g.R, g.DH) for q in range(2)]
        for n in range(g.F // 256):
            cols = slice(n * 256, n * 256 + 256)
            pre = nn(x[0], b.WI[0, :, cols]) + nn(x[1], b.WI[1, :, cols])
            value, slope = gelu_parts(pre)
            b.HQ[:, cols] = value.astype(BF16)
            grad = nt(b.GP[:, : g.DH], b.WB[0, cols, :]) + nt(b.GP[:, g.DH :], b.WB[1, cols, :])
            b.GR[:, cols] = (grad * slope).astype(BF16)
        shape = (g.SG, 2, g.CP, g.DH)
        for q in range(2):
            b.PO[pl.ds(first, g.SG), :, q] = nn(b.HQ[...], b.WB[q]).astype(BF16).reshape(shape)
            b.PG[pl.ds(first, g.SG), :, q] = nt(b.GR[...], b.WI[q]).astype(BF16).reshape(shape)
            b.DB[q] += tn(b.HQ[...], b.GP[:, q * g.DH : (q + 1) * g.DH])
            b.DI[q] += tn(x[q], b.GR[...])

    b.DB[...] = jnp.zeros_like(b.DB)
    b.DI[...] = jnp.zeros_like(b.DI)
    loop(g.ne // g.SG, sources)


def first_sends_end(g, p, b):
    n = g.ne
    if g.aligned:
        own = piece_rows(g, p.d, p.e)

        def z(k):
            left(b, p, "wz", b.wp, k)
            left(b, p, "mz", b.mp, k)

        loop(n - 1, z)

        def x(k):
            left(b, p, "wx", b.wp, k)
            left(b, p, "mx", b.mp, k)

        loop(n, x)

    def w(i):
        for name in ("wy", "wc", "wd"):
            left(b, p, name, piece_of(g, b.W, p.h, i), i)

    loop(pieces(g), w)
    for at in range(3):
        left(b, p, "ta", b.TA.at[0], at)
        left(b, p, "tp", b.TG.at[0], at)

    def slots(k):
        left(b, p, "uz", b.PKU.at[0], k)
        left(b, p, "xz", b.PKA.at[0], k)

    loop(n - 1, slots)

    def on(k):
        left(b, p, "uc", b.US.at[0, 0], k)
        for name in ("xy", "xc", "xd"):
            left(b, p, name, b.XS.at[0, 0, 0], k)

    loop(n, on)
    left(b, p, "ei", b.wi, 0)
    left(b, p, "eb", b.wb, 0)


def first_kernel(g, b):
    p = Place(g)
    p.enter()
    weights_out(g, p, b)
    route(g, p, b)
    weights_on(g, p, b)
    cotangent_out(g, p, b)
    weights_end(g, p, b)
    experts_out(g, p, b)
    small_weights(g, b)
    first_norm(g, b)
    attention(g, p, b)
    second_norm(g, b)
    tokens_out(g, p, b)
    cotangent_on(g, p, b)
    tokens_in(g, p, b)
    slots_out(g, p, b)
    slots_on(g, p, b)
    slots_in(g, p, b)
    arrived(b, p, "ei", b.WI.at[p.od], 0)
    arrived(b, p, "eb", b.WB.at[p.od], 0)
    expert(g, b)
    b.KI[...] = b.DI[p.d]
    b.KB[...] = b.DB[p.d]
    b.SI[...] = b.DI[p.od].astype(BF16)
    b.SB[...] = b.DB[p.od].astype(BF16)
    first_sends_end(g, p, b)


def grads_of_expert_out(g, p, b):
    send(b, "gi", b.SI, b.XI, 0, 0, p.twin)
    send(b, "gb", b.SB, b.XB, 0, 0, p.twin)


def grads_of_expert_in(g, p, b):
    arrived(b, p, "gi", b.XI, 0)
    b.o_gi[...] = b.KI[...] + b.XI[...].astype(F32)
    arrived(b, p, "gb", b.XB, 0)
    b.o_gb[...] = b.KB[...] + b.XB[...].astype(F32)


def returns(g, p, b):
    n = g.ne
    for kind, part in enumerate((b.PO, b.PG)):

        def to_core(k, kind=kind, part=part):
            s = p.other(k + 1)
            send(b, "rc", part.at[s, p.oc], b.RC.at[kind, s], kind * n + s, kind * n + s, p.core)

        loop(n, to_core)
    for kind, part in enumerate((b.PO, b.PG)):

        def to_across(k, kind=kind, part=part):
            s = p.other(k + 1)
            at = kind * n + s
            arrived(b, p, "rc", b.RC.at[kind, s], at)
            b.RC[kind, s, p.oy] = (
                part[s, p.c, p.oy].astype(F32) + b.RC[kind, s, p.oy].astype(F32)
            ).astype(BF16)
            send(b, "ry", b.RC.at[kind, s, p.oy], b.RY.at[kind, s], at, at, p.across)

        loop(n, to_across)
    for kind, part in enumerate((b.PO, b.PG)):

        def to_source(k, kind=kind, part=part):
            s = p.other(k + 1)
            at = kind * n + s
            arrived(b, p, "ry", b.RY.at[kind, s], at)
            total = (
                part[s, p.c, p.y].astype(F32)
                + b.RC[kind, s, p.y].astype(F32)
                + b.RY[kind, s].astype(F32)
            ).astype(BF16)

            @pl.when(k < n - 1)
            def _():
                b.RC[kind, s, p.y] = total
                send(b, "rz", b.RC.at[kind, s, p.y], b.RO.at[kind, p.e], at, kind * n + p.e, p.along(s))

            @pl.when(k == n - 1)
            def _():
                b.RO[kind, p.e] = total

        loop(n, to_source)


def slots_back(g, p, b):
    n = g.ne
    lane = iota((g.CP, 128), 1)

    def rows_of(k):
        s = p.other(k)

        @pl.when(k > 0)
        def _():
            arrived(b, p, "rz", b.RO.at[0, s], s)
            arrived(b, p, "rz", b.RO.at[1, s], n + s)

        rows = pack_rows(g, s)
        out = b.RO[0, s].astype(F32)
        dots = jnp.sum(out * b.UPK[s].astype(F32), axis=1, keepdims=True)
        top = dots.astype(BF16).astype(F32)
        b.RB[rows, 0 : g.DH] = (out * b.GC[s][:, 0:1]).astype(BF16)
        b.RB[rows, g.DH : 2 * g.DH] = b.RO[1, s]
        b.RB[rows, 2 * g.DH :] = jnp.where(
            lane == s, top, jnp.where(lane == s + 64, dots - top, 0.0)
        ).astype(BF16)

    loop(n, rows_of)


def unpack(g, p, b):
    for at, (image, device) in enumerate(((p.hy, p.across), (p.hdiag, p.diag), (p.hcore, p.core))):
        rows = tokens_of(g, image)
        b.UN[at] = nn(b.PT[rows, :], b.RB[...]).astype(BF16)
        send(b, "un", b.UN.at[at], b.TR.at[p.c, p.y], at, p.h, device)
    b.TR[p.c, p.y] = nn(b.PT[tokens_of(g, p.h), :], b.RB[...]).astype(BF16)
    for hh, cc, yy in ((p.hcore, p.oc, p.y), (p.hy, p.c, p.oy), (p.hdiag, p.oc, p.oy)):
        arrived(b, p, "un", b.TR.at[cc, yy], hh)


def tokens_back(g, p, b):
    lane = iota((16, 128), 1)
    b.GA[...] = jnp.zeros_like(b.GA)

    for blk in range(2):

        def rows16(i, blk=blk):
            local = pl.ds(pl.multiple_of(i * 16, 16), 16)
            rows = pl.ds(pl.multiple_of(blk * g.IP + i * 16, 16), 16)
            hidden = b.HID[rows, :]
            for q in range(2):
                cols = slice(q * g.DH, (q + 1) * g.DH)
                b.o_mixed[rows, cols] = (
                    hidden[:, cols] + b.TR[blk, q, local, 0 : g.DH].astype(F32)
                ).astype(BF16)
            gate = b.TR[blk, 0, local, 2 * g.DH :].astype(F32) + b.TR[
                blk, 1, local, 2 * g.DH :
            ].astype(F32)
            gate = jnp.where(lane < g.ne, gate + pltpu.roll(gate, 64, 1), 0.0)
            probs = b.PRB[rows, :]
            grad = probs * (gate - jnp.sum(probs * gate, axis=1, keepdims=True))
            b.GL[rows, :] = grad.astype(BF16)

        loop(g.IP // 16, rows16)
    for blk in range(2):
        rows = slice(blk * g.IP, (blk + 1) * g.IP)
        b.GHID[rows, :] = nt(b.GL[rows, :], b.RW[...])
    for blk in range(2):

        def rows16b(i, blk=blk):
            local = pl.ds(pl.multiple_of(i * 16, 16), 16)
            rows = pl.ds(pl.multiple_of(blk * g.IP + i * 16, 16), 16)
            normed, inverse = normalize(b.HID[rows, :])
            upstream = b.GHID[rows, :] + jnp.concatenate(
                [b.TR[blk, q, local, g.DH : 2 * g.DH].astype(F32) for q in range(2)], axis=1
            )
            prod = upstream * normed
            b.GA[8:16, :] += prod[0:8, :] + prod[8:16, :]
            b.ACT2[rows, :] = (normed * b.GN[1:2, :]).astype(BF16)
            hidden = b.up[rows, :].astype(F32) + norm_backward(
                upstream, normed, inverse, b.GN[1:2, :]
            )
            b.GHID[rows, :] = hidden
            b.GHL[rows, :] = hidden.astype(BF16)
            normed, _ = normalize(b.x[rows, :].astype(F32))
            b.ACT1[rows, :] = (normed * b.GN[0:1, :]).astype(BF16)

        loop(g.IP // 16, rows16b)


def attention_back(g, p, b):
    low, high = masks(g.IP)
    zero = jnp.zeros((g.IP, 128), BF16)
    scale = HD**-0.5
    b.DA[...] = jnp.zeros_like(b.DA)

    def group(k):
        yk = lax.rem(p.oy + k, 2)
        gi = 2 * yk + lax.rem(p.oc + lax.div(k, 2), 2)
        for blk in range(2):
            rows = slice(blk * g.IP, (blk + 1) * g.IP)
            grad = nn(b.GHL[rows, :], b.W[gi, :, 512:768]).astype(BF16)
            tiles = [grad[:, 0:128], grad[:, 128:256]]
            dq, dk, dv = [], [], []
            for j in range(3):
                probs = b.PB[gi, blk * 3 + j]
                gt = tiles[(j + 1) // 2]
                qt = b.QKV[gi, rows, (j // 2) * 128 : (j // 2) * 128 + 128]
                kt = b.QKV[gi, rows, 384 + (j // 2) * 128 : 384 + (j // 2) * 128 + 128]
                vt = b.QKV[gi, rows, 128 + ((j + 1) // 2) * 128 : 256 + ((j + 1) // 2) * 128]
                grad_probs = nt(jnp.where(low if j == 1 else high, gt, zero), vt)
                wide = probs.astype(F32)
                grad_scores = wide * (
                    grad_probs - jnp.sum(wide * grad_probs, axis=1, keepdims=True)
                )
                grad_scores = (grad_scores * scale).astype(BF16)
                dv.append(tn(probs, gt))
                dq.append(nn(grad_scores, kt))
                dk.append(tn(grad_scores, qt))
            b.GJ[rows, 0:128] = jnp.where(low, dq[0], dq[1]).astype(BF16)
            b.GJ[rows, 128:256] = jnp.where(low, dq[2], dv[0]).astype(BF16)
            b.GJ[rows, 256:384] = jnp.where(low, dv[1], dv[2]).astype(BF16)
            b.GJ[rows, 384:512] = jnp.where(low, dk[0], dk[1]).astype(BF16)
            b.GJ[rows, 512:640] = jnp.where(low, dk[2], 0.0).astype(BF16)
        for blk in range(2):
            rows = slice(blk * g.IP, (blk + 1) * g.IP)
            b.DA[rows, :] += nt(b.GJ[rows, :], b.W[gi, :, 0:640])
        for m in range(g.D // 256):
            cols = slice(m * 256, m * 256 + 256)
            first = tn(b.ACT1[:, cols], b.GJ[...])
            second = tn(b.GHL[:, cols], b.ATT[gi])
            b.DW[gi, cols, 0:512] = first[:, 0:512].astype(BF16)
            b.DW[gi, cols, 512:640] = (first[:, 512:] + second[:, 0:128]).astype(BF16)
            b.DW[gi, cols, 640:768] = second[:, 128:].astype(BF16)

        @pl.when(k < 2)
        def _():
            send(b, "dc", b.DW.at[gi], b.RDC.at[yk], yk, yk, p.core)

    loop(4, group)


def inputs_back(g, p, b):
    def rows16(i):
        rows = pl.ds(pl.multiple_of(i * 16, 16), 16)
        normed, inverse = normalize(b.x[rows, :].astype(F32))
        upstream = b.DA[rows, :]
        prod = upstream * normed
        b.GA[0:8, :] += prod[0:8, :] + prod[8:16, :]
        b.GIN[rows, :] = (
            b.GHID[rows, :] + norm_backward(upstream, normed, inverse, b.GN[0:1, :])
        ).astype(BF16)

    loop(2 * g.IP // 16, rows16)
    for blk in range(2):
        part = b.GIN.at[blk * g.IP : (blk + 1) * g.IP, :]
        send(b, "iy", part, b.o_gin.at[blk, p.h], blk, blk, p.across)
        send(b, "ic", part, b.o_gin.at[blk, p.h], blk, blk, p.core)
    for blk in range(2):
        b.o_gin[blk, p.h] = b.GIN[blk * g.IP : (blk + 1) * g.IP, :]


def inputs_end(g, p, b):
    for blk in range(2):
        part = b.o_gin.at[blk, p.hy]
        arrived(b, p, "iy", part, blk)
        send(b, "id", part, part, blk, blk, p.core)
    for blk in range(2):
        arrived(b, p, "ic", b.o_gin.at[blk, p.hcore], blk)
        arrived(b, p, "id", b.o_gin.at[blk, p.hdiag], blk)


def weights_back(g, p, b):
    for i in range(2):
        rows = pl.ds(pl.multiple_of(i * g.DH, 16), g.DH)
        if i == 0:
            arrived(b, p, "dc", b.RDC.at[p.oy], p.oy)
        b.DW[p.hy, rows, :] = (b.DW[p.hy, rows, :].astype(F32) + b.RDC[p.oy, rows, :].astype(F32)).astype(BF16)
        send(b, "dy", b.DW.at[p.hy, rows, :], b.RDY.at[rows, :], i, i, p.across)


def weights_back_on(g, p, b):
    arrived(b, p, "dc", b.RDC.at[p.y], p.y)

    def total(rows):
        return (
            b.DW[p.h, rows, :].astype(F32)
            + b.RDC[p.y, rows, :].astype(F32)
            + b.RDY[rows, :].astype(F32)
        )

    for i in range(2):
        arrived(b, p, "dy", b.RDY.at[pl.ds(i * g.DH, g.DH), :], i)
    if not g.aligned:
        b.o_dw[...] = total(slice(0, g.D)).astype(BF16)
        return
    half = g.D // 2
    away = pl.ds(pl.multiple_of(p.od * half, 16), half)
    b.DW[p.h, away, :] = total(away).astype(BF16)
    send(b, "dx", b.DW.at[p.h, away, :], b.RDX, 0, 0, p.twin)
    arrived(b, p, "dx", b.RDX, 0)

    def piece(k):
        e2 = p.other(k + 1)
        local = pl.ds(pl.multiple_of(e2 * g.PR, 16), g.PR)
        mine = total(piece_rows(g, p.d, e2)) + b.RDX[local, :].astype(F32)

        @pl.when(k < g.ne - 1)
        def _():
            b.SDZ[e2] = mine.astype(BF16)
            send(b, "dz", b.SDZ.at[e2], b.RDZ.at[p.e], k, p.e, p.along(e2))

        @pl.when(k == g.ne - 1)
        def _():
            b.o_dw[...] = mine

    loop(g.ne, piece)

    def add(k):
        e2 = p.other(k + 1)
        arrived(b, p, "dz", b.RDZ.at[e2], e2)
        b.o_dw[...] += b.RDZ[e2].astype(F32)

    loop(g.ne - 1, add)


def small_back(g, p, b):
    sub = iota((128, g.D), 0)
    one = jnp.sum(b.GA[0:8, :], axis=0, keepdims=True)
    two = jnp.sum(b.GA[8:16, :], axis=0, keepdims=True)
    gains = jnp.where(sub == 120, one, jnp.where(sub == 122, two, 0.0))
    b.GM[...] = tn(b.ACT2[...], b.GL[...]) + jnp.transpose(gains)
    if g.aligned:
        half = g.D // 2
        b.SMX[...] = b.GM[pl.ds(pl.multiple_of(p.od * half, 16), half), :].astype(BF16)
        send(b, "sx", b.SMX, b.RMX, 0, 0, p.twin)


def small_back_on(g, p, b):
    if g.aligned:
        arrived(b, p, "sx", b.RMX, 0)

        def piece(k):
            e2 = p.other(k + 1)
            mine = b.GM[piece_rows(g, p.d, e2), :] + b.RMX[
                pl.ds(pl.multiple_of(e2 * g.PR, 16), g.PR), :
            ].astype(F32)

            @pl.when(k < g.ne - 1)
            def _():
                b.SMZ[e2] = mine.astype(BF16)
                send(b, "sz", b.SMZ.at[e2], b.RMZ.at[p.e], k, p.e, p.along(e2))

            @pl.when(k == g.ne - 1)
            def _():
                b.o_small[...] = mine

        loop(g.ne, piece)

        def add(k):
            e2 = p.other(k + 1)
            arrived(b, p, "sz", b.RMZ.at[e2], e2)
            b.o_small[...] += b.RMZ[e2].astype(F32)

        loop(g.ne - 1, add)
    else:
        b.o_small[...] = b.GM[...]
    b.SMC[...] = b.o_small[...].astype(BF16)
    send(b, "sc", b.SMC, b.RMC, 0, 0, p.core)
    arrived(b, p, "sc", b.RMC, 0)
    b.SMY[...] = (b.SMC[...].astype(F32) + b.RMC[...].astype(F32)).astype(BF16)
    send(b, "sy", b.SMY, b.RMY, 0, 0, p.across)
    arrived(b, p, "sy", b.RMY, 0)
    b.o_small[...] = b.SMY[...].astype(F32) + b.RMY[...].astype(F32)


def second_sends_end(g, p, b):
    n = g.ne
    left(b, p, "gi", b.SI, 0)
    left(b, p, "gb", b.SB, 0)

    def rets(k):
        left(b, p, "rc", b.RC.at[0, 0], k)
        left(b, p, "ry", b.RY.at[0, 0], k)

    loop(2 * n, rets)

    def away(k):
        s = p.other(k + 1)
        left(b, p, "rz", b.RY.at[0, 0], s)
        left(b, p, "rz", b.RY.at[0, 0], n + s)
        if g.aligned:
            left(b, p, "dz", b.SDZ.at[0], k)
            left(b, p, "sz", b.SMZ.at[0], k)

    loop(n - 1, away)
    for at in range(3):
        left(b, p, "un", b.UN.at[0], at)
    for i in range(2):
        left(b, p, "dc", b.RDC.at[0], i)
        left(b, p, "dy", b.RDY.at[pl.ds(0, g.DH), :], i)
        for name in ("iy", "ic", "id"):
            left(b, p, name, b.o_gin.at[0, 0], i)
    if g.aligned:
        left(b, p, "dx", b.RDX, 0)
        left(b, p, "sx", b.SMX, 0)
    left(b, p, "sc", b.SMC, 0)
    left(b, p, "sy", b.SMY, 0)


def second_kernel(g, b):
    p = Place(g)
    p.enter()
    returns(g, p, b)
    grads_of_expert_out(g, p, b)
    slots_back(g, p, b)
    unpack(g, p, b)
    tokens_back(g, p, b)
    attention_back(g, p, b)
    inputs_back(g, p, b)
    small_back(g, p, b)
    weights_back(g, p, b)
    inputs_end(g, p, b)
    weights_back_on(g, p, b)
    small_back_on(g, p, b)
    grads_of_expert_in(g, p, b)
    second_sends_end(g, p, b)


def call(body, g, inputs, outs, scratch, sems, number, flops):
    names = [*inputs, *outs, *scratch]
    names += [name + end for name in sems for end in ("_s", "_r")]

    def kernel(*refs):
        body(g, types.SimpleNamespace(**dict(zip(names, refs, strict=True))))

    vmem = pl.BlockSpec(memory_space=pltpu.VMEM)
    made = pl.pallas_call(
        kernel,
        out_shape=[jax.ShapeDtypeStruct(*o) for o in outs.values()],
        in_specs=[vmem] * len(inputs),
        out_specs=[vmem] * len(outs),
        scratch_shapes=[pltpu.VMEM(*s) for s in scratch.values()]
        + [pltpu.SemaphoreType.DMA((n,)) for n in sems.values() for _ in range(2)],
        compiler_params=pltpu.CompilerParams(
            collective_id=number, has_side_effects=True, vmem_limit_bytes=LIMIT
        ),
        cost_estimate=pl.CostEstimate(flops=flops, bytes_accessed=2**24, transcendentals=0),
    )(*inputs.values())
    return dict(zip(outs, made, strict=True))


def shards(
    inputs, w_qkv, w_out, w_router, gain_one, gain_two, w_in, w_back, experts, priority, cotangent, *, mesh
):
    model, rows = inputs.shape[2], inputs.shape[1]
    g = Sizes(mesh, model, rows, w_in.shape[2])
    n, ip, cp, dh = g.ne, g.IP, g.CP, g.DH
    assert inputs.shape[0] == 2
    h = lax.axis_index("head")
    pad = ((0, 0), (0, 0), (0, ip - SEQ), (0, 0))
    x_all = inputs.reshape(2, g.NI, SEQ, model)
    x = jnp.pad(lax.dynamic_slice_in_dim(x_all, h, 1, 1), pad).reshape(2 * ip, model)
    up_all = jnp.pad(cotangent.reshape(2, g.NI, SEQ, model), pad)
    up_own = lax.dynamic_slice_in_dim(up_all, h, 1, 1).reshape(2 * ip, model)
    part = jnp.concatenate([w_qkv[:, 0], w_qkv[:, 2], w_qkv[:, 1], w_out.T], axis=1)
    gains = jnp.stack([gain_one, gain_two], axis=1)
    top = gains.astype(BF16)
    rest = (gains - top.astype(F32)).astype(BF16)
    small = jnp.concatenate(
        [
            w_router,
            jnp.zeros((w_router.shape[0], 120 - n), BF16),
            top[:, :1],
            rest[:, :1],
            top[:, 1:],
            rest[:, 1:],
            jnp.zeros((w_router.shape[0], 4), BF16),
        ],
        axis=1,
    )
    if not g.aligned:
        part = lax.all_gather(part, ("dp", "expert"), axis=0, tiled=True)
        small = lax.all_gather(small, ("dp", "expert"), axis=0, tiled=True)
    info = jnp.concatenate([experts, priority[:, :, None]], axis=2).astype(F32)
    info = jnp.pad(info.reshape(2, g.NI, SEQ, 3), pad, constant_values=-1000.0)
    mc = jnp.pad(info.reshape(2, g.TP, 3), ((0, 0), (0, 0), (0, 5)))
    mr = jnp.swapaxes(mc, 1, 2)
    np_ = pieces(g)
    one = call(
        first_kernel,
        g,
        dict(x=x, up=up_all.reshape(2, g.TP, model), wp=part, mp=small, wi=w_in[0], wb=w_back[0], mc=mc, mr=mr),
        dict(
            W=((4, model, model), BF16),
            RW=((model, 128), BF16),
            GN=((8, model), F32),
            QKV=((4, 2 * ip, 640), BF16),
            PB=((4, 6, ip, ip), BF16),
            ATT=((4, 2 * ip, 256), BF16),
            HID=((2 * ip, model), F32),
            PRB=((2 * ip, 128), F32),
            PT=((g.TP, g.SL), BF16),
            UPK=((n, cp, dh), BF16),
            GC=((n, cp, 128), F32),
            PO=((n, 2, 2, cp, dh), BF16),
            PG=((n, 2, 2, cp, dh), BF16),
            KI=((dh, g.F), F32),
            KB=((g.F, dh), F32),
            SI=((dh, g.F), BF16),
            SB=((g.F, dh), BF16),
        ),
        dict(
            DI=((2, dh, g.F), F32),
            DB=((2, g.F, dh), F32),
            MI=((model, 128), BF16),
            L=((g.TP, g.TP), BF16),
            O=((g.TP, 128), BF16),
            P=((g.SL, g.TP), BF16),
            ACT1=((2 * ip, model), BF16),
            ACT2=((2 * ip, model), BF16),
            PRH=((2 * ip, 128), BF16),
            TA=((4, ip, dh), BF16),
            TG=((4, ip, 128), BF16),
            US=((n, 2, cp, model), BF16),
            XS=((n, 2, 2, cp, dh), BF16),
            PKA=((n, cp, dh), BF16),
            PKU=((n, cp, model), BF16),
            WI=((2, dh, g.F), BF16),
            WB=((2, g.F, dh), BF16),
            GP=((g.R, model), BF16),
            HQ=((g.R, g.F), BF16),
            GR=((g.R, g.F), BF16),
        ),
        dict(wz=n, mz=n, wx=n, mx=n, wy=np_, wc=np_, wd=np_, ta=4, tp=4, uz=n, uc=n, xz=n, xy=n, xc=n, xd=n, ei=1, eb=1),
        1,
        14 * 10**9,
    )
    keep = ("W", "RW", "GN", "QKV", "PB", "ATT", "HID", "PRB", "PT", "UPK", "GC", "PO", "PG", "KI", "KB", "SI", "SB")
    rows_out = g.PR if g.aligned else model
    extra = (
        dict(
            RDX=((model // 2, model), BF16),
            SDZ=((n, g.PR, model), BF16),
            RDZ=((n, g.PR, model), BF16),
            SMX=((model // 2, 128), BF16),
            RMX=((model // 2, 128), BF16),
            SMZ=((n, g.PR, 128), BF16),
            RMZ=((n, g.PR, 128), BF16),
        )
        if g.aligned
        else {}
    )
    two = call(
        second_kernel,
        g,
        dict(x=x, up=up_own, **{name: one[name] for name in keep}),
        dict(
            o_mixed=((2 * ip, model), BF16),
            o_gin=((2, 4, ip, model), BF16),
            o_dw=((rows_out, model), F32 if g.aligned else BF16),
            o_small=((rows_out, 128), F32),
            o_gi=((dh, g.F), F32),
            o_gb=((g.F, dh), F32),
        ),
        dict(
            RC=((2, n, 2, cp, dh), BF16),
            RY=((2, n, cp, dh), BF16),
            RO=((2, n, cp, dh), BF16),
            RB=((g.SL, 2 * dh + 128), BF16),
            UN=((3, ip, 2 * dh + 128), BF16),
            TR=((2, 2, ip, 2 * dh + 128), BF16),
            GL=((2 * ip, 128), BF16),
            GA=((16, model), F32),
            ACT1=((2 * ip, model), BF16),
            ACT2=((2 * ip, model), BF16),
            GHID=((2 * ip, model), F32),
            GHL=((2 * ip, model), BF16),
            DA=((2 * ip, model), F32),
            GJ=((2 * ip, 640), BF16),
            DW=((4, model, model), BF16),
            RDC=((2, model, model), BF16),
            RDY=((model, model), BF16),
            GIN=((2 * ip, model), BF16),
            GM=((model, 128), F32),
            SMC=((rows_out, 128), BF16),
            RMC=((rows_out, 128), BF16),
            SMY=((rows_out, 128), BF16),
            RMY=((rows_out, 128), BF16),
            XI=((dh, g.F), BF16),
            XB=((g.F, dh), BF16),
            **extra,
        ),
        dict(rc=2 * n, ry=2 * n, rz=2 * n, un=4, gi=1, gb=1, dc=2, dy=2, dx=1, dz=n, sx=1, sz=n, sc=1, sy=1, iy=2, ic=2, id=2),
        2,
        14 * 10**9,
    )
    mixed = two["o_mixed"].reshape(2, ip, model)[:, :SEQ]
    grad_inputs = two["o_gin"][:, :, :SEQ].reshape(2, rows, model)
    dw, ds = two["o_dw"], two["o_small"]
    if not g.aligned:
        dw = lax.psum_scatter(dw, ("dp", "expert"), scatter_dimension=0, tiled=True)
        ds = lax.psum_scatter(ds.astype(BF16), ("dp", "expert"), scatter_dimension=0, tiled=True)
        dw, ds = dw.astype(F32), ds.astype(F32)
    lw = g.LW
    grad_qkv = jnp.stack([dw[:, :lw], dw[:, 2 * lw : 3 * lw], dw[:, lw : 2 * lw]], axis=1)
    return (
        mixed,
        grad_inputs,
        grad_qkv,
        dw[:, 3 * lw :].T,
        ds[:, :n],
        ds[:, 120],
        ds[:, 122],
        two["o_gi"][None],
        two["o_gb"][None],
    )


def solution(mesh):
    both = ("dp", "expert")
    in_specs = (
        P(both, None, None),
        P(both, None, "head"),
        P("head", both),
        P(both, None),
        P(both),
        P(both),
        P("expert", "dp", "head"),
        P("expert", "head", "dp"),
        P(both, None, None),
        P(both, None),
        P(both, None, None),
    )
    out_specs = (
        P(both, "head", None),
        P(both, None, None),
        P(both, None, "head"),
        P("head", both),
        P(both, None),
        P(both),
        P(both),
        P("expert", "dp", "head"),
        P("expert", "head", "dp"),
    )
    return jax.shard_map(
        functools.partial(shards, mesh=mesh),
        mesh=mesh,
        in_specs=in_specs,
        out_specs=out_specs,
        check_vma=False,
    )
```

```python
import functools
import types

import jax
import jax.numpy as jnp
from jax import lax
from jax.experimental import pallas as pl
from jax.experimental.pallas import tpu as pltpu
from jax.sharding import PartitionSpec as P

HD = 64
SEQ = 196
MESH = pl.DeviceIdType.MESH
F32, BF16 = jnp.float32, jnp.bfloat16
LIMIT = 63 * 2**20


def up16(n):
    return -(-n // 16) * 16


def nn(a, b):
    return lax.dot_general(a, b, (((1,), (0,)), ((), ())), preferred_element_type=F32)


def nt(a, b):
    return lax.dot_general(a, b, (((1,), (1,)), ((), ())), preferred_element_type=F32)


def tn(a, b):
    return lax.dot_general(a, b, (((0,), (0,)), ((), ())), preferred_element_type=F32)


def loop(count, body):
    def step(i, carry):
        body(i)
        return carry

    lax.fori_loop(0, count, step, 0)


def iota(shape, dim):
    return lax.broadcasted_iota(jnp.int32, shape, dim)


def fiota(shape, dim):
    return iota(shape, dim).astype(F32)


def normalize(v):
    centered = v - jnp.mean(v, axis=1, keepdims=True)
    inverse = lax.rsqrt(jnp.mean(centered * centered, axis=1, keepdims=True) + 1e-06)
    return centered * inverse, inverse


def norm_backward(upstream, normed, inverse, gain):
    scaled = upstream * gain
    return inverse * (
        scaled
        - jnp.mean(scaled, axis=1, keepdims=True)
        - normed * jnp.mean(scaled * normed, axis=1, keepdims=True)
    )


class Sizes:
    def __init__(self, mesh, model, rows, hidden):
        self.nd, self.ne, self.nh = mesh.shape["dp"], mesh.shape["expert"], mesh.shape["head"]
        self.D, self.DH = model, model // 2
        self.M = rows
        self.CAP = rows // self.ne
        self.CP = up16(self.CAP + 2)
        self.IP = up16(SEQ)
        self.NI = rows // SEQ
        self.TP = self.NI * self.IP
        self.SL = self.ne * self.CP
        self.F = hidden
        self.PR = model // (self.nd * self.ne)
        self.aligned = self.PR % 16 == 0
        self.SG = 1
        while self.SG * 2 * self.CP <= self.IP and self.ne % (self.SG * 2) == 0:
            self.SG *= 2
        self.R = self.SG * 2 * self.CP
        self.LW = model // self.nh
        assert self.nd == 2 and self.nh == 4 and self.NI == 4 and self.LW == 3 * HD
        assert self.ne <= 64 and 0 <= self.CAP - (self.CP - 16) <= 14


class Place:
    def __init__(self, g):
        self.ne = g.ne
        self.d = lax.axis_index("dp")
        self.e = lax.axis_index("expert")
        self.h = lax.axis_index("head")
        self.y = lax.div(self.h, 2)
        self.c = lax.rem(self.h, 2)
        self.oy, self.oc, self.od = 1 - self.y, 1 - self.c, 1 - self.d
        self.hcore = 2 * self.y + self.oc
        self.hy = 2 * self.oy + self.c
        self.hdiag = 2 * self.oy + self.oc
        self.core = (self.d, self.e, self.hcore)
        self.across = (self.d, self.e, self.hy)
        self.diag = (self.d, self.e, self.hdiag)
        self.twin = (self.od, self.e, self.h)

    def other(self, k):
        return lax.rem(self.e + k, self.ne)

    def along(self, e2):
        return (self.d, e2, self.h)

    def enter(self):
        barrier = pltpu.get_barrier_semaphore()

        def tell(device):
            pl.semaphore_signal(barrier, inc=1, device_id=device, device_id_type=MESH)

        for device in (self.core, self.across, self.diag, self.twin):
            tell(device)
        loop(self.ne - 1, lambda k: tell(self.along(self.other(k + 1))))
        pl.semaphore_wait(barrier, 4 + self.ne - 1)


def copy(b, name, src, dst, si, ri, device):
    return pltpu.make_async_remote_copy(
        src_ref=src,
        dst_ref=dst,
        send_sem=getattr(b, name + "_s").at[si],
        recv_sem=getattr(b, name + "_r").at[ri],
        device_id=device,
        device_id_type=MESH,
    )


def send(b, name, src, dst, si, ri, device):
    copy(b, name, src, dst, si, ri, device).start()


def arrived(b, p, name, ref, ri):
    copy(b, name, ref, ref, 0, ri, p.core).wait_recv()


def left(b, p, name, ref, si):
    copy(b, name, ref, ref, si, 0, p.core).wait_send()


def route(g, p, b):
    c = p.c
    pr_row, e0r, e1r = b.mr[c, 2:3, :], b.mr[c, 0:1, :], b.mr[c, 1:2, :]
    lane = fiota((g.IP, 128), 1)
    base = jnp.zeros((1, 128), F32)
    for i in range(g.NI):
        rows = slice(i * g.IP, (i + 1) * g.IP)
        col = b.mc[c, rows, :]
        e0c, e1c, prc = col[:, 0:1], col[:, 1:2], col[:, 2:3]
        b.L[rows, :] = jnp.where(pr_row < prc, 1.0, 0.0).astype(BF16)
        b.O[rows, :] = jnp.where((lane == e0c) | (lane == e1c + 64.0), 1.0, 0.0).astype(BF16)
        base = base + jnp.sum(jnp.where(lane == e0c + 64.0, 1.0, 0.0), axis=0, keepdims=True)
    slot_lane = fiota((g.IP, g.SL), 1)
    for i in range(g.NI):
        rows = slice(i * g.IP, (i + 1) * g.IP)
        col = b.mc[c, rows, :]
        e0c, e1c = col[:, 0:1], col[:, 1:2]
        own = b.O[rows, :].astype(F32)
        earlier = nn(b.L[rows, :], b.O[...])
        s0 = jnp.sum(jnp.where(lane < 64.0, earlier * own, 0.0), axis=1, keepdims=True)
        s1 = jnp.sum(jnp.where(lane < 64.0, 0.0, (earlier + base) * own), axis=1, keepdims=True)
        t0 = jnp.where(s0 < g.CAP, e0c * g.CP + s0, -1.0)
        t1 = jnp.where(s1 < g.CAP, e1c * g.CP + s1, -1.0)
        b.PT[rows, :] = jnp.where((slot_lane == t0) | (slot_lane == t1), 1.0, 0.0).astype(BF16)
    sub = fiota((128, g.TP), 0)
    own = jnp.where((sub == e0r) | (sub == e1r + 64.0), 1.0, 0.0)
    base = jnp.sum(jnp.where(sub == e0r + 64.0, 1.0, 0.0), axis=1, keepdims=True)
    earlier = nt(own.astype(BF16), b.L[...])
    s0 = jnp.sum(jnp.where(sub < 64.0, earlier * own, 0.0), axis=0, keepdims=True)
    s1 = jnp.sum(jnp.where(sub < 64.0, 0.0, (earlier + base) * own), axis=0, keepdims=True)
    t0 = jnp.where(s0 < g.CAP, e0r * g.CP + s0, -1.0)
    t1 = jnp.where(s1 < g.CAP, e1r * g.CP + s1, -1.0)
    slot_sub = fiota((g.CP, g.TP), 0)

    def fill(e2):
        at = slot_sub + (e2 * g.CP).astype(F32)
        b.P[pl.ds(pl.multiple_of(e2 * g.CP, 16), g.CP), :] = jnp.where(
            (at == t0) | (at == t1), 1.0, 0.0
        ).astype(BF16)

    loop(g.ne, fill)


def pack_rows(g, e2):
    return pl.ds(pl.multiple_of(e2 * g.CP, 16), g.CP)


def piece_rows(g, d, e2):
    return pl.ds(pl.multiple_of((d * g.ne + e2) * g.PR, 16), g.PR)


def weights_out(g, p, b):
    own = piece_rows(g, p.d, p.e)
    if g.aligned:
        mine = p.d * g.ne + p.e

        def to_expert(k):
            device = p.along(p.other(k + 1))
            send(b, "wz", b.wp, b.W.at[p.h, own, :], k, p.e, device)
            send(b, "mz", b.mp, b.MI.at[own, :], k, p.e, device)

        loop(g.ne - 1, to_expert)
        send(b, "wx", b.wp, b.W.at[p.h, own, :], p.e, p.e, p.twin)
        send(b, "mx", b.mp, b.MI.at[own, :], p.e, p.e, p.twin)
        send(b, "wy", b.wp, b.W.at[p.h, own, :], mine, mine, p.across)
        send(b, "wc", b.wp, b.W.at[p.h, own, :], mine, mine, p.core)
        b.W[p.h, own, :] = b.wp[...]
        b.MI[own, :] = b.mp[...]
    else:
        send(b, "wy", b.wp, b.W.at[p.h], 0, 0, p.across)
        send(b, "wc", b.wp, b.W.at[p.h], 0, 0, p.core)
        b.W[p.h] = b.wp[...]
        b.MI[...] = b.mp[...]


def weights_on(g, p, b):
    if not g.aligned:
        return

    def relay(k):
        e2 = p.other(k + 1)
        rows = piece_rows(g, p.d, e2)
        at = p.d * g.ne + e2
        part = b.W.at[p.h, rows, :]
        arrived(b, p, "wz", part, e2)
        send(b, "wx", part, part, e2, e2, p.twin)
        send(b, "wy", part, part, at, at, p.across)
        send(b, "wc", part, part, at, at, p.core)
        part = b.MI.at[rows, :]
        arrived(b, p, "mz", part, e2)
        send(b, "mx", part, part, e2, e2, p.twin)

    loop(g.ne - 1, relay)


def weights_end(g, p, b):
    if not g.aligned:
        return

    def relay(k):
        e2 = p.other(k)
        rows = piece_rows(g, p.od, e2)
        at = p.od * g.ne + e2
        part = b.W.at[p.h, rows, :]
        arrived(b, p, "wx", part, e2)
        send(b, "wy", part, part, at, at, p.across)
        send(b, "wc", part, part, at, at, p.core)
        arrived(b, p, "mx", b.MI.at[rows, :], e2)

    loop(g.ne, relay)


def pieces(g):
    return g.nd * g.ne if g.aligned else 1


def piece_of(g, ref, group, i):
    if not g.aligned:
        return ref.at[group]
    return ref.at[group, pl.ds(pl.multiple_of(i * g.PR, 16), g.PR), :]


def group_in(g, p, b, k):
    @pl.when(k == 1)
    def _():
        loop(pieces(g), lambda i: arrived(b, p, "wc", piece_of(g, b.W, p.hcore, i), i))

    @pl.when(k == 2)
    def _():
        def on(i):
            part = piece_of(g, b.W, p.hy, i)
            arrived(b, p, "wy", part, i)
            send(b, "wd", part, part, i, i, p.core)

        loop(pieces(g), on)

    @pl.when(k == 3)
    def _():
        loop(pieces(g), lambda i: arrived(b, p, "wd", piece_of(g, b.W, p.hdiag, i), i))


def masks(rows):
    lane = iota((rows, 128), 1)
    return lane < 64, lane >= 64


def attention(g, p, b):
    low, high = masks(g.IP)
    live = iota((g.IP, g.IP), 1) < SEQ
    zero = jnp.zeros((g.IP, 128), BF16)

    def group(k):
        group_in(g, p, b, k)
        gi = 2 * lax.rem(p.y + lax.div(k, 2), 2) + lax.rem(p.c + k, 2)
        for blk in range(2):
            rows = slice(blk * g.IP, (blk + 1) * g.IP)
            b.QKV[gi, rows, :] = nn(b.ACT1[rows, :], b.W[gi, :, 0:640]).astype(BF16)
        for blk in range(2):
            rows = slice(blk * g.IP, (blk + 1) * g.IP)
            outs = []
            for j in range(3):
                qt = b.QKV[gi, rows, (j // 2) * 128 : (j // 2) * 128 + 128]
                kt = b.QKV[gi, rows, 384 + (j // 2) * 128 : 384 + (j // 2) * 128 + 128]
                vt = b.QKV[gi, rows, 128 + ((j + 1) // 2) * 128 : 256 + ((j + 1) // 2) * 128]
                scores = nt(jnp.where(high if j == 1 else low, qt, zero), kt) * (HD**-0.5)
                scores = jnp.where(live, scores, -1e30)
                scores = jnp.exp(scores - jnp.max(scores, axis=1, keepdims=True))
                probs = (scores / jnp.sum(scores, axis=1, keepdims=True)).astype(BF16)
                b.PB[gi, blk * 3 + j] = probs
                outs.append(nn(probs, vt))
            b.ATT[gi, rows, 0:128] = jnp.where(high, outs[0], 0.0).astype(BF16)
            b.ATT[gi, rows, 128:256] = jnp.where(low, outs[1], outs[2]).astype(BF16)
        for blk in range(2):
            rows = slice(blk * g.IP, (blk + 1) * g.IP)
            b.HID[rows, :] += nt(b.ATT[gi, rows, :], b.W[gi, :, 512:768])

    loop(4, group)


def rows16s(count, body):
    run = count // 32

    def step(i):
        for j in range(run):
            body(pl.ds(pl.multiple_of((i * run + j) * 16, 16), 16))

    loop(2, step)


def first_norm(g, b):
    def rows16(rows):
        x = b.x[rows, :].astype(F32)
        normed, _ = normalize(x)
        b.ACT1[rows, :] = (normed * b.GN[0:1, :]).astype(BF16)
        b.HID[rows, :] = x

    rows16s(2 * g.IP, rows16)


def second_norm(g, b):
    def rows16(rows):
        normed, _ = normalize(b.HID[rows, :])
        b.ACT2[rows, :] = (normed * b.GN[1:2, :]).astype(BF16)

    rows16s(2 * g.IP, rows16)
    lane = iota((g.IP, 128), 1)
    for blk in range(2):
        rows = slice(blk * g.IP, (blk + 1) * g.IP)
        logits = jnp.where(lane < g.ne, nn(b.ACT2[rows, :], b.RW[...]), -1e30)
        weight = jnp.exp(logits - jnp.max(logits, axis=1, keepdims=True))
        probs = weight / jnp.sum(weight, axis=1, keepdims=True)
        b.PRB[rows, :] = probs
        top = probs.astype(BF16).astype(F32)
        rest = probs - top
        b.PRH[rows, :] = (top + pltpu.roll(rest, 64, 1)).astype(BF16)


def small_weights(g, b):
    lane = iota((g.D, 128), 1)
    small = b.MI[...].astype(F32)
    b.RW[...] = jnp.where(lane < g.ne, small, 0.0).astype(BF16)
    gains = jnp.transpose(small)[120:128, :]
    b.GN[0:1, :] = gains[0:1, :] + gains[1:2, :]
    b.GN[1:2, :] = gains[2:3, :] + gains[3:4, :]


def half_of(g, i):
    return pl.ds(pl.multiple_of(i * g.DH, 128), g.DH)


def tokens_of(g, blk):
    return pl.ds(pl.multiple_of(blk * g.IP, 16), g.IP)


def tokens_out(g, p, b):
    for at, (device, yy, cc) in enumerate(
        ((p.across, p.oy, p.c), (p.diag, p.oy, p.oc), (p.core, p.y, p.oc))
    ):
        send(b, "ta", b.ACT2.at[tokens_of(g, cc), half_of(g, yy)], b.TA.at[p.h], at, p.h, device)
        send(b, "tp", b.PRH.at[tokens_of(g, cc), :], b.TG.at[p.h], at, p.h, device)
    b.TA[p.h] = b.ACT2[tokens_of(g, p.c), half_of(g, p.y)]
    b.TG[p.h] = b.PRH[tokens_of(g, p.c), :]


def tokens_in(g, p, b):
    for src in (p.hcore, p.hy, p.hdiag):
        arrived(b, p, "ta", b.TA.at[src], src)
        arrived(b, p, "tp", b.TG.at[src], src)


def cotangent_out(g, p, b):
    def pack(k):
        e2 = p.other(k + 1)
        rows = nn(b.P[pack_rows(g, e2), :], b.up[p.c]).astype(BF16)
        b.PKU[e2] = rows

        @pl.when(k < g.ne - 1)
        def _():
            send(b, "uz", b.PKU.at[e2], b.US.at[p.e, p.c], k, p.e, p.along(e2))

        @pl.when(k == g.ne - 1)
        def _():
            b.US[p.e, p.c] = rows
            send(b, "uc", b.US.at[p.e, p.c], b.US.at[p.e, p.c], p.e, p.e, p.core)

    loop(g.ne, pack)


def cotangent_on(g, p, b):
    def relay(k):
        e2 = p.other(k + 1)
        part = b.US.at[e2, p.c]
        arrived(b, p, "uz", part, e2)
        send(b, "uc", part, part, e2, e2, p.core)

    loop(g.ne - 1, relay)


def slots_out(g, p, b):
    row = iota((g.CP, g.DH), 0)
    eye = row == iota((g.CP, g.DH), 1)
    lane = iota((g.CP, 128), 1)

    def pack(k):
        e2 = p.other(k + 1)
        hot = b.P[pack_rows(g, e2), :]
        tok = nn(hot, b.TA[...].reshape(g.TP, g.DH))
        gates = nn(hot, b.TG[...].reshape(g.TP, 128))
        gate = jnp.sum(
            jnp.where((lane == e2) | (lane == e2 + 64), gates, 0.0), axis=1, keepdims=True
        )
        b.GC[e2] = jnp.broadcast_to(gate, (g.CP, 128))
        across = jnp.sum(jnp.where(eye, gate, 0.0), axis=0, keepdims=True)
        top = across.astype(BF16).astype(F32)
        rows = jnp.where(row == g.CAP, top, jnp.where(row == g.CAP + 1, across - top, tok))
        rows = rows.astype(BF16)

        @pl.when(k < g.ne - 1)
        def _():
            b.PKA[e2] = rows
            send(b, "xz", b.PKA.at[e2], b.XS.at[p.e, p.c, p.y], k, p.e, p.along(e2))

        @pl.when(k == g.ne - 1)
        def _():
            part = b.XS.at[p.e, p.c, p.y]
            b.XS[p.e, p.c, p.y] = rows
            send(b, "xy", part, part, p.e, p.e, p.across)
            send(b, "xc", part, part, p.e, p.e, p.core)

    loop(g.ne, pack)


def slots_on(g, p, b, e2):
    part = b.XS.at[e2, p.c, p.y]
    arrived(b, p, "xz", part, e2)
    send(b, "xy", part, part, e2, e2, p.across)
    send(b, "xc", part, part, e2, e2, p.core)


def slots_over(g, p, b, e2):
    part = b.XS.at[e2, p.c, p.oy]
    arrived(b, p, "xy", part, e2)
    send(b, "xd", part, part, e2, e2, p.core)


def slots_in(g, p, b, e2):
    arrived(b, p, "xc", b.XS.at[e2, p.oc, p.y], e2)
    arrived(b, p, "xd", b.XS.at[e2, p.oc, p.oy], e2)
    arrived(b, p, "uc", b.US.at[e2, p.oc], e2)


def experts_out(g, p, b):
    b.WI[p.d] = b.wi[...]
    b.WB[p.d] = b.wb[...]
    send(b, "ei", b.wi, b.WI.at[p.d], 0, 0, p.twin)
    send(b, "eb", b.wb, b.WB.at[p.d], 0, 0, p.twin)


def gelu_parts(u):
    inner = 0.7978845608028654 * (u + 0.044715 * u * u * u)
    tangent = jnp.tanh(inner)
    value = 0.5 * u * (1.0 + tangent)
    slope = 0.5 * (1.0 + tangent) + 0.5 * u * (1.0 - tangent * tangent) * 0.7978845608028654 * (
        1.0 + 3.0 * 0.044715 * u * u
    )
    return value, slope


def expert(g, b, first):
    base = g.CP - 16
    row = iota((g.CP, g.DH), 0)
    eye = row == iota((g.CP, g.DH), 1)
    for i in range(g.SG):
        for blk in range(2):
            tail = b.XS[first + i, blk, 0, base:, :].astype(F32)
            gate = tail[g.CAP - base : g.CAP - base + 1] + tail[g.CAP - base + 1 : g.CAP - base + 2]
            gate = jnp.sum(jnp.where(eye, gate, 0.0), axis=1, keepdims=True)
            at = (i * 2 + blk) * g.CP
            b.GP[at : at + g.CP, :] = (b.US[first + i, blk].astype(F32) * gate).astype(BF16)
    x = [b.XS[pl.ds(first, g.SG), :, q].reshape(g.R, g.DH) for q in range(2)]
    for n in range(g.F // 256):
        cols = slice(n * 256, n * 256 + 256)
        pre = nn(x[0], b.WI[0, :, cols]) + nn(x[1], b.WI[1, :, cols])
        value, slope = gelu_parts(pre)
        b.HQ[:, cols] = value.astype(BF16)
        grad = nt(b.GP[:, : g.DH], b.WB[0, cols, :]) + nt(b.GP[:, g.DH :], b.WB[1, cols, :])
        b.GR[:, cols] = (grad * slope).astype(BF16)
    shape = (g.SG, 2, g.CP, g.DH)
    dots = []
    for q in range(2):
        out = nn(b.HQ[...], b.WB[q]).astype(BF16)
        b.PO[pl.ds(first, g.SG), :, q] = out.reshape(shape)
        up = b.US[pl.ds(first, g.SG), :, :, q * g.DH : (q + 1) * g.DH].reshape(g.R, g.DH)
        dots.append(jnp.sum(out.astype(F32) * up.astype(F32), axis=1, keepdims=True))
        b.DB[q] += tn(b.HQ[...], b.GP[:, q * g.DH : (q + 1) * g.DH])
        b.DI[q] += tn(x[q], b.GR[...])
    dots = dots[0] + dots[1]
    for q in range(2):
        back = nt(b.GR[...], b.WI[q])
        for i in range(g.SG):
            for blk in range(2):
                at = (i * 2 + blk) * g.CP
                along = jnp.sum(jnp.where(eye, dots[at : at + g.CP], 0.0), axis=0, keepdims=True)
                if q == 1:
                    along = along - along.astype(BF16).astype(F32)
                b.PG[first + i, blk, q] = jnp.where(
                    row == g.CAP, along, back[at : at + g.CP]
                ).astype(BF16)


def experts(g, p, b):
    b.DB[...] = jnp.zeros_like(b.DB)
    b.DI[...] = jnp.zeros_like(b.DI)
    n = g.ne
    if g.SG > 1:
        loop(n - 1, lambda k: slots_on(g, p, b, p.other(k + 1)))
        loop(n, lambda k: slots_over(g, p, b, p.other(k)))
        loop(n, lambda k: slots_in(g, p, b, p.other(k)))
        arrived(b, p, "ei", b.WI.at[p.od], 0)
        arrived(b, p, "eb", b.WB.at[p.od], 0)
        loop(n // g.SG, lambda t: expert(g, b, t * g.SG))
        return
    slots_over(g, p, b, p.e)
    slots_in(g, p, b, p.e)
    arrived(b, p, "ei", b.WI.at[p.od], 0)
    arrived(b, p, "eb", b.WB.at[p.od], 0)

    def source(k):
        @pl.when(k == 1)
        def _():
            loop(n - 1, lambda i: slots_on(g, p, b, p.other(i + 1)))

        @pl.when(k > 0)
        def _():
            slots_over(g, p, b, p.other(k))
            slots_in(g, p, b, p.other(k))

        expert(g, b, p.other(k))

    loop(n, source)


def first_sends_end(g, p, b):
    n = g.ne
    if g.aligned:
        own = piece_rows(g, p.d, p.e)

        def z(k):
            left(b, p, "wz", b.wp, k)
            left(b, p, "mz", b.mp, k)

        loop(n - 1, z)

        def x(k):
            left(b, p, "wx", b.wp, k)
            left(b, p, "mx", b.mp, k)

        loop(n, x)

    def w(i):
        for name in ("wy", "wc", "wd"):
            left(b, p, name, piece_of(g, b.W, p.h, i), i)

    loop(pieces(g), w)
    for at in range(3):
        left(b, p, "ta", b.TA.at[0], at)
        left(b, p, "tp", b.TG.at[0], at)

    def slots(k):
        left(b, p, "uz", b.PKU.at[0], k)
        left(b, p, "xz", b.PKA.at[0], k)

    loop(n - 1, slots)

    def on(k):
        left(b, p, "uc", b.US.at[0, 0], k)
        for name in ("xy", "xc", "xd"):
            left(b, p, name, b.XS.at[0, 0, 0], k)

    loop(n, on)
    left(b, p, "ei", b.wi, 0)
    left(b, p, "eb", b.wb, 0)


def first_kernel(g, b):
    p = Place(g)
    p.enter()
    weights_out(g, p, b)
    route(g, p, b)
    weights_on(g, p, b)
    cotangent_out(g, p, b)
    weights_end(g, p, b)
    experts_out(g, p, b)
    small_weights(g, b)
    first_norm(g, b)
    attention(g, p, b)
    second_norm(g, b)
    tokens_out(g, p, b)
    cotangent_on(g, p, b)
    tokens_in(g, p, b)
    slots_out(g, p, b)
    experts(g, p, b)
    b.KI[...] = b.DI[p.d]
    b.KB[...] = b.DB[p.d]
    b.SI[...] = b.DI[p.od].astype(BF16)
    b.SB[...] = b.DB[p.od].astype(BF16)
    first_sends_end(g, p, b)


def grads_of_expert_out(g, p, b):
    send(b, "gi", b.SI, b.XI, 0, 0, p.twin)
    send(b, "gb", b.SB, b.XB, 0, 0, p.twin)


def grads_of_expert_in(g, p, b):
    arrived(b, p, "gi", b.XI, 0)
    b.o_gi[...] = b.KI[...] + b.XI[...].astype(F32)
    arrived(b, p, "gb", b.XB, 0)
    b.o_gb[...] = b.KB[...] + b.XB[...].astype(F32)


def part_of(b, kind):
    return b.PG if kind else b.PO


def returns_start(g, p, b, kind):
    def to_core(k):
        s = p.other(k + 1)
        at = kind * g.ne + s
        send(b, "rc", part_of(b, kind).at[s, p.oc], b.RC.at[kind, s], at, at, p.core)

    loop(g.ne, to_core)


def returns_over(g, p, b, kind):
    def to_across(k):
        s = p.other(k + 1)
        at = kind * g.ne + s
        arrived(b, p, "rc", b.RC.at[kind, s], at)
        b.RC[kind, s, p.oy] = (
            part_of(b, kind)[s, p.c, p.oy].astype(F32) + b.RC[kind, s, p.oy].astype(F32)
        ).astype(BF16)
        send(b, "ry", b.RC.at[kind, s, p.oy], b.RY.at[kind, s], at, at, p.across)

    loop(g.ne, to_across)


def returns_on(g, p, b, kind):
    n = g.ne

    def to_source(k):
        s = p.other(k + 1)
        at = kind * n + s
        arrived(b, p, "ry", b.RY.at[kind, s], at)
        total = (
            part_of(b, kind)[s, p.c, p.y].astype(F32)
            + b.RC[kind, s, p.y].astype(F32)
            + b.RY[kind, s].astype(F32)
        ).astype(BF16)

        @pl.when(k < n - 1)
        def _():
            b.RC[kind, s, p.y] = total
            send(b, "rz", b.RC.at[kind, s, p.y], b.RO.at[kind, p.e], at, kind * n + p.e, p.along(s))

        @pl.when(k == n - 1)
        def _():
            b.RO[kind, p.e] = total

    loop(n, to_source)


def slots_back(g, p, b, kind):
    n = g.ne
    lane = iota((g.CP, 128), 1)
    base = g.CP - 16
    eye = iota((g.CP, g.DH), 0) == iota((g.CP, g.DH), 1)

    def rows_of(k):
        s = p.other(k)

        @pl.when(k > 0)
        def _():
            arrived(b, p, "rz", b.RO.at[kind, s], kind * n + s)

        rows = pack_rows(g, s)
        if kind:
            b.RG[rows, 0 : g.DH] = b.RO[1, s]
            dots = b.RO[1, s, base:, :].astype(F32)[g.CAP - base : g.CAP - base + 1]
            dots = jnp.sum(jnp.where(eye, dots, 0.0), axis=1, keepdims=True)
            b.RG[rows, g.DH :] = jnp.where(lane == s, dots, 0.0).astype(BF16)
        else:
            b.RB[rows, :] = (b.RO[0, s].astype(F32) * b.GC[s][:, 0:1]).astype(BF16)

    loop(n, rows_of)


def unpack(g, p, b, kind):
    name = "ug" if kind else "uo"
    rhs, out, landed = (b.RG, b.UG, b.TR) if kind else (b.RB, b.UO, b.TO)

    def rows(image):
        return nn(b.PT[tokens_of(g, image), :], rhs[...]).astype(BF16)

    for at, (image, device) in enumerate(((p.hy, p.across), (p.hdiag, p.diag), (p.hcore, p.core))):
        out[at] = rows(image)
        send(b, name, out.at[at], landed.at[p.y, tokens_of(g, p.c), :], at, p.h, device)
    landed[p.y, tokens_of(g, p.c), :] = rows(p.h)


def unpacked(g, p, b, kind):
    name = "ug" if kind else "uo"
    landed = b.TR if kind else b.TO
    for hh, cc, yy in ((p.hcore, p.oc, p.y), (p.hy, p.c, p.oy), (p.hdiag, p.oc, p.oy)):
        arrived(b, p, name, landed.at[yy, tokens_of(g, cc), :], hh)


def mix(g, b):
    def rows16(rows):
        for q in range(2):
            cols = slice(q * g.DH, (q + 1) * g.DH)
            b.o_mixed[rows, cols] = (b.HID[rows, cols] + b.TO[q, rows, :].astype(F32)).astype(BF16)

    rows16s(2 * g.IP, rows16)


def tokens_back(g, p, b):
    lane = iota((g.IP, 128), 1)
    b.GA[...] = jnp.zeros_like(b.GA)
    for blk in range(2):
        rows = slice(blk * g.IP, (blk + 1) * g.IP)
        gate = b.TR[0, rows, g.DH :].astype(F32) + b.TR[1, rows, g.DH :].astype(F32)
        probs = b.PRB[rows, :]
        grad = probs * (gate - jnp.sum(probs * gate, axis=1, keepdims=True))
        b.GL[rows, :] = grad.astype(BF16)
        b.GHID[rows, :] = nt(b.GL[rows, :], b.RW[...])

    def rows16(rows):
        normed, inverse = normalize(b.HID[rows, :])
        upstream = b.GHID[rows, :] + jnp.concatenate(
            [b.TR[q, rows, 0 : g.DH].astype(F32) for q in range(2)], axis=1
        )
        prod = upstream * normed
        b.GA[8:16, :] += prod[0:8, :] + prod[8:16, :]
        b.ACT2[rows, :] = (normed * b.GN[1:2, :]).astype(BF16)
        hidden = b.up[rows, :].astype(F32) + norm_backward(upstream, normed, inverse, b.GN[1:2, :])
        b.GHID[rows, :] = hidden
        b.GHL[rows, :] = hidden.astype(BF16)

    rows16s(2 * g.IP, rows16)


def first_norm_again(g, b):
    def rows16(rows):
        normed, _ = normalize(b.x[rows, :].astype(F32))
        b.ACT1[rows, :] = (normed * b.GN[0:1, :]).astype(BF16)

    rows16s(2 * g.IP, rows16)


def attention_back(g, p, b):
    low, high = masks(g.IP)
    zero = jnp.zeros((g.IP, 128), BF16)
    scale = HD**-0.5
    b.DA[...] = jnp.zeros_like(b.DA)

    def group(k):
        @pl.when(k == 1)
        def _():
            returns_on(g, p, b, 0)

        @pl.when(k == 2)
        def _():
            slots_back(g, p, b, 0)
            unpack(g, p, b, 0)

        yk = lax.rem(p.oy + k, 2)
        gi = 2 * yk + lax.rem(p.oc + lax.div(k, 2), 2)
        for blk in range(2):
            rows = slice(blk * g.IP, (blk + 1) * g.IP)
            grad = nn(b.GHL[rows, :], b.W[gi, :, 512:768]).astype(BF16)
            tiles = [grad[:, 0:128], grad[:, 128:256]]
            dq, dk, dv = [], [], []
            for j in range(3):
                probs = b.PB[gi, blk * 3 + j]
                gt = tiles[(j + 1) // 2]
                qt = b.QKV[gi, rows, (j // 2) * 128 : (j // 2) * 128 + 128]
                kt = b.QKV[gi, rows, 384 + (j // 2) * 128 : 384 + (j // 2) * 128 + 128]
                vt = b.QKV[gi, rows, 128 + ((j + 1) // 2) * 128 : 256 + ((j + 1) // 2) * 128]
                grad_probs = nt(jnp.where(low if j == 1 else high, gt, zero), vt)
                wide = probs.astype(F32)
                grad_scores = wide * (
                    grad_probs - jnp.sum(wide * grad_probs, axis=1, keepdims=True)
                )
                grad_scores = (grad_scores * scale).astype(BF16)
                dv.append(tn(probs, gt))
                dq.append(nn(grad_scores, kt))
                dk.append(tn(grad_scores, qt))
            b.GJ[rows, 0:128] = jnp.where(low, dq[0], dq[1]).astype(BF16)
            b.GJ[rows, 128:256] = jnp.where(low, dq[2], dv[0]).astype(BF16)
            b.GJ[rows, 256:384] = jnp.where(low, dv[1], dv[2]).astype(BF16)
            b.GJ[rows, 384:512] = jnp.where(low, dk[0], dk[1]).astype(BF16)
            b.GJ[rows, 512:640] = jnp.where(low, dk[2], 0.0).astype(BF16)
        for blk in range(2):
            rows = slice(blk * g.IP, (blk + 1) * g.IP)
            b.DA[rows, :] += nt(b.GJ[rows, :], b.W[gi, :, 0:640])
        for m in range(g.D // 256):
            cols = slice(m * 256, m * 256 + 256)
            first = tn(b.ACT1[:, cols], b.GJ[...])
            second = tn(b.GHL[:, cols], b.ATT[gi])
            b.DW[gi, cols, 0:512] = first[:, 0:512].astype(BF16)
            b.DW[gi, cols, 512:640] = (first[:, 512:] + second[:, 0:128]).astype(BF16)
            b.DW[gi, cols, 640:768] = second[:, 128:].astype(BF16)

        @pl.when(k < 2)
        def _():
            send(b, "dc", b.DW.at[gi], b.RDC.at[yk], yk, yk, p.core)

        @pl.when(k >= 2)
        def _():
            arrived(b, p, "dc", b.RDC.at[yk], yk)
            if g.aligned:

                def to_twin(i):
                    e2 = p.other(i + 1)
                    rows = piece_rows(g, p.od, e2)
                    at = yk * g.ne + e2
                    b.DW[gi, rows, :] = (
                        b.DW[gi, rows, :].astype(F32) + b.RDC[yk, rows, :].astype(F32)
                    ).astype(BF16)
                    send(b, "dx", b.DW.at[gi, rows, :], b.RDX.at[yk, e2], at, at, p.twin)

                loop(g.ne, to_twin)

    loop(4, group)


def inputs_back(g, p, b):
    def rows16(rows):
        normed, inverse = normalize(b.x[rows, :].astype(F32))
        upstream = b.DA[rows, :]
        prod = upstream * normed
        b.GA[0:8, :] += prod[0:8, :] + prod[8:16, :]
        b.GIN[rows, :] = (
            b.GHID[rows, :] + norm_backward(upstream, normed, inverse, b.GN[0:1, :])
        ).astype(BF16)

    rows16s(2 * g.IP, rows16)
    for blk in range(2):
        part = b.GIN.at[blk * g.IP : (blk + 1) * g.IP, :]
        send(b, "iy", part, b.o_gin.at[blk, p.h], blk, blk, p.across)
        send(b, "ic", part, b.o_gin.at[blk, p.h], blk, blk, p.core)
    for blk in range(2):
        b.o_gin[blk, p.h] = b.GIN[blk * g.IP : (blk + 1) * g.IP, :]


def inputs_end(g, p, b):
    for blk in range(2):
        part = b.o_gin.at[blk, p.hy]
        arrived(b, p, "iy", part, blk)
        send(b, "id", part, part, blk, blk, p.core)
    for blk in range(2):
        arrived(b, p, "ic", b.o_gin.at[blk, p.hcore], blk)
        arrived(b, p, "id", b.o_gin.at[blk, p.hdiag], blk)


def weights_back(g, p, b):
    if not g.aligned:
        b.DW[p.hy] = (b.DW[p.hy].astype(F32) + b.RDC[p.oy].astype(F32)).astype(BF16)
        send(b, "dy", b.DW.at[p.hy], b.RDY, 0, 0, p.across)
        return

    def to_across(i):
        e2 = p.other(i + 1)
        rows = piece_rows(g, p.d, e2)
        arrived(b, p, "dx", b.RDX.at[p.oy, e2], p.oy * g.ne + e2)
        b.RDX[p.oy, e2] = (
            b.DW[p.hy, rows, :].astype(F32)
            + b.RDC[p.oy, rows, :].astype(F32)
            + b.RDX[p.oy, e2].astype(F32)
        ).astype(BF16)
        send(b, "dy", b.RDX.at[p.oy, e2], b.RDY.at[e2], e2, e2, p.across)

    loop(g.ne, to_across)


def weights_back_on(g, p, b):
    if not g.aligned:
        arrived(b, p, "dy", b.RDY, 0)
        total = b.DW[p.h].astype(F32) + b.RDC[p.y].astype(F32) + b.RDY[...].astype(F32)
        b.o_dw[...] = total.astype(BF16)
        return

    def piece(k):
        e2 = p.other(k + 1)
        rows = piece_rows(g, p.d, e2)
        arrived(b, p, "dx", b.RDX.at[p.y, e2], p.y * g.ne + e2)
        arrived(b, p, "dy", b.RDY.at[e2], e2)
        mine = (
            b.DW[p.h, rows, :].astype(F32)
            + b.RDC[p.y, rows, :].astype(F32)
            + b.RDX[p.y, e2].astype(F32)
            + b.RDY[e2].astype(F32)
        )

        @pl.when(k < g.ne - 1)
        def _():
            b.SDZ[e2] = mine.astype(BF16)
            send(b, "dz", b.SDZ.at[e2], b.RDZ.at[p.e], k, p.e, p.along(e2))

        @pl.when(k == g.ne - 1)
        def _():
            b.o_dw[...] = mine

    loop(g.ne, piece)


def weights_back_end(g, p, b):
    if not g.aligned:
        return

    def add(k):
        e2 = p.other(k + 1)
        arrived(b, p, "dz", b.RDZ.at[e2], e2)
        b.o_dw[...] += b.RDZ[e2].astype(F32)

    loop(g.ne - 1, add)


def small_back(g, p, b):
    sub = iota((128, g.D), 0)
    one = jnp.sum(b.GA[0:8, :], axis=0, keepdims=True)
    two = jnp.sum(b.GA[8:16, :], axis=0, keepdims=True)
    gains = jnp.where(sub == 120, one, jnp.where(sub == 122, two, 0.0))
    b.GM[...] = tn(b.ACT2[...], b.GL[...]) + jnp.transpose(gains)
    if g.aligned:
        half = g.D // 2
        b.SMX[...] = b.GM[pl.ds(pl.multiple_of(p.od * half, 16), half), :].astype(BF16)
        send(b, "sx", b.SMX, b.RMX, 0, 0, p.twin)


def small_back_on(g, p, b):
    if g.aligned:
        arrived(b, p, "sx", b.RMX, 0)

        def piece(k):
            e2 = p.other(k + 1)
            mine = b.GM[piece_rows(g, p.d, e2), :] + b.RMX[
                pl.ds(pl.multiple_of(e2 * g.PR, 16), g.PR), :
            ].astype(F32)

            @pl.when(k < g.ne - 1)
            def _():
                b.SMZ[e2] = mine.astype(BF16)
                send(b, "sz", b.SMZ.at[e2], b.RMZ.at[p.e], k, p.e, p.along(e2))

            @pl.when(k == g.ne - 1)
            def _():
                b.o_small[...] = mine

        loop(g.ne, piece)

        def add(k):
            e2 = p.other(k + 1)
            arrived(b, p, "sz", b.RMZ.at[e2], e2)
            b.o_small[...] += b.RMZ[e2].astype(F32)

        loop(g.ne - 1, add)
    else:
        b.o_small[...] = b.GM[...]
    b.SMC[...] = b.o_small[...].astype(BF16)
    send(b, "sc", b.SMC, b.RMC, 0, 0, p.core)
    arrived(b, p, "sc", b.RMC, 0)
    b.SMY[...] = (b.SMC[...].astype(F32) + b.RMC[...].astype(F32)).astype(BF16)
    send(b, "sy", b.SMY, b.RMY, 0, 0, p.across)
    arrived(b, p, "sy", b.RMY, 0)
    b.o_small[...] = b.SMY[...].astype(F32) + b.RMY[...].astype(F32)


def second_sends_end(g, p, b):
    n = g.ne
    left(b, p, "gi", b.SI, 0)
    left(b, p, "gb", b.SB, 0)

    def rets(k):
        left(b, p, "rc", b.RC.at[0, 0], k)
        left(b, p, "ry", b.RY.at[0, 0], k)

    loop(2 * n, rets)

    def away(k):
        s = p.other(k + 1)
        left(b, p, "rz", b.RY.at[0, 0], s)
        left(b, p, "rz", b.RY.at[0, 0], n + s)
        if g.aligned:
            left(b, p, "dz", b.SDZ.at[0], k)
            left(b, p, "sz", b.SMZ.at[0], k)

    loop(n - 1, away)
    for at in range(3):
        left(b, p, "ug", b.UG.at[0], at)
        left(b, p, "uo", b.UO.at[0], at)
    for i in range(2):
        left(b, p, "dc", b.RDC.at[0], i)
        for name in ("iy", "ic", "id"):
            left(b, p, name, b.o_gin.at[0, 0], i)
    if g.aligned:
        left(b, p, "sx", b.SMX, 0)

        def moved(k):
            left(b, p, "dx", b.RDX.at[0, 0], k)
            left(b, p, "dx", b.RDX.at[0, 0], g.ne + k)
            left(b, p, "dy", b.RDY.at[0], k)

        loop(n, moved)
    else:
        left(b, p, "dy", b.RDY, 0)
    left(b, p, "sc", b.SMC, 0)
    left(b, p, "sy", b.SMY, 0)


def second_kernel(g, b):
    p = Place(g)
    p.enter()
    returns_start(g, p, b, 1)
    returns_start(g, p, b, 0)
    grads_of_expert_out(g, p, b)
    returns_over(g, p, b, 1)
    first_norm_again(g, b)
    returns_on(g, p, b, 1)
    slots_back(g, p, b, 1)
    unpack(g, p, b, 1)
    unpacked(g, p, b, 1)
    returns_over(g, p, b, 0)
    tokens_back(g, p, b)
    attention_back(g, p, b)
    inputs_back(g, p, b)
    weights_back(g, p, b)
    small_back(g, p, b)
    inputs_end(g, p, b)
    weights_back_on(g, p, b)
    unpacked(g, p, b, 0)
    mix(g, b)
    small_back_on(g, p, b)
    grads_of_expert_in(g, p, b)
    weights_back_end(g, p, b)
    second_sends_end(g, p, b)


def call(body, g, inputs, outs, scratch, sems, number, flops):
    names = [*inputs, *outs, *scratch]
    names += [name + end for name in sems for end in ("_s", "_r")]

    def kernel(*refs):
        body(g, types.SimpleNamespace(**dict(zip(names, refs, strict=True))))

    vmem = pl.BlockSpec(memory_space=pltpu.VMEM)
    made = pl.pallas_call(
        kernel,
        out_shape=[jax.ShapeDtypeStruct(*o) for o in outs.values()],
        in_specs=[vmem] * len(inputs),
        out_specs=[vmem] * len(outs),
        scratch_shapes=[pltpu.VMEM(*s) for s in scratch.values()]
        + [pltpu.SemaphoreType.DMA((n,)) for n in sems.values() for _ in range(2)],
        compiler_params=pltpu.CompilerParams(
            collective_id=number, has_side_effects=True, vmem_limit_bytes=LIMIT
        ),
        cost_estimate=pl.CostEstimate(flops=flops, bytes_accessed=2**24, transcendentals=0),
    )(*inputs.values())
    return dict(zip(outs, made, strict=True))


def shards(
    inputs, w_qkv, w_out, w_router, gain_one, gain_two, w_in, w_back, experts, priority, cotangent, *, mesh
):
    model, rows = inputs.shape[2], inputs.shape[1]
    g = Sizes(mesh, model, rows, w_in.shape[2])
    n, ip, cp, dh = g.ne, g.IP, g.CP, g.DH
    assert inputs.shape[0] == 2
    h = lax.axis_index("head")
    pad = ((0, 0), (0, 0), (0, ip - SEQ), (0, 0))
    x_all = inputs.reshape(2, g.NI, SEQ, model)
    x = jnp.pad(lax.dynamic_slice_in_dim(x_all, h, 1, 1), pad).reshape(2 * ip, model)
    up_all = jnp.pad(cotangent.reshape(2, g.NI, SEQ, model), pad)
    up_own = lax.dynamic_slice_in_dim(up_all, h, 1, 1).reshape(2 * ip, model)
    part = jnp.concatenate([w_qkv[:, 0], w_qkv[:, 2], w_qkv[:, 1], w_out.T], axis=1)
    gains = jnp.stack([gain_one, gain_two], axis=1)
    top = gains.astype(BF16)
    rest = (gains - top.astype(F32)).astype(BF16)
    small = jnp.concatenate(
        [
            w_router,
            jnp.zeros((w_router.shape[0], 120 - n), BF16),
            top[:, :1],
            rest[:, :1],
            top[:, 1:],
            rest[:, 1:],
            jnp.zeros((w_router.shape[0], 4), BF16),
        ],
        axis=1,
    )
    if not g.aligned:
        part = lax.all_gather(part, ("dp", "expert"), axis=0, tiled=True)
        small = lax.all_gather(small, ("dp", "expert"), axis=0, tiled=True)
    info = jnp.concatenate([experts, priority[:, :, None]], axis=2).astype(F32)
    info = jnp.pad(info.reshape(2, g.NI, SEQ, 3), pad, constant_values=-1000.0)
    mc = jnp.pad(info.reshape(2, g.TP, 3), ((0, 0), (0, 0), (0, 5)))
    mr = jnp.swapaxes(mc, 1, 2)
    np_ = pieces(g)
    one = call(
        first_kernel,
        g,
        dict(x=x, up=up_all.reshape(2, g.TP, model), wp=part, mp=small, wi=w_in[0], wb=w_back[0], mc=mc, mr=mr),
        dict(
            W=((4, model, model), BF16),
            RW=((model, 128), BF16),
            GN=((8, model), F32),
            QKV=((4, 2 * ip, 640), BF16),
            PB=((4, 6, ip, ip), BF16),
            ATT=((4, 2 * ip, 256), BF16),
            HID=((2 * ip, model), F32),
            PRB=((2 * ip, 128), F32),
            PT=((g.TP, g.SL), BF16),
            GC=((n, cp, 128), F32),
            PO=((n, 2, 2, cp, dh), BF16),
            PG=((n, 2, 2, cp, dh), BF16),
            KI=((dh, g.F), F32),
            KB=((g.F, dh), F32),
            SI=((dh, g.F), BF16),
            SB=((g.F, dh), BF16),
        ),
        dict(
            DI=((2, dh, g.F), F32),
            DB=((2, g.F, dh), F32),
            MI=((model, 128), BF16),
            L=((g.TP, g.TP), BF16),
            O=((g.TP, 128), BF16),
            P=((g.SL, g.TP), BF16),
            ACT1=((2 * ip, model), BF16),
            ACT2=((2 * ip, model), BF16),
            PRH=((2 * ip, 128), BF16),
            TA=((4, ip, dh), BF16),
            TG=((4, ip, 128), BF16),
            US=((n, 2, cp, model), BF16),
            XS=((n, 2, 2, cp, dh), BF16),
            PKA=((n, cp, dh), BF16),
            PKU=((n, cp, model), BF16),
            WI=((2, dh, g.F), BF16),
            WB=((2, g.F, dh), BF16),
            GP=((g.R, model), BF16),
            HQ=((g.R, g.F), BF16),
            GR=((g.R, g.F), BF16),
        ),
        dict(wz=n, mz=n, wx=n, mx=n, wy=np_, wc=np_, wd=np_, ta=4, tp=4, uz=n, uc=n, xz=n, xy=n, xc=n, xd=n, ei=1, eb=1),
        1,
        14 * 10**9,
    )
    keep = ("W", "RW", "GN", "QKV", "PB", "ATT", "HID", "PRB", "PT", "GC", "PO", "PG", "KI", "KB", "SI", "SB")
    rows_out = g.PR if g.aligned else model
    extra = (
        dict(
            RDX=((2, n, g.PR, model), BF16),
            SDZ=((n, g.PR, model), BF16),
            RDZ=((n, g.PR, model), BF16),
            SMX=((model // 2, 128), BF16),
            RMX=((model // 2, 128), BF16),
            SMZ=((n, g.PR, 128), BF16),
            RMZ=((n, g.PR, 128), BF16),
        )
        if g.aligned
        else {}
    )
    two = call(
        second_kernel,
        g,
        dict(x=x, up=up_own, **{name: one[name] for name in keep}),
        dict(
            o_mixed=((2 * ip, model), BF16),
            o_gin=((2, 4, ip, model), BF16),
            o_dw=((rows_out, model), F32 if g.aligned else BF16),
            o_small=((rows_out, 128), F32),
            o_gi=((dh, g.F), F32),
            o_gb=((g.F, dh), F32),
        ),
        dict(
            RC=((2, n, 2, cp, dh), BF16),
            RY=((2, n, cp, dh), BF16),
            RO=((2, n, cp, dh), BF16),
            RG=((g.SL, dh + 128), BF16),
            RB=((g.SL, dh), BF16),
            UG=((3, ip, dh + 128), BF16),
            UO=((3, ip, dh), BF16),
            TR=((2, 2 * ip, dh + 128), BF16),
            TO=((2, 2 * ip, dh), BF16),
            GL=((2 * ip, 128), BF16),
            GA=((16, model), F32),
            ACT1=((2 * ip, model), BF16),
            ACT2=((2 * ip, model), BF16),
            GHID=((2 * ip, model), F32),
            GHL=((2 * ip, model), BF16),
            DA=((2 * ip, model), F32),
            GJ=((2 * ip, 640), BF16),
            DW=((4, model, model), BF16),
            RDC=((2, model, model), BF16),
            RDY=((n, g.PR, model) if g.aligned else (model, model), BF16),
            GIN=((2 * ip, model), BF16),
            GM=((model, 128), F32),
            SMC=((rows_out, 128), BF16),
            RMC=((rows_out, 128), BF16),
            SMY=((rows_out, 128), BF16),
            RMY=((rows_out, 128), BF16),
            XI=((dh, g.F), BF16),
            XB=((g.F, dh), BF16),
            **extra,
        ),
        dict(rc=2 * n, ry=2 * n, rz=2 * n, ug=4, uo=4, gi=1, gb=1, dc=2, dy=n, dx=2 * n, dz=n, sx=1, sz=n, sc=1, sy=1, iy=2, ic=2, id=2),
        2,
        14 * 10**9,
    )
    mixed = two["o_mixed"].reshape(2, ip, model)[:, :SEQ]
    grad_inputs = two["o_gin"][:, :, :SEQ].reshape(2, rows, model)
    dw, ds = two["o_dw"], two["o_small"]
    if not g.aligned:
        dw = lax.psum_scatter(dw, ("dp", "expert"), scatter_dimension=0, tiled=True)
        ds = lax.psum_scatter(ds.astype(BF16), ("dp", "expert"), scatter_dimension=0, tiled=True)
        dw, ds = dw.astype(F32), ds.astype(F32)
    lw = g.LW
    grad_qkv = jnp.stack([dw[:, :lw], dw[:, 2 * lw : 3 * lw], dw[:, lw : 2 * lw]], axis=1)
    return (
        mixed,
        grad_inputs,
        grad_qkv,
        dw[:, 3 * lw :].T,
        ds[:, :n],
        ds[:, 120],
        ds[:, 122],
        two["o_gi"][None],
        two["o_gb"][None],
    )


def solution(mesh):
    both = ("dp", "expert")
    in_specs = (
        P(both, None, None),
        P(both, None, "head"),
        P("head", both),
        P(both, None),
        P(both),
        P(both),
        P("expert", "dp", "head"),
        P("expert", "head", "dp"),
        P(both, None, None),
        P(both, None),
        P(both, None, None),
    )
    out_specs = (
        P(both, "head", None),
        P(both, None, None),
        P(both, None, "head"),
        P("head", both),
        P(both, None),
        P(both),
        P(both),
        P("expert", "dp", "head"),
        P("expert", "head", "dp"),
    )
    return jax.shard_map(
        functools.partial(shards, mesh=mesh),
        mesh=mesh,
        in_specs=in_specs,
        out_specs=out_specs,
        check_vma=False,
    )
```

```python
import functools
import types

import jax
import jax.numpy as jnp
from jax import lax
from jax.experimental import pallas as pl
from jax.experimental.pallas import tpu as pltpu
from jax.sharding import PartitionSpec as P

HD = 64
SEQ = 196
MESH = pl.DeviceIdType.MESH
F32, BF16 = jnp.float32, jnp.bfloat16
LIMIT = 63 * 2**20


def up16(n):
    return -(-n // 16) * 16


def nn(a, b):
    return lax.dot_general(a, b, (((1,), (0,)), ((), ())), preferred_element_type=F32)


def nt(a, b):
    return lax.dot_general(a, b, (((1,), (1,)), ((), ())), preferred_element_type=F32)


def tn(a, b):
    return lax.dot_general(a, b, (((0,), (0,)), ((), ())), preferred_element_type=F32)


def loop(count, body):
    def step(i, carry):
        body(i)
        return carry

    lax.fori_loop(0, count, step, 0)


def iota(shape, dim):
    return lax.broadcasted_iota(jnp.int32, shape, dim)


def fiota(shape, dim):
    return iota(shape, dim).astype(F32)


def normalize(v):
    centered = v - jnp.mean(v, axis=1, keepdims=True)
    inverse = lax.rsqrt(jnp.mean(centered * centered, axis=1, keepdims=True) + 1e-06)
    return centered * inverse, inverse


def norm_backward(upstream, normed, inverse, gain):
    scaled = upstream * gain
    return inverse * (
        scaled
        - jnp.mean(scaled, axis=1, keepdims=True)
        - normed * jnp.mean(scaled * normed, axis=1, keepdims=True)
    )


class Sizes:
    def __init__(self, mesh, model, rows, hidden):
        self.nd, self.ne, self.nh = mesh.shape["dp"], mesh.shape["expert"], mesh.shape["head"]
        self.D, self.DH = model, model // 2
        self.M = rows
        self.CAP = rows // self.ne
        self.CP = up16(self.CAP + 2)
        self.IP = up16(SEQ)
        self.NI = rows // SEQ
        self.TP = self.NI * self.IP
        self.SL = self.ne * self.CP
        self.WIN = self.IP - 16
        self.LAG = SEQ - self.WIN
        self.F = hidden
        self.PR = model // (self.nd * self.ne)
        self.aligned = self.PR % 16 == 0
        self.SG = 1
        while self.SG * 2 * self.CP <= self.IP and self.ne % (self.SG * 2) == 0:
            self.SG *= 2
        self.R = self.SG * 2 * self.CP
        self.LW = model // self.nh
        assert self.nd == 2 and self.nh == 4 and self.NI == 4 and self.LW == 3 * HD
        assert (self.NI - 1) * self.WIN + self.IP <= rows and (self.NI - 1) * self.LAG + SEQ <= self.IP
        assert self.ne <= 64 and 0 <= self.CAP - (self.CP - 16) <= 14


class Place:
    def __init__(self, g):
        self.ne = g.ne
        self.d = lax.axis_index("dp")
        self.e = lax.axis_index("expert")
        self.h = lax.axis_index("head")
        self.y = lax.div(self.h, 2)
        self.c = lax.rem(self.h, 2)
        self.oy, self.oc, self.od = 1 - self.y, 1 - self.c, 1 - self.d
        self.hcore = 2 * self.y + self.oc
        self.hy = 2 * self.oy + self.c
        self.hdiag = 2 * self.oy + self.oc
        self.core = (self.d, self.e, self.hcore)
        self.across = (self.d, self.e, self.hy)
        self.diag = (self.d, self.e, self.hdiag)
        self.twin = (self.od, self.e, self.h)

    def other(self, k):
        return lax.rem(self.e + k, self.ne)

    def along(self, e2):
        return (self.d, e2, self.h)

    def enter(self):
        barrier = pltpu.get_barrier_semaphore()

        def tell(device):
            pl.semaphore_signal(barrier, inc=1, device_id=device, device_id_type=MESH)

        for device in (self.core, self.across, self.diag, self.twin):
            tell(device)
        loop(self.ne - 1, lambda k: tell(self.along(self.other(k + 1))))
        pl.semaphore_wait(barrier, 4 + self.ne - 1)


def copy(b, name, src, dst, si, ri, device):
    return pltpu.make_async_remote_copy(
        src_ref=src,
        dst_ref=dst,
        send_sem=getattr(b, name + "_s").at[si],
        recv_sem=getattr(b, name + "_r").at[ri],
        device_id=device,
        device_id_type=MESH,
    )


def send(b, name, src, dst, si, ri, device):
    copy(b, name, src, dst, si, ri, device).start()


def arrived(b, p, name, ref, ri):
    copy(b, name, ref, ref, 0, ri, p.core).wait_recv()


def left(b, p, name, ref, si):
    copy(b, name, ref, ref, si, 0, p.core).wait_send()


def fetch(b, name, src, dst, i=0):
    pltpu.make_async_copy(src, dst, getattr(b, name + "_s").at[i]).start()


def fetched(b, name, src, dst, i=0):
    pltpu.make_async_copy(src, dst, getattr(b, name + "_s").at[i]).wait()


def stow(b, *names):
    for name in names:
        fetch(b, "k" + name, getattr(b, name), getattr(b, "h" + name))


def stowed(b, *names):
    for name in names:
        fetched(b, "k" + name, getattr(b, name), getattr(b, "h" + name))


def load(b, *names):
    for name in names:
        fetch(b, "k" + name, getattr(b, "h" + name), getattr(b, name))


def loaded(b, *names):
    for name in names:
        fetched(b, "k" + name, getattr(b, "h" + name), getattr(b, name))


def shift(g, image, back=False):
    row, col = iota((g.IP, g.IP), 0), iota((g.IP, g.IP), 1)
    if back:
        hot = (row == col + g.LAG * image) & (col < SEQ)
    else:
        hot = (col == row + g.LAG * image) & (row < SEQ)
    return jnp.where(hot, 1.0, 0.0).astype(BF16)


def window(g, image):
    return pl.ds(pl.multiple_of(image * g.WIN, 16), g.IP)


def rows_out(g, p, b):
    for j in range(2):
        rows = slice(j * g.IP, (j + 1) * g.IP)
        fetch(b, "ldx", b.xin.at[p.y, window(g, 2 * p.c + j), :], b.X.at[rows, :], j)
        fetch(b, "ldu", b.uin.at[p.y, window(g, 2 * p.c + j), :], b.UPO.at[rows, :], j)
    fetch(b, "ldb", b.uin.at[p.c], b.UB)


def rows_in(g, p, b):
    for j in range(2):
        rows = slice(j * g.IP, (j + 1) * g.IP)
        fetched(b, "ldx", b.xin.at[p.y, window(g, 2 * p.c + j), :], b.X.at[rows, :], j)
        fetched(b, "ldu", b.uin.at[p.y, window(g, 2 * p.c + j), :], b.UPO.at[rows, :], j)
        hot = shift(g, 2 * p.c + j)
        b.X[rows, :] = nn(hot, b.X[rows, :]).astype(BF16)
        b.UPO[rows, :] = nn(hot, b.UPO[rows, :]).astype(BF16)
    fetched(b, "ldb", b.uin.at[p.c], b.UB)
    for i in range(g.NI):
        b.UPP[i * g.IP : (i + 1) * g.IP, :] = nn(
            shift(g, i), b.UB[i * g.WIN : i * g.WIN + g.IP, :]
        ).astype(BF16)


def route(g, b, c, both):
    pr_row, e0r, e1r = b.mr[c, 2:3, :], b.mr[c, 0:1, :], b.mr[c, 1:2, :]
    lane = fiota((g.IP, 128), 1)
    base = jnp.zeros((1, 128), F32)
    for i in range(g.NI):
        rows = slice(i * g.IP, (i + 1) * g.IP)
        col = b.mc[c, rows, :]
        e0c, e1c, prc = col[:, 0:1], col[:, 1:2], col[:, 2:3]
        b.L[rows, :] = jnp.where(pr_row < prc, 1.0, 0.0).astype(BF16)
        b.O[rows, :] = jnp.where((lane == e0c) | (lane == e1c + 64.0), 1.0, 0.0).astype(BF16)
        base = base + jnp.sum(jnp.where(lane == e0c + 64.0, 1.0, 0.0), axis=0, keepdims=True)
    slot_lane = fiota((g.IP, g.SL), 1)
    for i in range(g.NI if both else 0):
        rows = slice(i * g.IP, (i + 1) * g.IP)
        col = b.mc[c, rows, :]
        e0c, e1c = col[:, 0:1], col[:, 1:2]
        own = b.O[rows, :].astype(F32)
        earlier = nn(b.L[rows, :], b.O[...])
        s0 = jnp.sum(jnp.where(lane < 64.0, earlier * own, 0.0), axis=1, keepdims=True)
        s1 = jnp.sum(jnp.where(lane < 64.0, 0.0, (earlier + base) * own), axis=1, keepdims=True)
        t0 = jnp.where(s0 < g.CAP, e0c * g.CP + s0, -1.0)
        t1 = jnp.where(s1 < g.CAP, e1c * g.CP + s1, -1.0)
        b.PT[rows, :] = jnp.where((slot_lane == t0) | (slot_lane == t1), 1.0, 0.0).astype(BF16)
    sub = fiota((128, g.TP), 0)
    own = jnp.where((sub == e0r) | (sub == e1r + 64.0), 1.0, 0.0)
    base = jnp.sum(jnp.where(sub == e0r + 64.0, 1.0, 0.0), axis=1, keepdims=True)
    earlier = nt(own.astype(BF16), b.L[...])
    s0 = jnp.sum(jnp.where(sub < 64.0, earlier * own, 0.0), axis=0, keepdims=True)
    s1 = jnp.sum(jnp.where(sub < 64.0, 0.0, (earlier + base) * own), axis=0, keepdims=True)
    t0 = jnp.where(s0 < g.CAP, e0r * g.CP + s0, -1.0)
    t1 = jnp.where(s1 < g.CAP, e1r * g.CP + s1, -1.0)
    slot_sub = fiota((g.CP, g.TP), 0)

    def fill(e2):
        at = slot_sub + (e2 * g.CP).astype(F32)
        b.P[pl.ds(pl.multiple_of(e2 * g.CP, 16), g.CP), :] = jnp.where(
            (at == t0) | (at == t1), 1.0, 0.0
        ).astype(BF16)

    loop(g.ne, fill)


def pack_rows(g, e2):
    return pl.ds(pl.multiple_of(e2 * g.CP, 16), g.CP)


def piece_rows(g, d, e2):
    return pl.ds(pl.multiple_of((d * g.ne + e2) * g.PR, 16), g.PR)


def weights_out(g, p, b):
    own = piece_rows(g, p.d, p.e)
    if g.aligned:
        mine = p.d * g.ne + p.e

        def to_expert(k):
            device = p.along(p.other(k + 1))
            send(b, "wz", b.wp, b.W.at[p.h, own, :], k, p.e, device)
            send(b, "mz", b.mp, b.MI.at[own, :], k, p.e, device)

        loop(g.ne - 1, to_expert)
        send(b, "wx", b.wp, b.W.at[p.h, own, :], p.e, p.e, p.twin)
        send(b, "mx", b.mp, b.MI.at[own, :], p.e, p.e, p.twin)
        send(b, "wy", b.wp, b.W.at[p.h, own, :], mine, mine, p.across)
        send(b, "wc", b.wp, b.W.at[p.h, own, :], mine, mine, p.core)
        b.W[p.h, own, :] = b.wp[...]
        b.MI[own, :] = b.mp[...]
    else:
        send(b, "wy", b.wp, b.W.at[p.h], 0, 0, p.across)
        send(b, "wc", b.wp, b.W.at[p.h], 0, 0, p.core)
        b.W[p.h] = b.wp[...]
        b.MI[...] = b.mp[...]


def weights_on(g, p, b):
    if not g.aligned:
        return

    def relay(k):
        e2 = p.other(k + 1)
        rows = piece_rows(g, p.d, e2)
        at = p.d * g.ne + e2
        part = b.W.at[p.h, rows, :]
        arrived(b, p, "wz", part, e2)
        send(b, "wx", part, part, e2, e2, p.twin)
        send(b, "wy", part, part, at, at, p.across)
        send(b, "wc", part, part, at, at, p.core)
        part = b.MI.at[rows, :]
        arrived(b, p, "mz", part, e2)
        send(b, "mx", part, part, e2, e2, p.twin)

    loop(g.ne - 1, relay)


def weights_end(g, p, b):
    if not g.aligned:
        return

    def relay(k):
        e2 = p.other(k)
        rows = piece_rows(g, p.od, e2)
        at = p.od * g.ne + e2
        part = b.W.at[p.h, rows, :]
        arrived(b, p, "wx", part, e2)
        send(b, "wy", part, part, at, at, p.across)
        send(b, "wc", part, part, at, at, p.core)
        arrived(b, p, "mx", b.MI.at[rows, :], e2)

    loop(g.ne, relay)


def pieces(g):
    return g.nd * g.ne if g.aligned else 1


def piece_of(g, ref, group, i):
    if not g.aligned:
        return ref.at[group]
    return ref.at[group, pl.ds(pl.multiple_of(i * g.PR, 16), g.PR), :]


def group_in(g, p, b, k):
    @pl.when(k == 1)
    def _():
        loop(pieces(g), lambda i: arrived(b, p, "wc", piece_of(g, b.W, p.hcore, i), i))

    @pl.when(k == 2)
    def _():
        def on(i):
            part = piece_of(g, b.W, p.hy, i)
            arrived(b, p, "wy", part, i)
            send(b, "wd", part, part, i, i, p.core)

        loop(pieces(g), on)

    @pl.when(k == 3)
    def _():
        loop(pieces(g), lambda i: arrived(b, p, "wd", piece_of(g, b.W, p.hdiag, i), i))


def masks(rows):
    lane = iota((rows, 128), 1)
    return lane < 64, lane >= 64


def attention(g, p, b):
    low, high = masks(g.IP)
    live = iota((g.IP, g.IP), 1) < SEQ
    zero = jnp.zeros((g.IP, 128), BF16)

    def group(k):
        group_in(g, p, b, k)
        gi = 2 * lax.rem(p.y + lax.div(k, 2), 2) + lax.rem(p.c + k, 2)
        for blk in range(2):
            rows = slice(blk * g.IP, (blk + 1) * g.IP)
            b.QKV[gi, rows, :] = nn(b.ACT1[rows, :], b.W[gi, :, 0:640]).astype(BF16)
        for blk in range(2):
            rows = slice(blk * g.IP, (blk + 1) * g.IP)
            outs = []
            for j in range(3):
                qt = b.QKV[gi, rows, (j // 2) * 128 : (j // 2) * 128 + 128]
                kt = b.QKV[gi, rows, 384 + (j // 2) * 128 : 384 + (j // 2) * 128 + 128]
                vt = b.QKV[gi, rows, 128 + ((j + 1) // 2) * 128 : 256 + ((j + 1) // 2) * 128]
                scores = nt(jnp.where(high if j == 1 else low, qt, zero), kt) * (HD**-0.5)
                scores = jnp.where(live, scores, -1e30)
                scores = jnp.exp(scores - jnp.max(scores, axis=1, keepdims=True))
                probs = (scores / jnp.sum(scores, axis=1, keepdims=True)).astype(BF16)
                b.PB[gi, blk * 3 + j] = probs
                outs.append(nn(probs, vt))
            b.ATT[gi, rows, 0:128] = jnp.where(high, outs[0], 0.0).astype(BF16)
            b.ATT[gi, rows, 128:256] = jnp.where(low, outs[1], outs[2]).astype(BF16)
        for blk in range(2):
            rows = slice(blk * g.IP, (blk + 1) * g.IP)
            b.HID[rows, :] += nt(b.ATT[gi, rows, :], b.W[gi, :, 512:768])

    loop(4, group)


def rows16s(count, body):
    run = count // 32

    def step(i):
        for j in range(run):
            body(pl.ds(pl.multiple_of((i * run + j) * 16, 16), 16))

    loop(2, step)


def first_norm(g, b):
    def rows16(rows):
        x = b.X[rows, :].astype(F32)
        normed, _ = normalize(x)
        b.ACT1[rows, :] = (normed * b.GN[0:1, :]).astype(BF16)
        b.HID[rows, :] = x

    rows16s(2 * g.IP, rows16)


def second_norm(g, b):
    def rows16(rows):
        normed, _ = normalize(b.HID[rows, :])
        b.ACT2[rows, :] = (normed * b.GN[1:2, :]).astype(BF16)

    rows16s(2 * g.IP, rows16)
    lane = iota((g.IP, 128), 1)
    for blk in range(2):
        rows = slice(blk * g.IP, (blk + 1) * g.IP)
        logits = jnp.where(lane < g.ne, nn(b.ACT2[rows, :], b.RW[...]), -1e30)
        weight = jnp.exp(logits - jnp.max(logits, axis=1, keepdims=True))
        probs = weight / jnp.sum(weight, axis=1, keepdims=True)
        b.PRB[rows, :] = probs
        top = probs.astype(BF16).astype(F32)
        rest = probs - top
        b.PRH[rows, :] = (top + pltpu.roll(rest, 64, 1)).astype(BF16)


def small_weights(g, b):
    lane = iota((g.D, 128), 1)
    small = b.MI[...].astype(F32)
    b.RW[...] = jnp.where(lane < g.ne, small, 0.0).astype(BF16)
    gains = jnp.transpose(small)[120:128, :]
    b.GN[0:1, :] = gains[0:1, :] + gains[1:2, :]
    b.GN[1:2, :] = gains[2:3, :] + gains[3:4, :]


def half_of(g, i):
    return pl.ds(pl.multiple_of(i * g.DH, 128), g.DH)


def own_rows(g, c):
    return pl.ds(pl.multiple_of(c * 2 * g.IP, 16), 2 * g.IP)


def tokens_out(g, p, b):
    rows = own_rows(g, p.c)
    send(b, "ta", b.ACT2.at[:, half_of(g, p.oc)], b.TA.at[rows, :], 0, 0, p.core)
    send(b, "tp", b.PRH, b.TG.at[rows, :], 0, 0, p.core)
    b.TA[rows, :] = b.ACT2[:, half_of(g, p.c)]
    b.TG[rows, :] = b.PRH[...]


def tokens_in(g, p, b):
    arrived(b, p, "ta", b.TA.at[own_rows(g, p.oc), :], 0)
    arrived(b, p, "tp", b.TG.at[own_rows(g, p.oc), :], 0)


def cotangent_out(g, p, b):
    def pack(k):
        e2 = p.other(k + 1)
        rows = nn(b.P[pack_rows(g, e2), :], b.UPP[...]).astype(BF16)
        b.PKU[e2] = rows

        @pl.when(k < g.ne - 1)
        def _():
            send(b, "uz", b.PKU.at[e2], b.US.at[p.e, p.c], k, p.e, p.along(e2))

        @pl.when(k == g.ne - 1)
        def _():
            b.US[p.e, p.c] = rows
            send(b, "uc", b.US.at[p.e, p.c], b.US.at[p.e, p.c], p.e, p.e, p.core)

    loop(g.ne, pack)


def cotangent_on(g, p, b):
    def relay(k):
        e2 = p.other(k + 1)
        part = b.US.at[e2, p.c]
        arrived(b, p, "uz", part, e2)
        send(b, "uc", part, part, e2, e2, p.core)

    loop(g.ne - 1, relay)


def slots_out(g, p, b):
    row = iota((g.CP, g.DH), 0)
    eye = row == iota((g.CP, g.DH), 1)
    lane = iota((g.CP, 128), 1)

    def pack(k):
        e2 = p.other(k + 1)
        hot = b.P[pack_rows(g, e2), :]
        tok = nn(hot, b.TA[...])
        gates = nn(hot, b.TG[...])
        gate = jnp.sum(
            jnp.where((lane == e2) | (lane == e2 + 64), gates, 0.0), axis=1, keepdims=True
        )
        b.GC[e2] = jnp.broadcast_to(gate, (g.CP, 128))
        across = jnp.sum(jnp.where(eye, gate, 0.0), axis=0, keepdims=True)
        top = across.astype(BF16).astype(F32)
        rows = jnp.where(row == g.CAP, top, jnp.where(row == g.CAP + 1, across - top, tok))
        rows = rows.astype(BF16)

        @pl.when(k < g.ne - 1)
        def _():
            b.PKA[e2] = rows
            send(b, "xz", b.PKA.at[e2], b.XS.at[p.e, p.y, p.c], k, p.e, p.along(e2))

        @pl.when(k == g.ne - 1)
        def _():
            part = b.XS.at[p.e, p.y, p.c]
            b.XS[p.e, p.y, p.c] = rows
            send(b, "xy", part, part, p.e, p.e, p.across)
            send(b, "xc", part, part, p.e, p.e, p.core)

    loop(g.ne, pack)


def slots_on(g, p, b, e2):
    part = b.XS.at[e2, p.y, p.c]
    arrived(b, p, "xz", part, e2)
    send(b, "xy", part, part, e2, e2, p.across)
    send(b, "xc", part, part, e2, e2, p.core)


def slots_over(g, p, b, e2):
    part = b.XS.at[e2, p.oy, p.c]
    arrived(b, p, "xy", part, e2)
    send(b, "xd", part, part, e2, e2, p.core)


def slots_in(g, p, b, e2):
    arrived(b, p, "xc", b.XS.at[e2, p.y, p.oc], e2)
    arrived(b, p, "xd", b.XS.at[e2, p.oy, p.oc], e2)
    arrived(b, p, "uc", b.US.at[e2, p.oc], e2)


def experts_out(g, p, b):
    b.WI[p.d] = b.wi[...]
    b.WB[p.d] = b.wb[...]
    send(b, "ei", b.wi, b.WI.at[p.d], 0, 0, p.twin)
    send(b, "eb", b.wb, b.WB.at[p.d], 0, 0, p.twin)


def back_core(g, p, b, part, s):
    send(b, "rc", part.at[s, :, p.oc], b.RC.at[s], s, s, p.core)


def back_over(g, p, b, part, s):
    arrived(b, p, "rc", b.RC.at[s], s)
    b.RC[s, p.oy] = (part[s, p.oy, p.c].astype(F32) + b.RC[s, p.oy].astype(F32)).astype(BF16)
    send(b, "ry", b.RC.at[s, p.oy], b.RY.at[s], s, s, p.across)


def back_on(g, p, b, part, s):
    arrived(b, p, "ry", b.RY.at[s], s)
    total = (
        part[s, p.y, p.c].astype(F32) + b.RC[s, p.y].astype(F32) + b.RY[s].astype(F32)
    ).astype(BF16)

    @pl.when(s != p.e)
    def _():
        b.RC[s, p.y] = total
        send(b, "rz", b.RC.at[s, p.y], b.RO.at[p.e], s, p.e, p.along(s))

    @pl.when(s == p.e)
    def _():
        b.RO[p.e] = total


def back_in(g, p, b):
    def rows_of(k):
        s = p.other(k + 1)
        arrived(b, p, "rz", b.RO.at[s], s)

    loop(g.ne - 1, rows_of)


def back_end(g, p, b):
    def rets(s):
        left(b, p, "rc", b.RC.at[0], s)
        left(b, p, "ry", b.RY.at[0], s)

    loop(g.ne, rets)
    loop(g.ne - 1, lambda k: left(b, p, "rz", b.RY.at[0], p.other(k + 1)))


def gelu_parts(u):
    inner = 0.7978845608028654 * (u + 0.044715 * u * u * u)
    tangent = jnp.tanh(inner)
    value = 0.5 * u * (1.0 + tangent)
    slope = 0.5 * (1.0 + tangent) + 0.5 * u * (1.0 - tangent * tangent) * 0.7978845608028654 * (
        1.0 + 3.0 * 0.044715 * u * u
    )
    return value, slope


def expert(g, b, first):
    base = g.CP - 16
    row = iota((g.CP, g.DH), 0)
    eye = row == iota((g.CP, g.DH), 1)
    for i in range(g.SG):
        for blk in range(2):
            tail = b.XS[first + i, blk, 0, base:, :].astype(F32)
            gate = tail[g.CAP - base : g.CAP - base + 1] + tail[g.CAP - base + 1 : g.CAP - base + 2]
            gate = jnp.sum(jnp.where(eye, gate, 0.0), axis=1, keepdims=True)
            at = (i * 2 + blk) * g.CP
            b.GP[at : at + g.CP, :] = (b.US[first + i, blk].astype(F32) * gate).astype(BF16)
    x = [b.XS[pl.ds(first, g.SG), :, q].reshape(g.R, g.DH) for q in range(2)]
    for n in range(g.F // 256):
        cols = slice(n * 256, n * 256 + 256)
        pre = nn(x[0], b.WI[0, :, cols]) + nn(x[1], b.WI[1, :, cols])
        value, slope = gelu_parts(pre)
        b.HQ[:, cols] = value.astype(BF16)
        grad = nt(b.GP[:, : g.DH], b.WB[0, cols, :]) + nt(b.GP[:, g.DH :], b.WB[1, cols, :])
        b.GR[:, cols] = (grad * slope).astype(BF16)
    shape = (g.SG, 2, g.CP, g.DH)
    dots = []
    for q in range(2):
        out = nn(b.HQ[...], b.WB[q]).astype(BF16)
        b.PO[pl.ds(first, g.SG), :, q] = out.reshape(shape)
        up = b.US[pl.ds(first, g.SG), :, :, q * g.DH : (q + 1) * g.DH].reshape(g.R, g.DH)
        dots.append(jnp.sum(out.astype(F32) * up.astype(F32), axis=1, keepdims=True))
        b.DB[q] += tn(b.HQ[...], b.GP[:, q * g.DH : (q + 1) * g.DH])
        b.DI[q] += tn(x[q], b.GR[...])
    dots = dots[0] + dots[1]
    for q in range(2):
        back = nt(b.GR[...], b.WI[q])
        for i in range(g.SG):
            for blk in range(2):
                at = (i * 2 + blk) * g.CP
                along = jnp.sum(jnp.where(eye, dots[at : at + g.CP], 0.0), axis=0, keepdims=True)
                if q == 1:
                    along = along - along.astype(BF16).astype(F32)
                b.PG[first + i, blk, q] = jnp.where(
                    row == g.CAP, along, back[at : at + g.CP]
                ).astype(BF16)


def experts(g, p, b):
    b.DB[...] = jnp.zeros_like(b.DB)
    b.DI[...] = jnp.zeros_like(b.DI)
    n = g.ne
    if g.SG > 1:
        loop(n - 1, lambda k: slots_on(g, p, b, p.other(k + 1)))
        loop(n, lambda k: slots_over(g, p, b, p.other(k)))
        loop(n, lambda k: slots_in(g, p, b, p.other(k)))
        arrived(b, p, "ei", b.WI.at[p.od], 0)
        arrived(b, p, "eb", b.WB.at[p.od], 0)
        loop(n // g.SG, lambda t: expert(g, b, t * g.SG))
        loop(n, lambda k: back_core(g, p, b, b.PG, p.other(k)))
        loop(n, lambda k: back_over(g, p, b, b.PG, p.other(k)))
        loop(n, lambda k: back_on(g, p, b, b.PG, p.other(k)))
        return
    slots_over(g, p, b, p.e)
    slots_in(g, p, b, p.e)
    arrived(b, p, "ei", b.WI.at[p.od], 0)
    arrived(b, p, "eb", b.WB.at[p.od], 0)

    def source(k):
        @pl.when(k == 1)
        def _():
            loop(n - 1, lambda i: slots_on(g, p, b, p.other(i + 1)))

        @pl.when(k > 0)
        def _():
            back_over(g, p, b, b.PG, p.other(k - 1))
            slots_over(g, p, b, p.other(k))
            slots_in(g, p, b, p.other(k))

        expert(g, b, p.other(k))
        back_core(g, p, b, b.PG, p.other(k))

    loop(n, source)
    back_over(g, p, b, b.PG, p.other(n - 1))
    loop(n, lambda k: back_on(g, p, b, b.PG, p.other(k)))


def first_sends_end(g, p, b):
    n = g.ne
    if g.aligned:
        own = piece_rows(g, p.d, p.e)

        def z(k):
            left(b, p, "wz", b.wp, k)
            left(b, p, "mz", b.mp, k)

        loop(n - 1, z)

        def x(k):
            left(b, p, "wx", b.wp, k)
            left(b, p, "mx", b.mp, k)

        loop(n, x)

    def w(i):
        for name in ("wy", "wc", "wd"):
            left(b, p, name, piece_of(g, b.W, p.h, i), i)

    loop(pieces(g), w)
    left(b, p, "ta", b.TA.at[own_rows(g, 0), :], 0)
    left(b, p, "tp", b.TG.at[own_rows(g, 0), :], 0)

    def slots(k):
        left(b, p, "uz", b.PKU.at[0], k)
        left(b, p, "xz", b.PKA.at[0], k)

    loop(n - 1, slots)

    def on(k):
        left(b, p, "uc", b.US.at[0, 0], k)
        for name in ("xy", "xc", "xd"):
            left(b, p, name, b.XS.at[0, 0, 0], k)

    loop(n, on)
    left(b, p, "ei", b.wi, 0)
    left(b, p, "eb", b.wb, 0)


KEEP = ("X", "UPO", "W", "RW", "GN", "QKV", "PB", "ATT", "HID", "PRB", "PT", "GC", "PO", "RO", "KI", "KB", "SI", "SB")


def first_kernel(g, b):
    p = Place(g)
    rows_out(g, p, b)
    p.enter()
    weights_out(g, p, b)
    rows_in(g, p, b)
    route(g, b, p.c, False)
    weights_on(g, p, b)
    cotangent_out(g, p, b)
    weights_end(g, p, b)
    experts_out(g, p, b)
    route(g, b, p.y, True)
    small_weights(g, b)
    first_norm(g, b)
    stow(b, "X", "UPO", "RW", "GN", "PT")
    attention(g, p, b)
    stow(b, "W", "QKV", "PB", "ATT", "HID")
    second_norm(g, b)
    stow(b, "PRB")
    tokens_out(g, p, b)
    cotangent_on(g, p, b)
    tokens_in(g, p, b)
    slots_out(g, p, b)
    stow(b, "GC")
    experts(g, p, b)
    stow(b, "PO")
    b.KI[...] = b.DI[p.d]
    b.KB[...] = b.DB[p.d]
    b.SI[...] = b.DI[p.od].astype(BF16)
    b.SB[...] = b.DB[p.od].astype(BF16)
    stow(b, "KI", "KB", "SI", "SB")
    back_in(g, p, b)
    stow(b, "RO")
    first_sends_end(g, p, b)
    back_end(g, p, b)
    stowed(b, *KEEP)


def grads_of_expert_out(g, p, b):
    send(b, "gi", b.hSI, b.XI, 0, 0, p.twin)
    send(b, "gb", b.hSB, b.XB, 0, 0, p.twin)


def grads_of_expert_in(g, p, b):
    loaded(b, "KI", "KB")
    arrived(b, p, "gi", b.XI, 0)
    b.o_gi[...] = b.KI[...] + b.XI[...].astype(F32)
    arrived(b, p, "gb", b.XB, 0)
    b.o_gb[...] = b.KB[...] + b.XB[...].astype(F32)


def slots_back(g, p, b, kind):
    lane = iota((g.CP, 128), 1)
    base = g.CP - 16
    eye = iota((g.CP, g.DH), 0) == iota((g.CP, g.DH), 1)

    def rows_of(s):
        rows = pack_rows(g, s)
        if kind:
            b.RG[rows, 0 : g.DH] = b.RB[s]
            dots = b.RB[s, base:, :].astype(F32)[g.CAP - base : g.CAP - base + 1]
            dots = jnp.sum(jnp.where(eye, dots, 0.0), axis=1, keepdims=True)
            b.RG[rows, g.DH :] = jnp.where(lane == s, dots, 0.0).astype(BF16)
        else:
            b.RG[rows, 0 : g.DH] = (b.RO[s].astype(F32) * b.GC[s][:, 0:1]).astype(BF16)

    loop(g.ne, rows_of)


def unpack(g, p, b, kind):
    name, width = ("ug", g.DH + 128) if kind else ("uo", g.DH)
    out, landed = (b.UG, b.TR) if kind else (b.UO, b.TO)

    def rows(c, j):
        image = pl.ds(pl.multiple_of((2 * c + j) * g.IP, 16), g.IP)
        return nn(b.PT[image, :], b.RG[:, 0:width]).astype(BF16)

    for j in range(2):
        here = slice(j * g.IP, (j + 1) * g.IP)
        out[here, :] = rows(p.oc, j)
        send(b, name, out.at[here, :], landed.at[p.c, here, :], j, j, p.core)
    for j in range(2):
        landed[p.c, j * g.IP : (j + 1) * g.IP, :] = rows(p.c, j)


def unpacked(g, p, b, kind):
    name, landed = ("ug", b.TR) if kind else ("uo", b.TO)
    for j in range(2):
        arrived(b, p, name, landed.at[p.oc, j * g.IP : (j + 1) * g.IP, :], j)


def mix(g, p, b):
    def rows16(rows):
        for q in range(2):
            cols = slice(q * g.DH, (q + 1) * g.DH)
            b.MX[rows, cols] = (b.HID[rows, cols] + b.TO[q, rows, :].astype(F32)).astype(BF16)

    rows16s(2 * g.IP, rows16)
    for j in range(2):
        part = b.MX.at[j * g.IP : (j + 1) * g.IP, :]
        here = (p.c == p.y) & (p.c == j)

        @pl.when(here)
        def _(j=j):
            b.MIX[p.y] = b.MX[j * g.IP : (j + 1) * g.IP, :]

        @pl.when(jnp.logical_not(here))
        def _(j=j, part=part):
            send(b, "mo", part, b.MIX.at[p.y], j, p.y, (p.d, p.e, 2 * p.c + j))


def mixed_in(g, p, b):
    for blk in range(2):

        @pl.when(jnp.logical_not((p.y == blk) & (p.c == p.y)))
        def _(blk=blk):
            arrived(b, p, "mo", b.MIX.at[blk], blk)

        b.o_mixed[blk] = b.MIX[blk, 0:SEQ, :]
    for j in range(2):

        @pl.when(jnp.logical_not((p.c == p.y) & (p.c == j)))
        def _(j=j):
            left(b, p, "mo", b.MIX.at[0], j)


def tokens_back(g, p, b):
    lane = iota((g.IP, 128), 1)
    b.GA[...] = jnp.zeros_like(b.GA)
    for blk in range(2):
        rows = slice(blk * g.IP, (blk + 1) * g.IP)
        gate = b.TR[0, rows, g.DH :].astype(F32) + b.TR[1, rows, g.DH :].astype(F32)
        probs = b.PRB[rows, :]
        grad = probs * (gate - jnp.sum(probs * gate, axis=1, keepdims=True))
        b.GL[rows, :] = grad.astype(BF16)
        b.GHID[rows, :] = nt(b.GL[rows, :], b.RW[...])

    def rows16(rows):
        normed, inverse = normalize(b.HID[rows, :])
        upstream = b.GHID[rows, :] + jnp.concatenate(
            [b.TR[q, rows, 0 : g.DH].astype(F32) for q in range(2)], axis=1
        )
        prod = upstream * normed
        b.GA[8:16, :] += prod[0:8, :] + prod[8:16, :]
        b.ACT2[rows, :] = (normed * b.GN[1:2, :]).astype(BF16)
        hidden = b.UPO[rows, :].astype(F32) + norm_backward(upstream, normed, inverse, b.GN[1:2, :])
        b.GHID[rows, :] = hidden
        b.GHL[rows, :] = hidden.astype(BF16)

    rows16s(2 * g.IP, rows16)


def first_norm_again(g, b):
    def rows16(rows):
        normed, _ = normalize(b.X[rows, :].astype(F32))
        b.ACT1[rows, :] = (normed * b.GN[0:1, :]).astype(BF16)

    rows16s(2 * g.IP, rows16)


def attention_back(g, p, b):
    low, high = masks(g.IP)
    zero = jnp.zeros((g.IP, 128), BF16)
    scale = HD**-0.5
    b.DA[...] = jnp.zeros_like(b.DA)

    def group(k):
        @pl.when(k == 1)
        def _():
            loop(g.ne, lambda i: back_on(g, p, b, b.PO, p.other(i + 1)))

        @pl.when(k == 2)
        def _():
            back_in(g, p, b)
            slots_back(g, p, b, 0)
            unpack(g, p, b, 0)

        @pl.when(k == 3)
        def _():
            unpacked(g, p, b, 0)
            mix(g, p, b)

        yk = lax.rem(p.oy + k, 2)
        gi = 2 * yk + lax.rem(p.oc + lax.div(k, 2), 2)
        for blk in range(2):
            rows = slice(blk * g.IP, (blk + 1) * g.IP)
            grad = nn(b.GHL[rows, :], b.W[gi, :, 512:768]).astype(BF16)
            tiles = [grad[:, 0:128], grad[:, 128:256]]
            dq, dk, dv = [], [], []
            for j in range(3):
                probs = b.PB[gi, blk * 3 + j]
                gt = tiles[(j + 1) // 2]
                qt = b.QKV[gi, rows, (j // 2) * 128 : (j // 2) * 128 + 128]
                kt = b.QKV[gi, rows, 384 + (j // 2) * 128 : 384 + (j // 2) * 128 + 128]
                vt = b.QKV[gi, rows, 128 + ((j + 1) // 2) * 128 : 256 + ((j + 1) // 2) * 128]
                grad_probs = nt(jnp.where(low if j == 1 else high, gt, zero), vt)
                wide = probs.astype(F32)
                grad_scores = wide * (
                    grad_probs - jnp.sum(wide * grad_probs, axis=1, keepdims=True)
                )
                grad_scores = (grad_scores * scale).astype(BF16)
                dv.append(tn(probs, gt))
                dq.append(nn(grad_scores, kt))
                dk.append(tn(grad_scores, qt))
            b.GJ[rows, 0:128] = jnp.where(low, dq[0], dq[1]).astype(BF16)
            b.GJ[rows, 128:256] = jnp.where(low, dq[2], dv[0]).astype(BF16)
            b.GJ[rows, 256:384] = jnp.where(low, dv[1], dv[2]).astype(BF16)
            b.GJ[rows, 384:512] = jnp.where(low, dk[0], dk[1]).astype(BF16)
            b.GJ[rows, 512:640] = jnp.where(low, dk[2], 0.0).astype(BF16)
        for blk in range(2):
            rows = slice(blk * g.IP, (blk + 1) * g.IP)
            b.DA[rows, :] += nt(b.GJ[rows, :], b.W[gi, :, 0:640])
        for m in range(g.D // 256):
            cols = slice(m * 256, m * 256 + 256)
            first = tn(b.ACT1[:, cols], b.GJ[...])
            second = tn(b.GHL[:, cols], b.ATT[gi])
            b.DW[gi, cols, 0:512] = first[:, 0:512].astype(BF16)
            b.DW[gi, cols, 512:640] = (first[:, 512:] + second[:, 0:128]).astype(BF16)
            b.DW[gi, cols, 640:768] = second[:, 128:].astype(BF16)

        @pl.when(k < 2)
        def _():
            send(b, "dc", b.DW.at[gi], b.RDC.at[yk], yk, yk, p.core)

        @pl.when(k >= 2)
        def _():
            arrived(b, p, "dc", b.RDC.at[yk], yk)
            if g.aligned:

                def to_twin(i):
                    e2 = p.other(i + 1)
                    rows = piece_rows(g, p.od, e2)
                    at = yk * g.ne + e2
                    b.DW[gi, rows, :] = (
                        b.DW[gi, rows, :].astype(F32) + b.RDC[yk, rows, :].astype(F32)
                    ).astype(BF16)
                    send(b, "dx", b.DW.at[gi, rows, :], b.RDX.at[yk, e2], at, at, p.twin)

                loop(g.ne, to_twin)

    loop(4, group)


def inputs_back(g, p, b):
    def rows16(rows):
        normed, inverse = normalize(b.X[rows, :].astype(F32))
        upstream = b.DA[rows, :]
        prod = upstream * normed
        b.GA[0:8, :] += prod[0:8, :] + prod[8:16, :]
        b.GIN[rows, :] = (
            b.GHID[rows, :] + norm_backward(upstream, normed, inverse, b.GN[0:1, :])
        ).astype(BF16)

    rows16s(2 * g.IP, rows16)
    for j in range(2):
        rows = slice(j * g.IP, (j + 1) * g.IP)
        image = 2 * p.c + j
        b.GIN[rows, :] = nn(shift(g, image, True), b.GIN[rows, :]).astype(BF16)
        b.EG[j, 0] = b.GIN[j * g.IP : j * g.IP + 16, :]
        b.EG[j, 1] = b.GIN[(j + 1) * g.IP - 16 : (j + 1) * g.IP, :]
        for name, device in (("i", p.across), ("j", p.core)):
            middle = b.GIN.at[j * g.IP + 16 : (j + 1) * g.IP - 16, :]
            send(b, name + "m", middle, b.o_gin.at[p.y, middle_of(g, image), :], j, j, device)
            send(b, name + "e", b.EG.at[j], b.ED.at[p.y, image], j, j, device)
        b.o_gin[p.y, middle_of(g, image), :] = b.GIN[j * g.IP + 16 : (j + 1) * g.IP - 16, :]
        b.ED[p.y, image] = b.EG[j]


def middle_of(g, image):
    return pl.ds(pl.multiple_of(image * g.WIN + 16, 16), g.WIN - 16)


def inputs_end(g, p, b):
    for j in range(2):
        image = 2 * p.c + j
        middle, edge = b.o_gin.at[p.oy, middle_of(g, image), :], b.ED.at[p.oy, image]
        arrived(b, p, "im", middle, j)
        send(b, "km", middle, middle, j, j, p.core)
        arrived(b, p, "ie", edge, j)
        send(b, "ke", edge, edge, j, j, p.core)


def inputs_last(g, p, b):
    for j in range(2):
        image = 2 * p.oc + j
        for name, yy in (("j", p.y), ("k", p.oy)):
            arrived(b, p, name + "m", b.o_gin.at[yy, middle_of(g, image), :], j)
            arrived(b, p, name + "e", b.ED.at[yy, image], j)
    for blk in range(2):
        b.o_gin[blk, 0:16, :] = b.ED[blk, 0, 0]
        for i in range(1, g.NI):
            b.o_gin[blk, i * g.WIN : i * g.WIN + 16, :] = b.ED[blk, i, 0] + b.ED[blk, i - 1, 1]
        b.o_gin[blk, g.NI * g.WIN : g.NI * g.WIN + 16, :] = b.ED[blk, g.NI - 1, 1]


def weights_back(g, p, b):
    if not g.aligned:
        b.DW[p.hy] = (b.DW[p.hy].astype(F32) + b.RDC[p.oy].astype(F32)).astype(BF16)
        send(b, "dy", b.DW.at[p.hy], b.RDY, 0, 0, p.across)
        return

    def to_across(i):
        e2 = p.other(i + 1)
        rows = piece_rows(g, p.d, e2)
        arrived(b, p, "dx", b.RDX.at[p.oy, e2], p.oy * g.ne + e2)
        b.RDX[p.oy, e2] = (
            b.DW[p.hy, rows, :].astype(F32)
            + b.RDC[p.oy, rows, :].astype(F32)
            + b.RDX[p.oy, e2].astype(F32)
        ).astype(BF16)
        send(b, "dy", b.RDX.at[p.oy, e2], b.RDY.at[e2], e2, e2, p.across)

    loop(g.ne, to_across)


def weights_back_on(g, p, b):
    if not g.aligned:
        arrived(b, p, "dy", b.RDY, 0)
        total = b.DW[p.h].astype(F32) + b.RDC[p.y].astype(F32) + b.RDY[...].astype(F32)
        b.o_dw[...] = total.astype(BF16)
        return

    def piece(k):
        e2 = p.other(k + 1)
        rows = piece_rows(g, p.d, e2)
        arrived(b, p, "dx", b.RDX.at[p.y, e2], p.y * g.ne + e2)
        arrived(b, p, "dy", b.RDY.at[e2], e2)
        mine = (
            b.DW[p.h, rows, :].astype(F32)
            + b.RDC[p.y, rows, :].astype(F32)
            + b.RDX[p.y, e2].astype(F32)
            + b.RDY[e2].astype(F32)
        )

        @pl.when(k < g.ne - 1)
        def _():
            b.SDZ[e2] = mine.astype(BF16)
            send(b, "dz", b.SDZ.at[e2], b.RDZ.at[p.e], k, p.e, p.along(e2))

        @pl.when(k == g.ne - 1)
        def _():
            b.o_dw[...] = mine

    loop(g.ne, piece)


def weights_back_end(g, p, b):
    if not g.aligned:
        return

    def add(k):
        e2 = p.other(k + 1)
        arrived(b, p, "dz", b.RDZ.at[e2], e2)
        b.o_dw[...] += b.RDZ[e2].astype(F32)

    loop(g.ne - 1, add)


def small_back(g, p, b):
    sub = iota((128, g.D), 0)
    one = jnp.sum(b.GA[0:8, :], axis=0, keepdims=True)
    two = jnp.sum(b.GA[8:16, :], axis=0, keepdims=True)
    gains = jnp.where(sub == 120, one, jnp.where(sub == 122, two, 0.0))
    b.GM[...] = tn(b.ACT2[...], b.GL[...]) + jnp.transpose(gains)
    if g.aligned:
        half = g.D // 2
        b.SMX[...] = b.GM[pl.ds(pl.multiple_of(p.od * half, 16), half), :].astype(BF16)
        send(b, "sx", b.SMX, b.RMX, 0, 0, p.twin)


def small_back_on(g, p, b):
    if g.aligned:
        arrived(b, p, "sx", b.RMX, 0)

        def piece(k):
            e2 = p.other(k + 1)
            mine = b.GM[piece_rows(g, p.d, e2), :] + b.RMX[
                pl.ds(pl.multiple_of(e2 * g.PR, 16), g.PR), :
            ].astype(F32)

            @pl.when(k < g.ne - 1)
            def _():
                b.SMZ[e2] = mine.astype(BF16)
                send(b, "sz", b.SMZ.at[e2], b.RMZ.at[p.e], k, p.e, p.along(e2))

            @pl.when(k == g.ne - 1)
            def _():
                b.o_small[...] = mine

        loop(g.ne, piece)

        def add(k):
            e2 = p.other(k + 1)
            arrived(b, p, "sz", b.RMZ.at[e2], e2)
            b.o_small[...] += b.RMZ[e2].astype(F32)

        loop(g.ne - 1, add)
    else:
        b.o_small[...] = b.GM[...]
    b.SMC[...] = b.o_small[...].astype(BF16)
    send(b, "sc", b.SMC, b.RMC, 0, 0, p.core)
    arrived(b, p, "sc", b.RMC, 0)
    b.SMY[...] = (b.SMC[...].astype(F32) + b.RMC[...].astype(F32)).astype(BF16)
    send(b, "sy", b.SMY, b.RMY, 0, 0, p.across)
    arrived(b, p, "sy", b.RMY, 0)
    b.o_small[...] = b.SMY[...].astype(F32) + b.RMY[...].astype(F32)


def second_sends_end(g, p, b):
    n = g.ne
    left(b, p, "gi", b.XI, 0)
    left(b, p, "gb", b.XB, 0)

    back_end(g, p, b)

    def away(k):
        if g.aligned:
            left(b, p, "dz", b.SDZ.at[0], k)
            left(b, p, "sz", b.SMZ.at[0], k)

    loop(n - 1, away)
    for i in range(2):
        left(b, p, "dc", b.RDC.at[0], i)
        left(b, p, "ug", b.UG.at[0 : g.IP, :], i)
        left(b, p, "uo", b.UO.at[0 : g.IP, :], i)
        for name in ("i", "j", "k"):
            left(b, p, name + "m", b.o_gin.at[0, middle_of(g, 0), :], i)
            left(b, p, name + "e", b.ED.at[0, 0], i)
    if g.aligned:
        left(b, p, "sx", b.SMX, 0)

        def moved(k):
            left(b, p, "dx", b.RDX.at[0, 0], k)
            left(b, p, "dx", b.RDX.at[0, 0], g.ne + k)
            left(b, p, "dy", b.RDY.at[0], k)

        loop(n, moved)
    else:
        left(b, p, "dy", b.RDY, 0)
    left(b, p, "sc", b.SMC, 0)
    left(b, p, "sy", b.SMY, 0)


def second_kernel(g, b):
    p = Place(g)
    fetch(b, "kRO", b.hRO, b.RB)
    names = ("PT", "HID", "PRB", "RW", "GN", "UPO", "X", "PO", "GC", "W", "QKV", "PB", "ATT", "KI", "KB")
    load(b, *names)
    p.enter()
    loop(g.ne, lambda k: send(b, "rc", b.hPO.at[p.other(k), :, p.oc], b.RC.at[p.other(k)], p.other(k), p.other(k), p.core))
    grads_of_expert_out(g, p, b)
    fetched(b, "kRO", b.hRO, b.RB)
    slots_back(g, p, b, 1)
    loaded(b, "PT")
    unpack(g, p, b, 1)
    loaded(b, "GN", "X")
    first_norm_again(g, b)
    unpacked(g, p, b, 1)
    loaded(b, "PO")
    loop(g.ne, lambda k: back_over(g, p, b, b.PO, p.other(k + 1)))
    loaded(b, "HID", "PRB", "RW", "UPO")
    tokens_back(g, p, b)
    loaded(b, "W", "QKV", "PB", "ATT", "GC")
    attention_back(g, p, b)
    inputs_back(g, p, b)
    weights_back(g, p, b)
    small_back(g, p, b)
    inputs_end(g, p, b)
    weights_back_on(g, p, b)
    small_back_on(g, p, b)
    mixed_in(g, p, b)
    grads_of_expert_in(g, p, b)
    inputs_last(g, p, b)
    weights_back_end(g, p, b)
    second_sends_end(g, p, b)


def call(body, g, inputs, far, outs, far_outs, scratch, sems, number, flops):
    names = [*inputs, *far, *outs, *far_outs, *scratch]
    single = [n for n in sems if n[0] == "k" and n[1].isupper() or n.startswith("ld")]
    names += [name + end for name in sems for end in (("_s",) if name in single else ("_s", "_r"))]

    def kernel(*refs):
        body(g, types.SimpleNamespace(**dict(zip(names, refs, strict=True))))

    vmem, anywhere = pl.BlockSpec(memory_space=pltpu.VMEM), pl.BlockSpec(memory_space=pl.ANY)
    made = pl.pallas_call(
        kernel,
        out_shape=[jax.ShapeDtypeStruct(*o) for o in [*outs.values(), *far_outs.values()]],
        in_specs=[vmem] * len(inputs) + [anywhere] * len(far),
        out_specs=[vmem] * len(outs) + [anywhere] * len(far_outs),
        scratch_shapes=[pltpu.VMEM(*s) for s in scratch.values()]
        + [pltpu.SemaphoreType.DMA((n,)) for name, n in sems.items() for _ in range(1 if name in single else 2)],
        compiler_params=pltpu.CompilerParams(
            collective_id=number, has_side_effects=True, vmem_limit_bytes=LIMIT
        ),
        cost_estimate=pl.CostEstimate(flops=flops, bytes_accessed=2**24, transcendentals=0),
    )(*inputs.values(), *far.values())
    return dict(zip([*outs, *far_outs], made, strict=True))


def shards(
    inputs, w_qkv, w_out, w_router, gain_one, gain_two, w_in, w_back, experts, priority, cotangent, *, mesh
):
    model, rows = inputs.shape[2], inputs.shape[1]
    g = Sizes(mesh, model, rows, w_in.shape[2])
    n, ip, cp, dh = g.ne, g.IP, g.CP, g.DH
    assert inputs.shape[0] == 2
    pad = ((0, 0), (0, 0), (0, ip - SEQ), (0, 0))
    part = jnp.concatenate([w_qkv[:, 0], w_qkv[:, 2], w_qkv[:, 1], w_out.T], axis=1)
    gains = jnp.stack([gain_one, gain_two], axis=1)
    top = gains.astype(BF16)
    rest = (gains - top.astype(F32)).astype(BF16)
    small = jnp.concatenate(
        [
            w_router,
            jnp.zeros((w_router.shape[0], 120 - n), BF16),
            top[:, :1],
            rest[:, :1],
            top[:, 1:],
            rest[:, 1:],
            jnp.zeros((w_router.shape[0], 4), BF16),
        ],
        axis=1,
    )
    if not g.aligned:
        part = lax.all_gather(part, ("dp", "expert"), axis=0, tiled=True)
        small = lax.all_gather(small, ("dp", "expert"), axis=0, tiled=True)
    info = jnp.concatenate([experts, priority[:, :, None]], axis=2).astype(F32)
    info = jnp.pad(info.reshape(2, g.NI, SEQ, 3), pad, constant_values=-1000.0)
    mc = jnp.pad(info.reshape(2, g.TP, 3), ((0, 0), (0, 0), (0, 5)))
    mr = jnp.swapaxes(mc, 1, 2)
    np_ = pieces(g)
    kept = dict(
        X=((2 * ip, model), BF16),
        UPO=((2 * ip, model), BF16),
        W=((4, model, model), BF16),
        RW=((model, 128), BF16),
        GN=((8, model), F32),
        QKV=((4, 2 * ip, 640), BF16),
        PB=((4, 6, ip, ip), BF16),
        ATT=((4, 2 * ip, 256), BF16),
        HID=((2 * ip, model), F32),
        PRB=((2 * ip, 128), F32),
        PT=((g.TP, g.SL), BF16),
        GC=((n, cp, 128), F32),
        PO=((n, 2, 2, cp, dh), BF16),
        RO=((n, cp, dh), BF16),
        KI=((dh, g.F), F32),
        KB=((g.F, dh), F32),
        SI=((dh, g.F), BF16),
        SB=((g.F, dh), BF16),
    )
    assert set(kept) == set(KEEP)
    one = call(
        first_kernel,
        g,
        dict(wp=part, mp=small, wi=w_in[0], wb=w_back[0], mc=mc, mr=mr),
        dict(xin=inputs, uin=cotangent),
        {},
        {"h" + name: made for name, made in kept.items()},
        dict(
            **kept,
            PG=((n, 2, 2, cp, dh), BF16),
            RC=((n, 2, cp, dh), BF16),
            RY=((n, cp, dh), BF16),
            UB=((rows, model), BF16),
            UPP=((g.TP, model), BF16),
            DI=((2, dh, g.F), F32),
            DB=((2, g.F, dh), F32),
            MI=((model, 128), BF16),
            L=((g.TP, g.TP), BF16),
            O=((g.TP, 128), BF16),
            P=((g.SL, g.TP), BF16),
            ACT1=((2 * ip, model), BF16),
            ACT2=((2 * ip, model), BF16),
            PRH=((2 * ip, 128), BF16),
            TA=((g.TP, dh), BF16),
            TG=((g.TP, 128), BF16),
            US=((n, 2, cp, model), BF16),
            XS=((n, 2, 2, cp, dh), BF16),
            PKA=((n, cp, dh), BF16),
            PKU=((n, cp, model), BF16),
            WI=((2, dh, g.F), BF16),
            WB=((2, g.F, dh), BF16),
            GP=((g.R, model), BF16),
            HQ=((g.R, g.F), BF16),
            GR=((g.R, g.F), BF16),
        ),
        dict(wz=n, mz=n, wx=n, mx=n, wy=np_, wc=np_, wd=np_, ta=1, tp=1, uz=n, uc=n, xz=n, xy=n, xc=n, xd=n, ei=1, eb=1,
             rc=n, ry=n, rz=n, ldx=2, ldu=2, ldb=1, **{"k" + name: 1 for name in KEEP}),
        1,
        14 * 10**9,
    )
    rows_out = g.PR if g.aligned else model
    extra = (
        dict(
            RDX=((2, n, g.PR, model), BF16),
            SDZ=((n, g.PR, model), BF16),
            RDZ=((n, g.PR, model), BF16),
            SMX=((model // 2, 128), BF16),
            RMX=((model // 2, 128), BF16),
            SMZ=((n, g.PR, 128), BF16),
            RMZ=((n, g.PR, 128), BF16),
        )
        if g.aligned
        else {}
    )
    two = call(
        second_kernel,
        g,
        {},
        {"h" + name: one["h" + name] for name in KEEP},
        dict(
            o_mixed=((2, SEQ, model), BF16),
            o_gin=((2, rows, model), BF16),
            o_dw=((rows_out, model), F32 if g.aligned else BF16),
            o_small=((rows_out, 128), F32),
            o_gi=((dh, g.F), F32),
            o_gb=((g.F, dh), F32),
        ),
        {},
        dict(
            **{name: made for name, made in kept.items() if name not in ("SI", "SB", "RO")},
            RO=((n, cp, dh), BF16),
            RB=((n, cp, dh), BF16),
            RC=((n, 2, cp, dh), BF16),
            RY=((n, cp, dh), BF16),
            RG=((g.SL, dh + 128), BF16),
            UG=((2 * ip, dh + 128), BF16),
            UO=((2 * ip, dh), BF16),
            TR=((2, 2 * ip, dh + 128), BF16),
            TO=((2, 2 * ip, dh), BF16),
            MX=((2 * ip, model), BF16),
            MIX=((2, ip, model), BF16),
            EG=((2, 2, 16, model), BF16),
            ED=((2, 4, 2, 16, model), BF16),
            GL=((2 * ip, 128), BF16),
            GA=((16, model), F32),
            ACT1=((2 * ip, model), BF16),
            ACT2=((2 * ip, model), BF16),
            GHID=((2 * ip, model), F32),
            GHL=((2 * ip, model), BF16),
            DA=((2 * ip, model), F32),
            GJ=((2 * ip, 640), BF16),
            DW=((4, model, model), BF16),
            RDC=((2, model, model), BF16),
            RDY=((n, g.PR, model) if g.aligned else (model, model), BF16),
            GIN=((2 * ip, model), BF16),
            GM=((model, 128), F32),
            SMC=((rows_out, 128), BF16),
            RMC=((rows_out, 128), BF16),
            SMY=((rows_out, 128), BF16),
            RMY=((rows_out, 128), BF16),
            XI=((dh, g.F), BF16),
            XB=((g.F, dh), BF16),
            **extra,
        ),
        dict(rc=n, ry=n, rz=n, ug=2, uo=2, mo=2, gi=1, gb=1, dc=2, dy=n, dx=2 * n, dz=n, sx=1, sz=n, sc=1, sy=1, im=2, ie=2, jm=2, je=2, km=2, ke=2,
             **{"k" + name: 1 for name in KEEP if name not in ("SI", "SB")}),
        2,
        14 * 10**9,
    )
    dw, ds = two["o_dw"], two["o_small"]
    if not g.aligned:
        dw = lax.psum_scatter(dw, ("dp", "expert"), scatter_dimension=0, tiled=True)
        ds = lax.psum_scatter(ds.astype(BF16), ("dp", "expert"), scatter_dimension=0, tiled=True)
        dw, ds = dw.astype(F32), ds.astype(F32)
    lw = g.LW
    grad_qkv = jnp.stack([dw[:, :lw], dw[:, 2 * lw : 3 * lw], dw[:, lw : 2 * lw]], axis=1)
    return (
        two["o_mixed"],
        two["o_gin"],
        grad_qkv,
        dw[:, 3 * lw :].T,
        ds[:, :n],
        ds[:, 120],
        ds[:, 122],
        two["o_gi"][None],
        two["o_gb"][None],
    )


def solution(mesh):
    both = ("dp", "expert")
    in_specs = (
        P(both, None, None),
        P(both, None, "head"),
        P("head", both),
        P(both, None),
        P(both),
        P(both),
        P("expert", "dp", "head"),
        P("expert", "head", "dp"),
        P(both, None, None),
        P(both, None),
        P(both, None, None),
    )
    out_specs = (
        P(both, "head", None),
        P(both, None, None),
        P(both, None, "head"),
        P("head", both),
        P(both, None),
        P(both),
        P(both),
        P("expert", "dp", "head"),
        P("expert", "head", "dp"),
    )
    return jax.shard_map(
        functools.partial(shards, mesh=mesh),
        mesh=mesh,
        in_specs=in_specs,
        out_specs=out_specs,
        check_vma=False,
    )
```

```python
import functools
import types

import jax
import jax.numpy as jnp
from jax import lax
from jax.experimental import pallas as pl
from jax.experimental.pallas import tpu as pltpu
from jax.sharding import PartitionSpec as P

HD = 64
SEQ = 196
MESH = pl.DeviceIdType.MESH
F32, BF16 = jnp.float32, jnp.bfloat16
LIMIT = 63 * 2**20


def up16(n):
    return -(-n // 16) * 16


def nn(a, b):
    return lax.dot_general(a, b, (((1,), (0,)), ((), ())), preferred_element_type=F32)


def nt(a, b):
    return lax.dot_general(a, b, (((1,), (1,)), ((), ())), preferred_element_type=F32)


def tn(a, b):
    return lax.dot_general(a, b, (((0,), (0,)), ((), ())), preferred_element_type=F32)


def loop(count, body):
    def step(i, carry):
        body(i)
        return carry

    lax.fori_loop(0, count, step, 0)


def iota(shape, dim):
    return lax.broadcasted_iota(jnp.int32, shape, dim)


def fiota(shape, dim):
    return iota(shape, dim).astype(F32)


def normalize(v):
    centered = v - jnp.mean(v, axis=1, keepdims=True)
    inverse = lax.rsqrt(jnp.mean(centered * centered, axis=1, keepdims=True) + 1e-06)
    return centered * inverse, inverse


def norm_backward(upstream, normed, inverse, gain):
    scaled = upstream * gain
    return inverse * (
        scaled
        - jnp.mean(scaled, axis=1, keepdims=True)
        - normed * jnp.mean(scaled * normed, axis=1, keepdims=True)
    )


class Sizes:
    def __init__(self, mesh, model, rows, hidden):
        self.nd, self.ne, self.nh = mesh.shape["dp"], mesh.shape["expert"], mesh.shape["head"]
        self.D, self.DH = model, model // 2
        self.M = rows
        self.CAP = rows // self.ne
        self.CP = up16(self.CAP + 2)
        self.IP = up16(SEQ)
        self.NI = rows // SEQ
        self.TP = self.NI * self.IP
        self.SL = self.ne * self.CP
        self.WIN = self.IP - 16
        self.LAG = SEQ - self.WIN
        self.F = hidden
        self.PR = model // (self.nd * self.ne)
        self.aligned = self.PR % 16 == 0
        self.SG = 1
        while self.SG * 2 * self.CP <= self.IP and self.ne % (self.SG * 2) == 0:
            self.SG *= 2
        self.R = self.SG * 2 * self.CP
        self.LW = model // self.nh
        assert self.nd == 2 and self.nh == 4 and self.NI == 4 and self.LW == 3 * HD
        assert (self.NI - 1) * self.WIN + self.IP <= rows and (self.NI - 1) * self.LAG + SEQ <= self.IP
        assert self.ne & (self.ne - 1) == 0
        assert self.ne <= 64 and 0 <= self.CAP - (self.CP - 16) <= 14


class Place:
    def __init__(self, g):
        self.ne = g.ne
        self.d = lax.axis_index("dp")
        self.e = lax.axis_index("expert")
        self.h = lax.axis_index("head")
        self.y = lax.div(self.h, 2)
        self.c = lax.rem(self.h, 2)
        self.oy, self.oc, self.od = 1 - self.y, 1 - self.c, 1 - self.d
        self.hcore = 2 * self.y + self.oc
        self.hy = 2 * self.oy + self.c
        self.hdiag = 2 * self.oy + self.oc
        self.core = (self.d, self.e, self.hcore)
        self.across = (self.d, self.e, self.hy)
        self.diag = (self.d, self.e, self.hdiag)
        self.twin = (self.od, self.e, self.h)

    def other(self, k):
        index, bit = 0, 1
        while bit < self.ne:
            index = index + lax.rem(lax.div(self.e, bit) + k // bit, 2) * bit
            bit *= 2
        return index

    def along(self, e2):
        return (self.d, e2, self.h)

    def enter(self, wide=False):
        barrier = pltpu.get_barrier_semaphore()

        def tell(device):
            pl.semaphore_signal(barrier, inc=1, device_id=device, device_id_type=MESH)

        for device in (self.core, self.across, self.diag, self.twin):
            tell(device)
        loop(self.ne - 1, lambda k: tell(self.along(self.other(k + 1))))
        if wide:
            loop(self.ne - 1, lambda k: tell((self.od, self.other(k + 1), self.h)))
        pl.semaphore_wait(barrier, 4 + (self.ne - 1) * (2 if wide else 1))


def copy(b, name, src, dst, si, ri, device):
    return pltpu.make_async_remote_copy(
        src_ref=src,
        dst_ref=dst,
        send_sem=getattr(b, name + "_s").at[si],
        recv_sem=getattr(b, name + "_r").at[ri],
        device_id=device,
        device_id_type=MESH,
    )


def send(b, name, src, dst, si, ri, device):
    copy(b, name, src, dst, si, ri, device).start()


def arrived(b, p, name, ref, ri):
    copy(b, name, ref, ref, 0, ri, p.core).wait_recv()


def left(b, p, name, ref, si):
    copy(b, name, ref, ref, si, 0, p.core).wait_send()


def fetch(b, name, src, dst, i=0):
    pltpu.make_async_copy(src, dst, getattr(b, name + "_s").at[i]).start()


def fetched(b, name, src, dst, i=0):
    pltpu.make_async_copy(src, dst, getattr(b, name + "_s").at[i]).wait()


def stow(b, *names):
    for name in names:
        fetch(b, "k" + name, getattr(b, name), getattr(b, "h" + name))


def stowed(b, *names):
    for name in names:
        fetched(b, "k" + name, getattr(b, name), getattr(b, "h" + name))


def load(b, *names):
    for name in names:
        fetch(b, "k" + name, getattr(b, "h" + name), getattr(b, name))


def loaded(b, *names):
    for name in names:
        fetched(b, "k" + name, getattr(b, "h" + name), getattr(b, name))


def shift(g, image, back=False):
    row, col = iota((g.IP, g.IP), 0), iota((g.IP, g.IP), 1)
    if back:
        hot = (row == col + g.LAG * image) & (col < SEQ)
    else:
        hot = (col == row + g.LAG * image) & (row < SEQ)
    return jnp.where(hot, 1.0, 0.0).astype(BF16)


def window(g, image):
    return pl.ds(pl.multiple_of(image * g.WIN, 16), g.IP)


def rows_out(g, p, b):
    for j in range(2):
        rows = slice(j * g.IP, (j + 1) * g.IP)
        fetch(b, "ldx", b.xin.at[p.y, window(g, 2 * p.c + j), :], b.X.at[rows, :], j)
        fetch(b, "ldu", b.uin.at[p.y, window(g, 2 * p.c + j), :], b.UPO.at[rows, :], j)
    fetch(b, "ldb", b.uin.at[p.c, :, half_of(g, p.y)], b.UB)


def rows_in(g, p, b):
    for j in range(2):
        rows = slice(j * g.IP, (j + 1) * g.IP)
        fetched(b, "ldx", b.xin.at[p.y, window(g, 2 * p.c + j), :], b.X.at[rows, :], j)
        fetched(b, "ldu", b.uin.at[p.y, window(g, 2 * p.c + j), :], b.UPO.at[rows, :], j)
        hot = shift(g, 2 * p.c + j)
        b.X[rows, :] = nn(hot, b.X[rows, :]).astype(BF16)
        b.UPO[rows, :] = nn(hot, b.UPO[rows, :]).astype(BF16)
    fetched(b, "ldb", b.uin.at[p.c, :, half_of(g, p.y)], b.UB)
    for i in range(g.NI):
        b.UPP[i * g.IP : (i + 1) * g.IP, :] = nn(
            shift(g, i), b.UB[i * g.WIN : i * g.WIN + g.IP, :]
        ).astype(BF16)


def route(g, b, c, both):
    pr_row, e0r, e1r = b.mr[c, 2:3, :], b.mr[c, 0:1, :], b.mr[c, 1:2, :]
    lane = fiota((g.IP, 128), 1)
    base = jnp.zeros((1, 128), F32)
    for i in range(g.NI):
        rows = slice(i * g.IP, (i + 1) * g.IP)
        col = b.mc[c, rows, :]
        e0c, e1c, prc = col[:, 0:1], col[:, 1:2], col[:, 2:3]
        b.L[rows, :] = jnp.where(pr_row < prc, 1.0, 0.0).astype(BF16)
        b.O[rows, :] = jnp.where((lane == e0c) | (lane == e1c + 64.0), 1.0, 0.0).astype(BF16)
        base = base + jnp.sum(jnp.where(lane == e0c + 64.0, 1.0, 0.0), axis=0, keepdims=True)
    slot_lane = fiota((g.IP, g.SL), 1)
    for i in range(g.NI if both else 0):
        rows = slice(i * g.IP, (i + 1) * g.IP)
        col = b.mc[c, rows, :]
        e0c, e1c = col[:, 0:1], col[:, 1:2]
        own = b.O[rows, :].astype(F32)
        earlier = nn(b.L[rows, :], b.O[...])
        s0 = jnp.sum(jnp.where(lane < 64.0, earlier * own, 0.0), axis=1, keepdims=True)
        s1 = jnp.sum(jnp.where(lane < 64.0, 0.0, (earlier + base) * own), axis=1, keepdims=True)
        t0 = jnp.where(s0 < g.CAP, e0c * g.CP + s0, -1.0)
        t1 = jnp.where(s1 < g.CAP, e1c * g.CP + s1, -1.0)
        b.PT[rows, :] = jnp.where((slot_lane == t0) | (slot_lane == t1), 1.0, 0.0).astype(BF16)
    sub = fiota((128, g.TP), 0)
    own = jnp.where((sub == e0r) | (sub == e1r + 64.0), 1.0, 0.0)
    base = jnp.sum(jnp.where(sub == e0r + 64.0, 1.0, 0.0), axis=1, keepdims=True)
    earlier = nt(own.astype(BF16), b.L[...])
    s0 = jnp.sum(jnp.where(sub < 64.0, earlier * own, 0.0), axis=0, keepdims=True)
    s1 = jnp.sum(jnp.where(sub < 64.0, 0.0, (earlier + base) * own), axis=0, keepdims=True)
    t0 = jnp.where(s0 < g.CAP, e0r * g.CP + s0, -1.0)
    t1 = jnp.where(s1 < g.CAP, e1r * g.CP + s1, -1.0)
    slot_sub = fiota((g.CP, g.TP), 0)

    def fill(e2):
        at = slot_sub + (e2 * g.CP).astype(F32)
        b.P[pl.ds(pl.multiple_of(e2 * g.CP, 16), g.CP), :] = jnp.where(
            (at == t0) | (at == t1), 1.0, 0.0
        ).astype(BF16)

    loop(g.ne, fill)


def pack_rows(g, e2):
    return pl.ds(pl.multiple_of(e2 * g.CP, 16), g.CP)


def piece_rows(g, d, e2):
    return pl.ds(pl.multiple_of((d * g.ne + e2) * g.PR, 16), g.PR)


def weights_out(g, p, b):
    own = piece_rows(g, p.d, p.e)
    if g.aligned:
        mine = p.d * g.ne + p.e

        def to_expert(k):
            device = p.along(p.other(k + 1))
            send(b, "wz", b.wp, b.W.at[p.h, own, :], k, p.e, device)
            send(b, "mz", b.mp, b.MI.at[own, :], k, p.e, device)

        loop(g.ne - 1, to_expert)
        send(b, "wx", b.wp, b.W.at[p.h, own, :], p.e, p.e, p.twin)
        send(b, "mx", b.mp, b.MI.at[own, :], p.e, p.e, p.twin)
        send(b, "wy", b.wp, b.W.at[p.h, own, :], mine, mine, p.across)
        send(b, "wc", b.wp, b.W.at[p.h, own, :], mine, mine, p.core)
        b.W[p.h, own, :] = b.wp[...]
        b.MI[own, :] = b.mp[...]
    else:
        send(b, "wy", b.wp, b.W.at[p.h], 0, 0, p.across)
        send(b, "wc", b.wp, b.W.at[p.h], 0, 0, p.core)
        b.W[p.h] = b.wp[...]
        b.MI[...] = b.mp[...]


def weights_on(g, p, b):
    if not g.aligned:
        return

    def relay(k):
        e2 = p.other(k + 1)
        rows = piece_rows(g, p.d, e2)
        at = p.d * g.ne + e2
        part = b.W.at[p.h, rows, :]
        arrived(b, p, "wz", part, e2)
        send(b, "wx", part, part, e2, e2, p.twin)
        send(b, "wy", part, part, at, at, p.across)
        send(b, "wc", part, part, at, at, p.core)
        part = b.MI.at[rows, :]
        arrived(b, p, "mz", part, e2)
        send(b, "mx", part, part, e2, e2, p.twin)

    loop(g.ne - 1, relay)


def weights_end(g, p, b):
    if not g.aligned:
        return

    def relay(k):
        e2 = p.other(k)
        rows = piece_rows(g, p.od, e2)
        at = p.od * g.ne + e2
        part = b.W.at[p.h, rows, :]
        arrived(b, p, "wx", part, e2)
        send(b, "wy", part, part, at, at, p.across)
        send(b, "wc", part, part, at, at, p.core)
        arrived(b, p, "mx", b.MI.at[rows, :], e2)

    loop(g.ne, relay)


def pieces(g):
    return g.nd * g.ne if g.aligned else 1


def piece_of(g, ref, group, i):
    if not g.aligned:
        return ref.at[group]
    return ref.at[group, pl.ds(pl.multiple_of(i * g.PR, 16), g.PR), :]


def group_in(g, p, b, k):
    @pl.when(k == 1)
    def _():
        loop(pieces(g), lambda i: arrived(b, p, "wc", piece_of(g, b.W, p.hcore, i), i))

    @pl.when(k == 2)
    def _():
        def on(i):
            part = piece_of(g, b.W, p.hy, i)
            arrived(b, p, "wy", part, i)
            send(b, "wd", part, part, i, i, p.core)

        loop(pieces(g), on)

    @pl.when(k == 3)
    def _():
        loop(pieces(g), lambda i: arrived(b, p, "wd", piece_of(g, b.W, p.hdiag, i), i))


def masks(rows):
    lane = iota((rows, 128), 1)
    return lane < 64, lane >= 64


def attention(g, p, b):
    low, high = masks(g.IP)
    live = iota((g.IP, g.IP), 1) < SEQ
    zero = jnp.zeros((g.IP, 128), BF16)

    def group(k):
        group_in(g, p, b, k)

        @pl.when(k == 1)
        def _():
            loop(g.ne // 2 - 1, lambda i: cotangent_on(g, p, b, p.other(i + 1)))
            cotangent_over(g, p, b, p.e)

        @pl.when(k == 3)
        def _():
            loop(g.ne - g.ne // 2, lambda i: cotangent_on(g, p, b, p.other(i + g.ne // 2)))

        gi = 2 * lax.rem(p.y + lax.div(k, 2), 2) + lax.rem(p.c + k, 2)
        for blk in range(2):
            rows = slice(blk * g.IP, (blk + 1) * g.IP)
            b.QKV[gi, rows, :] = nn(b.ACT1[rows, :], b.W[gi, :, 0:640]).astype(BF16)
        for blk in range(2):
            rows = slice(blk * g.IP, (blk + 1) * g.IP)
            outs = []
            for j in range(3):
                qt = b.QKV[gi, rows, (j // 2) * 128 : (j // 2) * 128 + 128]
                kt = b.QKV[gi, rows, 384 + (j // 2) * 128 : 384 + (j // 2) * 128 + 128]
                vt = b.QKV[gi, rows, 128 + ((j + 1) // 2) * 128 : 256 + ((j + 1) // 2) * 128]
                scores = nt(jnp.where(high if j == 1 else low, qt, zero), kt) * (HD**-0.5)
                scores = jnp.where(live, scores, -1e30)
                scores = jnp.exp(scores - jnp.max(scores, axis=1, keepdims=True))
                probs = (scores / jnp.sum(scores, axis=1, keepdims=True)).astype(BF16)
                b.PB[gi, blk * 3 + j] = probs
                outs.append(nn(probs, vt))
            b.ATT[gi, rows, 0:128] = jnp.where(high, outs[0], 0.0).astype(BF16)
            b.ATT[gi, rows, 128:256] = jnp.where(low, outs[1], outs[2]).astype(BF16)
        for blk in range(2):
            rows = slice(blk * g.IP, (blk + 1) * g.IP)
            b.HID[rows, :] += nt(b.ATT[gi, rows, :], b.W[gi, :, 512:768])

    loop(4, group)


def rows16s(count, body):
    run = count // 32

    def step(i):
        for j in range(run):
            body(pl.ds(pl.multiple_of((i * run + j) * 16, 16), 16))

    loop(2, step)


def first_norm(g, b):
    def rows16(rows):
        x = b.X[rows, :].astype(F32)
        normed, _ = normalize(x)
        b.ACT1[rows, :] = (normed * b.GN[0:1, :]).astype(BF16)
        b.HID[rows, :] = x

    rows16s(2 * g.IP, rows16)


def second_norm(g, b):
    def rows16(rows):
        normed, _ = normalize(b.HID[rows, :])
        b.ACT2[rows, :] = (normed * b.GN[1:2, :]).astype(BF16)

    rows16s(2 * g.IP, rows16)
    lane = iota((g.IP, 128), 1)
    for blk in range(2):
        rows = slice(blk * g.IP, (blk + 1) * g.IP)
        logits = jnp.where(lane < g.ne, nn(b.ACT2[rows, :], b.RW[...]), -1e30)
        weight = jnp.exp(logits - jnp.max(logits, axis=1, keepdims=True))
        probs = weight / jnp.sum(weight, axis=1, keepdims=True)
        b.PRB[rows, :] = probs
        top = probs.astype(BF16).astype(F32)
        rest = probs - top
        b.PRH[rows, :] = (top + pltpu.roll(rest, 64, 1)).astype(BF16)


def small_weights(g, b):
    lane = iota((g.D, 128), 1)
    small = b.MI[...].astype(F32)
    b.RW[...] = jnp.where(lane < g.ne, small, 0.0).astype(BF16)
    gains = jnp.transpose(small)[120:128, :]
    b.GN[0:1, :] = gains[0:1, :] + gains[1:2, :]
    b.GN[1:2, :] = gains[2:3, :] + gains[3:4, :]


def half_of(g, i):
    return pl.ds(pl.multiple_of(i * g.DH, 128), g.DH)


def own_rows(g, c):
    return pl.ds(pl.multiple_of(c * 2 * g.IP, 16), 2 * g.IP)


def tokens_out(g, p, b):
    rows = own_rows(g, p.c)
    send(b, "ta", b.ACT2.at[:, half_of(g, p.oc)], b.TA.at[rows, :], 0, 0, p.core)
    send(b, "tp", b.PRH, b.TG.at[rows, :], 0, 0, p.core)
    b.TA[rows, :] = b.ACT2[:, half_of(g, p.c)]
    b.TG[rows, :] = b.PRH[...]


def tokens_in(g, p, b):
    arrived(b, p, "ta", b.TA.at[own_rows(g, p.oc), :], 0)
    arrived(b, p, "tp", b.TG.at[own_rows(g, p.oc), :], 0)


def cotangent_out(g, p, b):
    def pack(k):
        e2 = p.other(k)
        rows = nn(b.P[pack_rows(g, e2), :], b.UPP[...]).astype(BF16)

        @pl.when(k > 0)
        def _():
            b.PKU[e2] = rows
            send(b, "uz", b.PKU.at[e2], b.US.at[p.e, p.c, p.y], k, p.e, p.along(e2))

        @pl.when(k == 0)
        def _():
            part = b.US.at[p.e, p.c, p.y]
            b.US[p.e, p.c, p.y] = rows
            send(b, "uy", part, part, p.e, p.e, p.across)
            send(b, "uc", part, part, p.e, p.e, p.core)

    loop(g.ne, pack)


def cotangent_on(g, p, b, e2):
    part = b.US.at[e2, p.c, p.y]
    arrived(b, p, "uz", part, e2)
    send(b, "uy", part, part, e2, e2, p.across)
    send(b, "uc", part, part, e2, e2, p.core)


def cotangent_over(g, p, b, e2):
    part = b.US.at[e2, p.c, p.oy]
    arrived(b, p, "uy", part, e2)
    send(b, "ud", part, part, e2, e2, p.core)


def slots_out(g, p, b):
    row = iota((g.CP, g.DH), 0)
    eye = row == iota((g.CP, g.DH), 1)
    lane = iota((g.CP, 128), 1)

    def pack(k):
        e2 = p.other(k)
        hot = b.P[pack_rows(g, e2), :]
        tok = nn(hot, b.TA[...])
        gates = nn(hot, b.TG[...])
        gate = jnp.sum(
            jnp.where((lane == e2) | (lane == e2 + 64), gates, 0.0), axis=1, keepdims=True
        )
        b.GC[e2] = jnp.broadcast_to(gate, (g.CP, 128))
        across = jnp.sum(jnp.where(eye, gate, 0.0), axis=0, keepdims=True)
        top = across.astype(BF16).astype(F32)
        rows = jnp.where(row == g.CAP, top, jnp.where(row == g.CAP + 1, across - top, tok))
        rows = rows.astype(BF16)

        @pl.when(k > 0)
        def _():
            b.PKA[e2] = rows
            send(b, "xz", b.PKA.at[e2], b.XS.at[p.e, p.y, p.c], k, p.e, p.along(e2))

        @pl.when(k == 0)
        def _():
            part = b.XS.at[p.e, p.y, p.c]
            b.XS[p.e, p.y, p.c] = rows
            send(b, "xy", part, part, p.e, p.e, p.across)
            send(b, "xc", part, part, p.e, p.e, p.core)

    loop(g.ne, pack)


def slots_on(g, p, b, e2):
    part = b.XS.at[e2, p.y, p.c]
    arrived(b, p, "xz", part, e2)
    send(b, "xy", part, part, e2, e2, p.across)
    send(b, "xc", part, part, e2, e2, p.core)


def slots_over(g, p, b, e2):
    part = b.XS.at[e2, p.oy, p.c]
    arrived(b, p, "xy", part, e2)
    send(b, "xd", part, part, e2, e2, p.core)


def slots_in(g, p, b, e2):
    arrived(b, p, "xc", b.XS.at[e2, p.y, p.oc], e2)
    arrived(b, p, "xd", b.XS.at[e2, p.oy, p.oc], e2)
    arrived(b, p, "uc", b.US.at[e2, p.oc, p.y], e2)
    arrived(b, p, "ud", b.US.at[e2, p.oc, p.oy], e2)


CHUNKS = 4


def chunk(rows, i):
    size = rows // CHUNKS
    return pl.ds(i * size, size)


def experts_out(g, p, b, which):
    for i in which:
        name, src, dst = ("ei", b.wi, b.WI) if i < CHUNKS else ("eb", b.wb, b.WB)
        rows = chunk(src.shape[0], i % CHUNKS)
        send(b, name, src.at[rows, :], dst.at[p.d, rows, :], i % CHUNKS, i % CHUNKS, p.twin)


def experts_in(g, p, b):
    for i in range(CHUNKS):
        arrived(b, p, "ei", b.WI.at[p.od, chunk(g.DH, i), :], i)
    for i in range(CHUNKS):
        arrived(b, p, "eb", b.WB.at[p.od, chunk(g.F, i), :], i)


def back_core(g, p, b, part, s):
    send(b, "rc", part.at[s, :, p.oc], b.RC.at[s], s, s, p.core)


def back_over(g, p, b, part, s):
    arrived(b, p, "rc", b.RC.at[s], s)
    b.RC[s, p.oy] = (part[s, p.oy, p.c].astype(F32) + b.RC[s, p.oy].astype(F32)).astype(BF16)
    send(b, "ry", b.RC.at[s, p.oy], b.RY.at[s], s, s, p.across)


def back_on(g, p, b, part, s):
    arrived(b, p, "ry", b.RY.at[s], s)
    total = (
        part[s, p.y, p.c].astype(F32) + b.RC[s, p.y].astype(F32) + b.RY[s].astype(F32)
    ).astype(BF16)

    @pl.when(s != p.e)
    def _():
        b.RC[s, p.y] = total
        send(b, "rz", b.RC.at[s, p.y], b.RO.at[p.e], s, p.e, p.along(s))

    @pl.when(s == p.e)
    def _():
        b.RO[p.e] = total


def back_in(g, p, b):
    def rows_of(k):
        s = p.other(k + 1)
        arrived(b, p, "rz", b.RO.at[s], s)

    loop(g.ne - 1, rows_of)


def back_end(g, p, b):
    def rets(s):
        left(b, p, "rc", b.RC.at[0], s)
        left(b, p, "ry", b.RY.at[0], s)

    loop(g.ne, rets)
    loop(g.ne - 1, lambda k: left(b, p, "rz", b.RY.at[0], p.other(k + 1)))


def gelu_parts(u):
    inner = 0.7978845608028654 * (u + 0.044715 * u * u * u)
    tangent = jnp.tanh(inner)
    value = 0.5 * u * (1.0 + tangent)
    slope = 0.5 * (1.0 + tangent) + 0.5 * u * (1.0 - tangent * tangent) * 0.7978845608028654 * (
        1.0 + 3.0 * 0.044715 * u * u
    )
    return value, slope


def expert(g, b, first, between=None):
    base = g.CP - 16
    row = iota((g.CP, g.DH), 0)
    eye = row == iota((g.CP, g.DH), 1)
    for i in range(g.SG):
        for blk in range(2):
            tail = b.XS[first + i, blk, 0, base:, :].astype(F32)
            gate = tail[g.CAP - base : g.CAP - base + 1] + tail[g.CAP - base + 1 : g.CAP - base + 2]
            gate = jnp.sum(jnp.where(eye, gate, 0.0), axis=1, keepdims=True)
            at = (i * 2 + blk) * g.CP
            for q in range(2):
                b.GP[at : at + g.CP, q * g.DH : (q + 1) * g.DH] = (
                    b.US[first + i, blk, q].astype(F32) * gate
                ).astype(BF16)
    x = [b.XS[pl.ds(first, g.SG), :, q].reshape(g.R, g.DH) for q in range(2)]
    for n in range(g.F // 256):
        cols = slice(n * 256, n * 256 + 256)
        pre = nn(x[0], b.WI[0, :, cols]) + nn(x[1], b.WI[1, :, cols])
        value, slope = gelu_parts(pre)
        b.HQ[:, cols] = value.astype(BF16)
        grad = nt(b.GP[:, : g.DH], b.WB[0, cols, :]) + nt(b.GP[:, g.DH :], b.WB[1, cols, :])
        b.GR[:, cols] = (grad * slope).astype(BF16)
    if between is not None:
        between()
    shape = (g.SG, 2, g.CP, g.DH)
    dots = []
    for q in range(2):
        out = nn(b.HQ[...], b.WB[q]).astype(BF16)
        b.PO[pl.ds(first, g.SG), :, q] = out.reshape(shape)
        up = b.US[pl.ds(first, g.SG), :, q].reshape(g.R, g.DH)
        dots.append(jnp.sum(out.astype(F32) * up.astype(F32), axis=1, keepdims=True))
        b.DB[q] += tn(b.HQ[...], b.GP[:, q * g.DH : (q + 1) * g.DH])
        b.DI[q] += tn(x[q], b.GR[...])
    dots = dots[0] + dots[1]
    for q in range(2):
        back = nt(b.GR[...], b.WI[q])
        for i in range(g.SG):
            for blk in range(2):
                at = (i * 2 + blk) * g.CP
                along = jnp.sum(jnp.where(eye, dots[at : at + g.CP], 0.0), axis=0, keepdims=True)
                if q == 1:
                    along = along - along.astype(BF16).astype(F32)
                b.PG[first + i, blk, q] = jnp.where(
                    row == g.CAP, along, back[at : at + g.CP]
                ).astype(BF16)


def experts(g, p, b):
    b.DB[...] = jnp.zeros_like(b.DB)
    b.DI[...] = jnp.zeros_like(b.DI)
    n = g.ne
    if g.SG > 1:
        loop(n - 1, lambda k: cotangent_over(g, p, b, p.other(k + 1)))
        loop(n - 1, lambda k: slots_on(g, p, b, p.other(k + 1)))
        loop(n, lambda k: slots_over(g, p, b, p.other(k)))
        loop(n, lambda k: slots_in(g, p, b, p.other(k)))
        experts_in(g, p, b)
        loop(n // g.SG, lambda t: expert(g, b, t * g.SG))
        loop(n, lambda k: back_core(g, p, b, b.PG, p.other(k)))
        loop(n, lambda k: back_over(g, p, b, b.PG, p.other(k)))
        loop(n - 1, lambda k: back_on(g, p, b, b.PG, p.other(k)))
        return
    loop(n - 1, lambda k: cotangent_over(g, p, b, p.other(k + 1)))
    slots_over(g, p, b, p.e)
    slots_in(g, p, b, p.e)
    experts_in(g, p, b)

    def source(k):
        @pl.when(k > 0)
        def _():
            back_over(g, p, b, b.PG, p.other(k - 1))
            slots_over(g, p, b, p.other(k))
            slots_in(g, p, b, p.other(k))

        def between():
            @pl.when(k < n - 1)
            def _():
                slots_on(g, p, b, p.other(k + 1))

            @pl.when(k > 1)
            def _():
                back_on(g, p, b, b.PG, p.other(k - 2))

        expert(g, b, p.other(k), between)
        back_core(g, p, b, b.PG, p.other(k))

    loop(n, source)
    back_on(g, p, b, b.PG, p.other(n - 2))
    back_over(g, p, b, b.PG, p.other(n - 1))


def first_sends_end(g, p, b):
    n = g.ne
    if g.aligned:
        own = piece_rows(g, p.d, p.e)

        def z(k):
            left(b, p, "wz", b.wp, k)
            left(b, p, "mz", b.mp, k)

        loop(n - 1, z)

        def x(k):
            left(b, p, "wx", b.wp, k)
            left(b, p, "mx", b.mp, k)

        loop(n, x)

    def w(i):
        for name in ("wy", "wc", "wd"):
            left(b, p, name, piece_of(g, b.W, p.h, i), i)

    loop(pieces(g), w)
    left(b, p, "ta", b.TA.at[own_rows(g, 0), :], 0)
    left(b, p, "tp", b.TG.at[own_rows(g, 0), :], 0)

    def slots(k):
        left(b, p, "uz", b.PKU.at[0], k + 1)
        left(b, p, "xz", b.PKA.at[0], k + 1)

    loop(n - 1, slots)

    def on(k):
        for name in ("uy", "uc", "ud"):
            left(b, p, name, b.US.at[0, 0, 0], k)
        for name in ("xy", "xc", "xd"):
            left(b, p, name, b.XS.at[0, 0, 0], k)

    loop(n, on)
    for i in range(CHUNKS):
        left(b, p, "ei", b.wi.at[chunk(g.DH, 0), :], i)
        left(b, p, "eb", b.wb.at[chunk(g.F, 0), :], i)


KEEP = ("X", "UPO", "W", "RW", "GN", "QKV", "PB", "ATT", "HID", "PRB", "PT", "GC", "PO", "RO", "KI", "KB", "SI", "SB")


def first_kernel(g, b):
    p = Place(g)
    rows_out(g, p, b)
    p.enter()
    weights_out(g, p, b)
    experts_out(g, p, b, range(2))
    b.WI[p.d] = b.wi[...]
    b.WB[p.d] = b.wb[...]
    rows_in(g, p, b)
    route(g, b, p.c, False)
    weights_on(g, p, b)
    cotangent_out(g, p, b)
    weights_end(g, p, b)
    experts_out(g, p, b, range(2, 2 * CHUNKS))
    route(g, b, p.y, True)
    small_weights(g, b)
    first_norm(g, b)
    stow(b, "X", "UPO", "RW", "GN", "PT")
    attention(g, p, b)
    stow(b, "W", "QKV", "PB", "ATT", "HID")
    second_norm(g, b)
    stow(b, "PRB")
    tokens_out(g, p, b)
    tokens_in(g, p, b)
    slots_out(g, p, b)
    stow(b, "GC")
    experts(g, p, b)
    stow(b, "PO")
    b.KI[...] = b.DI[p.d]
    b.KB[...] = b.DB[p.d]
    b.SI[...] = b.DI[p.od].astype(BF16)
    b.SB[...] = b.DB[p.od].astype(BF16)
    stow(b, "KI", "KB", "SI", "SB")
    back_on(g, p, b, b.PG, p.other(g.ne - 1))
    back_in(g, p, b)
    stow(b, "RO")
    first_sends_end(g, p, b)
    back_end(g, p, b)
    stowed(b, *KEEP)


def grads_of_expert_out(g, p, b):
    send(b, "gi", b.hSI, b.XI, 0, 0, p.twin)
    send(b, "gb", b.hSB, b.XB, 0, 0, p.twin)


def grads_of_expert_in(g, p, b):
    loaded(b, "KI", "KB")
    arrived(b, p, "gi", b.XI, 0)
    b.o_gi[...] = b.KI[...] + b.XI[...].astype(F32)
    arrived(b, p, "gb", b.XB, 0)
    b.o_gb[...] = b.KB[...] + b.XB[...].astype(F32)


def slots_back(g, p, b, kind):
    lane = iota((g.CP, 128), 1)
    base = g.CP - 16
    eye = iota((g.CP, g.DH), 0) == iota((g.CP, g.DH), 1)

    def rows_of(s):
        rows = pack_rows(g, s)
        if kind:
            b.RG[rows, 0 : g.DH] = b.RB[s]
            dots = b.RB[s, base:, :].astype(F32)[g.CAP - base : g.CAP - base + 1]
            dots = jnp.sum(jnp.where(eye, dots, 0.0), axis=1, keepdims=True)
            b.RG[rows, g.DH :] = jnp.where(lane == s, dots, 0.0).astype(BF16)
        else:
            b.RG[rows, 0 : g.DH] = (b.RO[s].astype(F32) * b.GC[s][:, 0:1]).astype(BF16)

    loop(g.ne, rows_of)


def unpack(g, p, b, kind):
    name, width = ("ug", g.DH + 128) if kind else ("uo", g.DH)
    out, landed = (b.UG, b.TR) if kind else (b.UO, b.TO)

    def rows(c, j):
        image = pl.ds(pl.multiple_of((2 * c + j) * g.IP, 16), g.IP)
        return nn(b.PT[image, :], b.RG[:, 0:width]).astype(BF16)

    for j in range(2):
        here = slice(j * g.IP, (j + 1) * g.IP)
        out[here, :] = rows(p.oc, j)
        send(b, name, out.at[here, :], landed.at[p.c, here, :], j, j, p.core)
    for j in range(2):
        landed[p.c, j * g.IP : (j + 1) * g.IP, :] = rows(p.c, j)


def unpacked(g, p, b, kind):
    name, landed = ("ug", b.TR) if kind else ("uo", b.TO)
    for j in range(2):
        arrived(b, p, name, landed.at[p.oc, j * g.IP : (j + 1) * g.IP, :], j)


def mix(g, p, b):
    def rows16(rows):
        for q in range(2):
            cols = slice(q * g.DH, (q + 1) * g.DH)
            b.MX[rows, cols] = (b.HID[rows, cols] + b.TO[q, rows, :].astype(F32)).astype(BF16)

    rows16s(2 * g.IP, rows16)
    for j in range(2):
        part = b.MX.at[j * g.IP : (j + 1) * g.IP, :]
        here = (p.c == p.y) & (p.c == j)

        @pl.when(here)
        def _(j=j):
            b.MIX[p.y] = b.MX[j * g.IP : (j + 1) * g.IP, :]

        @pl.when(jnp.logical_not(here))
        def _(j=j, part=part):
            send(b, "mo", part, b.MIX.at[p.y], j, p.y, (p.d, p.e, 2 * p.c + j))


def mixed_in(g, p, b):
    for blk in range(2):

        @pl.when(jnp.logical_not((p.y == blk) & (p.c == p.y)))
        def _(blk=blk):
            arrived(b, p, "mo", b.MIX.at[blk], blk)

        b.o_mixed[blk] = b.MIX[blk, 0:SEQ, :]
    for j in range(2):

        @pl.when(jnp.logical_not((p.c == p.y) & (p.c == j)))
        def _(j=j):
            left(b, p, "mo", b.MIX.at[0], j)


def tokens_back(g, p, b):
    lane = iota((g.IP, 128), 1)
    b.GA[...] = jnp.zeros_like(b.GA)
    for blk in range(2):
        rows = slice(blk * g.IP, (blk + 1) * g.IP)
        gate = b.TR[0, rows, g.DH :].astype(F32) + b.TR[1, rows, g.DH :].astype(F32)
        probs = b.PRB[rows, :]
        grad = probs * (gate - jnp.sum(probs * gate, axis=1, keepdims=True))
        b.GL[rows, :] = grad.astype(BF16)
        b.GHID[rows, :] = nt(b.GL[rows, :], b.RW[...])

    def rows16(rows):
        normed, inverse = normalize(b.HID[rows, :])
        upstream = b.GHID[rows, :] + jnp.concatenate(
            [b.TR[q, rows, 0 : g.DH].astype(F32) for q in range(2)], axis=1
        )
        prod = upstream * normed
        b.GA[8:16, :] += prod[0:8, :] + prod[8:16, :]
        b.ACT2[rows, :] = (normed * b.GN[1:2, :]).astype(BF16)
        hidden = b.UPO[rows, :].astype(F32) + norm_backward(upstream, normed, inverse, b.GN[1:2, :])
        b.GHID[rows, :] = hidden
        b.GHL[rows, :] = hidden.astype(BF16)

    rows16s(2 * g.IP, rows16)


def first_norm_again(g, b):
    def rows16(rows):
        normed, _ = normalize(b.X[rows, :].astype(F32))
        b.ACT1[rows, :] = (normed * b.GN[0:1, :]).astype(BF16)

    rows16s(2 * g.IP, rows16)


def attention_back(g, p, b):
    low, high = masks(g.IP)
    zero = jnp.zeros((g.IP, 128), BF16)
    scale = HD**-0.5
    b.DA[...] = jnp.zeros_like(b.DA)

    def group(k):
        @pl.when(k == 2)
        def _():
            loop(g.ne // 2, lambda i: back_on(g, p, b, b.PO, p.other(i + 1)))

        @pl.when(k == 3)
        def _():
            loop(g.ne - g.ne // 2, lambda i: back_on(g, p, b, b.PO, p.other(i + g.ne // 2 + 1)))
            weights_back(g, p, b, 0, 1)

        yk = lax.rem(p.oy + lax.div(k, 2), 2)
        gi = 2 * yk + lax.rem(p.oc + k, 2)
        for blk in range(2):
            rows = slice(blk * g.IP, (blk + 1) * g.IP)
            grad = nn(b.GHL[rows, :], b.W[gi, :, 512:768]).astype(BF16)
            tiles = [grad[:, 0:128], grad[:, 128:256]]
            dq, dk, dv = [], [], []
            for j in range(3):
                probs = b.PB[gi, blk * 3 + j]
                gt = tiles[(j + 1) // 2]
                qt = b.QKV[gi, rows, (j // 2) * 128 : (j // 2) * 128 + 128]
                kt = b.QKV[gi, rows, 384 + (j // 2) * 128 : 384 + (j // 2) * 128 + 128]
                vt = b.QKV[gi, rows, 128 + ((j + 1) // 2) * 128 : 256 + ((j + 1) // 2) * 128]
                grad_probs = nt(jnp.where(low if j == 1 else high, gt, zero), vt)
                wide = probs.astype(F32)
                grad_scores = wide * (
                    grad_probs - jnp.sum(wide * grad_probs, axis=1, keepdims=True)
                )
                grad_scores = (grad_scores * scale).astype(BF16)
                dv.append(tn(probs, gt))
                dq.append(nn(grad_scores, kt))
                dk.append(tn(grad_scores, qt))
            b.GJ[rows, 0:128] = jnp.where(low, dq[0], dq[1]).astype(BF16)
            b.GJ[rows, 128:256] = jnp.where(low, dq[2], dv[0]).astype(BF16)
            b.GJ[rows, 256:384] = jnp.where(low, dv[1], dv[2]).astype(BF16)
            b.GJ[rows, 384:512] = jnp.where(low, dk[0], dk[1]).astype(BF16)
            b.GJ[rows, 512:640] = jnp.where(low, dk[2], 0.0).astype(BF16)
        for blk in range(2):
            rows = slice(blk * g.IP, (blk + 1) * g.IP)
            b.DA[rows, :] += nt(b.GJ[rows, :], b.W[gi, :, 0:640])
        for m in range(g.D // 256):
            cols = slice(m * 256, m * 256 + 256)
            first = tn(b.ACT1[:, cols], b.GJ[...])
            second = tn(b.GHL[:, cols], b.ATT[gi])
            b.DW[gi, cols, 0:512] = first[:, 0:512].astype(BF16)
            b.DW[gi, cols, 512:640] = (first[:, 512:] + second[:, 0:128]).astype(BF16)
            b.DW[gi, cols, 640:768] = second[:, 128:].astype(BF16)

        @pl.when(lax.rem(k, 2) == 0)
        def _():
            send(b, "dc", b.DW.at[gi], b.RDC.at[yk], yk, yk, p.core)

        @pl.when(lax.rem(k, 2) == 1)
        def _():
            arrived(b, p, "dc", b.RDC.at[yk], yk)
            if g.aligned:

                def to_twin(i):
                    e2 = p.other(i + 1)
                    rows = piece_rows(g, p.od, e2)
                    at = yk * g.ne + e2
                    b.DW[gi, rows, :] = (
                        b.DW[gi, rows, :].astype(F32) + b.RDC[yk, rows, :].astype(F32)
                    ).astype(BF16)
                    send(b, "dx", b.DW.at[gi, rows, :], b.RDX.at[yk, e2], at, at, p.twin)

                loop(g.ne, to_twin)

    loop(4, group)


def inputs_back(g, p, b):
    def rows16(rows):
        normed, inverse = normalize(b.X[rows, :].astype(F32))
        upstream = b.DA[rows, :]
        prod = upstream * normed
        b.GA[0:8, :] += prod[0:8, :] + prod[8:16, :]
        b.GIN[rows, :] = (
            b.GHID[rows, :] + norm_backward(upstream, normed, inverse, b.GN[0:1, :])
        ).astype(BF16)

    rows16s(2 * g.IP, rows16)
    for j in range(2):
        rows = slice(j * g.IP, (j + 1) * g.IP)
        image = 2 * p.c + j
        b.GIN[rows, :] = nn(shift(g, image, True), b.GIN[rows, :]).astype(BF16)
        b.EG[j, 0] = b.GIN[j * g.IP : j * g.IP + 16, :]
        b.EG[j, 1] = b.GIN[(j + 1) * g.IP - 16 : (j + 1) * g.IP, :]
        for name, device in (("i", p.across), ("j", p.core)):
            middle = b.GIN.at[j * g.IP + 16 : (j + 1) * g.IP - 16, :]
            send(b, name + "m", middle, b.o_gin.at[p.y, middle_of(g, image), :], j, j, device)
            send(b, name + "e", b.EG.at[j], b.ED.at[p.y, image], j, j, device)
        b.o_gin[p.y, middle_of(g, image), :] = b.GIN[j * g.IP + 16 : (j + 1) * g.IP - 16, :]
        b.ED[p.y, image] = b.EG[j]


def middle_of(g, image):
    return pl.ds(pl.multiple_of(image * g.WIN + 16, 16), g.WIN - 16)


def inputs_end(g, p, b):
    for j in range(2):
        image = 2 * p.c + j
        middle, edge = b.o_gin.at[p.oy, middle_of(g, image), :], b.ED.at[p.oy, image]
        arrived(b, p, "im", middle, j)
        send(b, "km", middle, middle, j, j, p.core)
        arrived(b, p, "ie", edge, j)
        send(b, "ke", edge, edge, j, j, p.core)


def inputs_last(g, p, b):
    for j in range(2):
        image = 2 * p.oc + j
        for name, yy in (("j", p.y), ("k", p.oy)):
            arrived(b, p, name + "m", b.o_gin.at[yy, middle_of(g, image), :], j)
            arrived(b, p, name + "e", b.ED.at[yy, image], j)
    for blk in range(2):
        b.o_gin[blk, 0:16, :] = b.ED[blk, 0, 0]
        for i in range(1, g.NI):
            b.o_gin[blk, i * g.WIN : i * g.WIN + 16, :] = b.ED[blk, i, 0] + b.ED[blk, i - 1, 1]
        b.o_gin[blk, g.NI * g.WIN : g.NI * g.WIN + 16, :] = b.ED[blk, g.NI - 1, 1]


def weights_back(g, p, b, first, count):
    if not g.aligned:
        if first == 0:
            b.DW[p.hy] = (b.DW[p.hy].astype(F32) + b.RDC[p.oy].astype(F32)).astype(BF16)
            send(b, "dy", b.DW.at[p.hy], b.RDY, 0, 0, p.across)
        return

    def to_across(i):
        e2 = p.other(first + i + 1)
        rows = piece_rows(g, p.d, e2)
        arrived(b, p, "dx", b.RDX.at[p.oy, e2], p.oy * g.ne + e2)
        b.RDX[p.oy, e2] = (
            b.DW[p.hy, rows, :].astype(F32)
            + b.RDC[p.oy, rows, :].astype(F32)
            + b.RDX[p.oy, e2].astype(F32)
        ).astype(BF16)
        send(b, "dy", b.RDX.at[p.oy, e2], b.RDY.at[e2], e2, e2, p.across)

    loop(count, to_across)


def weights_back_on(g, p, b):
    if not g.aligned:
        arrived(b, p, "dy", b.RDY, 0)
        total = b.DW[p.h].astype(F32) + b.RDC[p.y].astype(F32) + b.RDY[...].astype(F32)
        b.o_dw[...] = total.astype(BF16)
        return

    def piece(k):
        e2 = p.other(k + 1)
        rows = piece_rows(g, p.d, e2)
        arrived(b, p, "dx", b.RDX.at[p.y, e2], p.y * g.ne + e2)
        arrived(b, p, "dy", b.RDY.at[e2], e2)
        mine = (
            b.DW[p.h, rows, :].astype(F32)
            + b.RDC[p.y, rows, :].astype(F32)
            + b.RDX[p.y, e2].astype(F32)
            + b.RDY[e2].astype(F32)
        )

        @pl.when(k < g.ne - 1)
        def _():
            b.SDZ[e2] = mine.astype(BF16)
            send(b, "dz", b.SDZ.at[e2], b.RDZ.at[p.e], k, p.e, p.along(e2))

        @pl.when(k == g.ne - 1)
        def _():
            b.o_dw[...] = mine

    loop(g.ne, piece)


def weights_back_end(g, p, b):
    if not g.aligned:
        return

    def add(k):
        e2 = p.other(k + 1)
        arrived(b, p, "dz", b.RDZ.at[e2], e2)
        b.o_dw[...] += b.RDZ[e2].astype(F32)

    loop(g.ne - 1, add)


def small_back(g, p, b):
    sub = iota((128, g.D), 0)
    one = jnp.sum(b.GA[0:8, :], axis=0, keepdims=True)
    two = jnp.sum(b.GA[8:16, :], axis=0, keepdims=True)
    gains = jnp.where(sub == 120, one, jnp.where(sub == 122, two, 0.0))
    b.GM[...] = tn(b.ACT2[...], b.GL[...]) + jnp.transpose(gains)
    if not g.aligned:
        b.SMC[...] = b.GM[...].astype(BF16)
        return
    b.SMX[...] = b.GM[...].astype(BF16)
    mine = p.d * g.ne + p.e

    def to(k):
        for far, d2 in enumerate((p.d, p.od)):
            e2 = p.other(k)
            part = b.SMX.at[piece_rows(g, d2, e2), :]

            @pl.when((k > 0) | (far > 0))
            def _(far=far, d2=d2, e2=e2, part=part):
                send(b, "sp", part, b.RMP.at[mine], far * g.ne + k, mine, (d2, e2, p.h))

    loop(g.ne, to)


def small_back_on(g, p, b):
    if g.aligned:
        mine = p.d * g.ne + p.e
        b.RMP[mine] = b.SMX[piece_rows(g, p.d, p.e), :]

        def come(k):
            for far, d2 in enumerate((p.d, p.od)):
                at = d2 * g.ne + p.other(k)

                @pl.when((k > 0) | (far > 0))
                def _(at=at):
                    arrived(b, p, "sp", b.RMP.at[at], at)

        loop(g.ne, come)
        total = b.RMP[0].astype(F32)
        for i in range(1, g.nd * g.ne):
            total = total + b.RMP[i].astype(F32)
        b.SMC[...] = total.astype(BF16)
    for i, device in enumerate((p.core, p.across, p.diag)):
        send(b, "sh", b.SMC, b.RMH.at[p.h], i, p.h, device)
    b.RMH[p.h] = b.SMC[...]


def small_back_end(g, p, b):
    for h2 in (p.hcore, p.hy, p.hdiag):
        arrived(b, p, "sh", b.RMH.at[h2], h2)
    b.o_small[...] = (b.RMH[0].astype(F32) + b.RMH[1].astype(F32)) + (
        b.RMH[2].astype(F32) + b.RMH[3].astype(F32)
    )


def second_sends_end(g, p, b):
    n = g.ne
    left(b, p, "gi", b.XI, 0)
    left(b, p, "gb", b.XB, 0)

    back_end(g, p, b)

    def away(k):
        if g.aligned:
            left(b, p, "dz", b.SDZ.at[0], k)
            left(b, p, "sp", b.RMP.at[0], k + 1)

    loop(n - 1, away)
    for i in range(2):
        left(b, p, "dc", b.RDC.at[0], i)
        left(b, p, "ug", b.UG.at[0 : g.IP, :], i)
        left(b, p, "uo", b.UO.at[0 : g.IP, :], i)
        for name in ("i", "j", "k"):
            left(b, p, name + "m", b.o_gin.at[0, middle_of(g, 0), :], i)
            left(b, p, name + "e", b.ED.at[0, 0], i)
    if g.aligned:

        def moved(k):
            left(b, p, "sp", b.RMP.at[0], g.ne + k)
            left(b, p, "dx", b.RDX.at[0, 0], k)
            left(b, p, "dx", b.RDX.at[0, 0], g.ne + k)
            left(b, p, "dy", b.RDY.at[0], k)

        loop(n, moved)
    else:
        left(b, p, "dy", b.RDY, 0)
    for i in range(3):
        left(b, p, "sh", b.SMC, i)


def second_kernel(g, b):
    p = Place(g)
    fetch(b, "kRO", b.hRO, b.RB)
    names = ("PT", "PO", "GN", "X", "HID", "PRB", "RW", "UPO", "GC", "W", "QKV", "PB", "ATT", "KI", "KB")
    load(b, *names)
    p.enter(g.aligned)

    def outputs_out(k):
        s = p.other(k + 1)
        send(b, "rc", b.hPO.at[s, :, p.oc], b.RC.at[s], s, s, p.core)

    loop(g.ne, outputs_out)
    grads_of_expert_out(g, p, b)
    fetched(b, "kRO", b.hRO, b.RB)
    slots_back(g, p, b, 1)
    loaded(b, "PT")
    unpack(g, p, b, 1)
    loaded(b, "PO")
    loop(g.ne, lambda k: back_over(g, p, b, b.PO, p.other(k + 1)))
    loaded(b, "GN", "X")
    first_norm_again(g, b)
    unpacked(g, p, b, 1)
    loaded(b, "HID", "PRB", "RW", "UPO")
    tokens_back(g, p, b)
    loaded(b, "W", "QKV", "PB", "ATT", "GC")
    attention_back(g, p, b)
    weights_back(g, p, b, 1, 1)
    inputs_back(g, p, b)
    small_back(g, p, b)
    weights_back(g, p, b, 2, g.ne - 2)
    back_in(g, p, b)
    slots_back(g, p, b, 0)
    unpack(g, p, b, 0)
    inputs_end(g, p, b)
    unpacked(g, p, b, 0)
    mix(g, p, b)
    small_back_on(g, p, b)
    weights_back_on(g, p, b)
    mixed_in(g, p, b)
    grads_of_expert_in(g, p, b)
    inputs_last(g, p, b)
    small_back_end(g, p, b)
    weights_back_end(g, p, b)
    second_sends_end(g, p, b)


def call(body, g, inputs, far, outs, far_outs, scratch, sems, number, flops):
    names = [*inputs, *far, *outs, *far_outs, *scratch]
    single = [n for n in sems if n[0] == "k" and n[1].isupper() or n.startswith("ld")]
    names += [name + end for name in sems for end in (("_s",) if name in single else ("_s", "_r"))]

    def kernel(*refs):
        body(g, types.SimpleNamespace(**dict(zip(names, refs, strict=True))))

    vmem, anywhere = pl.BlockSpec(memory_space=pltpu.VMEM), pl.BlockSpec(memory_space=pl.ANY)
    made = pl.pallas_call(
        kernel,
        out_shape=[jax.ShapeDtypeStruct(*o) for o in [*outs.values(), *far_outs.values()]],
        in_specs=[vmem] * len(inputs) + [anywhere] * len(far),
        out_specs=[vmem] * len(outs) + [anywhere] * len(far_outs),
        scratch_shapes=[pltpu.VMEM(*s) for s in scratch.values()]
        + [pltpu.SemaphoreType.DMA((n,)) for name, n in sems.items() for _ in range(1 if name in single else 2)],
        compiler_params=pltpu.CompilerParams(
            collective_id=number, has_side_effects=True, vmem_limit_bytes=LIMIT
        ),
        cost_estimate=pl.CostEstimate(flops=flops, bytes_accessed=2**24, transcendentals=0),
    )(*inputs.values(), *far.values())
    return dict(zip([*outs, *far_outs], made, strict=True))


def shards(
    inputs, w_qkv, w_out, w_router, gain_one, gain_two, w_in, w_back, experts, priority, cotangent, *, mesh
):
    model, rows = inputs.shape[2], inputs.shape[1]
    g = Sizes(mesh, model, rows, w_in.shape[2])
    n, ip, cp, dh = g.ne, g.IP, g.CP, g.DH
    assert inputs.shape[0] == 2
    pad = ((0, 0), (0, 0), (0, ip - SEQ), (0, 0))
    part = jnp.concatenate([w_qkv[:, 0], w_qkv[:, 2], w_qkv[:, 1], w_out.T], axis=1)
    gains = jnp.stack([gain_one, gain_two], axis=1)
    top = gains.astype(BF16)
    rest = (gains - top.astype(F32)).astype(BF16)
    small = jnp.concatenate(
        [
            w_router,
            jnp.zeros((w_router.shape[0], 120 - n), BF16),
            top[:, :1],
            rest[:, :1],
            top[:, 1:],
            rest[:, 1:],
            jnp.zeros((w_router.shape[0], 4), BF16),
        ],
        axis=1,
    )
    if not g.aligned:
        part = lax.all_gather(part, ("dp", "expert"), axis=0, tiled=True)
        small = lax.all_gather(small, ("dp", "expert"), axis=0, tiled=True)
    info = jnp.concatenate([experts, priority[:, :, None]], axis=2).astype(F32)
    info = jnp.pad(info.reshape(2, g.NI, SEQ, 3), pad, constant_values=-1000.0)
    mc = jnp.pad(info.reshape(2, g.TP, 3), ((0, 0), (0, 0), (0, 5)))
    mr = jnp.swapaxes(mc, 1, 2)
    np_ = pieces(g)
    kept = dict(
        X=((2 * ip, model), BF16),
        UPO=((2 * ip, model), BF16),
        W=((4, model, model), BF16),
        RW=((model, 128), BF16),
        GN=((8, model), F32),
        QKV=((4, 2 * ip, 640), BF16),
        PB=((4, 6, ip, ip), BF16),
        ATT=((4, 2 * ip, 256), BF16),
        HID=((2 * ip, model), F32),
        PRB=((2 * ip, 128), F32),
        PT=((g.TP, g.SL), BF16),
        GC=((n, cp, 128), F32),
        PO=((n, 2, 2, cp, dh), BF16),
        RO=((n, cp, dh), BF16),
        KI=((dh, g.F), F32),
        KB=((g.F, dh), F32),
        SI=((dh, g.F), BF16),
        SB=((g.F, dh), BF16),
    )
    assert set(kept) == set(KEEP)
    one = call(
        first_kernel,
        g,
        dict(wp=part, mp=small, wi=w_in[0], wb=w_back[0], mc=mc, mr=mr),
        dict(xin=inputs, uin=cotangent),
        {},
        {"h" + name: made for name, made in kept.items()},
        dict(
            **kept,
            PG=((n, 2, 2, cp, dh), BF16),
            RC=((n, 2, cp, dh), BF16),
            RY=((n, cp, dh), BF16),
            UB=((rows, dh), BF16),
            UPP=((g.TP, dh), BF16),
            DI=((2, dh, g.F), F32),
            DB=((2, g.F, dh), F32),
            MI=((model, 128), BF16),
            L=((g.TP, g.TP), BF16),
            O=((g.TP, 128), BF16),
            P=((g.SL, g.TP), BF16),
            ACT1=((2 * ip, model), BF16),
            ACT2=((2 * ip, model), BF16),
            PRH=((2 * ip, 128), BF16),
            TA=((g.TP, dh), BF16),
            TG=((g.TP, 128), BF16),
            US=((n, 2, 2, cp, dh), BF16),
            XS=((n, 2, 2, cp, dh), BF16),
            PKA=((n, cp, dh), BF16),
            PKU=((n, cp, dh), BF16),
            WI=((2, dh, g.F), BF16),
            WB=((2, g.F, dh), BF16),
            GP=((g.R, model), BF16),
            HQ=((g.R, g.F), BF16),
            GR=((g.R, g.F), BF16),
        ),
        dict(wz=n, mz=n, wx=n, mx=n, wy=np_, wc=np_, wd=np_, ta=1, tp=1, uz=n, uy=n, uc=n, ud=n, xz=n, xy=n, xc=n, xd=n, ei=CHUNKS, eb=CHUNKS,
             rc=n, ry=n, rz=n, ldx=2, ldu=2, ldb=1, **{"k" + name: 1 for name in KEEP}),
        1,
        14 * 10**9,
    )
    rows_out = g.PR if g.aligned else model
    extra = (
        dict(
            RDX=((2, n, g.PR, model), BF16),
            SDZ=((n, g.PR, model), BF16),
            RDZ=((n, g.PR, model), BF16),
            SMX=((model, 128), BF16),
            RMP=((g.nd * n, g.PR, 128), BF16),
        )
        if g.aligned
        else {}
    )
    two = call(
        second_kernel,
        g,
        {},
        {"h" + name: one["h" + name] for name in KEEP},
        dict(
            o_mixed=((2, SEQ, model), BF16),
            o_gin=((2, rows, model), BF16),
            o_dw=((rows_out, model), F32 if g.aligned else BF16),
            o_small=((rows_out, 128), F32),
            o_gi=((dh, g.F), F32),
            o_gb=((g.F, dh), F32),
        ),
        {},
        dict(
            **{name: made for name, made in kept.items() if name not in ("SI", "SB", "RO")},
            RO=((n, cp, dh), BF16),
            RB=((n, cp, dh), BF16),
            RC=((n, 2, cp, dh), BF16),
            RY=((n, cp, dh), BF16),
            RG=((g.SL, dh + 128), BF16),
            UG=((2 * ip, dh + 128), BF16),
            UO=((2 * ip, dh), BF16),
            TR=((2, 2 * ip, dh + 128), BF16),
            TO=((2, 2 * ip, dh), BF16),
            MX=((2 * ip, model), BF16),
            MIX=((2, ip, model), BF16),
            EG=((2, 2, 16, model), BF16),
            ED=((2, 4, 2, 16, model), BF16),
            GL=((2 * ip, 128), BF16),
            GA=((16, model), F32),
            ACT1=((2 * ip, model), BF16),
            ACT2=((2 * ip, model), BF16),
            GHID=((2 * ip, model), F32),
            GHL=((2 * ip, model), BF16),
            DA=((2 * ip, model), F32),
            GJ=((2 * ip, 640), BF16),
            DW=((4, model, model), BF16),
            RDC=((2, model, model), BF16),
            RDY=((n, g.PR, model) if g.aligned else (model, model), BF16),
            GIN=((2 * ip, model), BF16),
            GM=((model, 128), F32),
            SMC=((rows_out, 128), BF16),
            RMH=((4, rows_out, 128), BF16),
            XI=((dh, g.F), BF16),
            XB=((g.F, dh), BF16),
            **extra,
        ),
        dict(rc=n, ry=n, rz=n, ug=2, uo=2, mo=2, gi=1, gb=1, dc=2, dy=n, dx=2 * n, dz=n, sp=2 * n, sh=4, im=2, ie=2, jm=2, je=2, km=2, ke=2,
             **{"k" + name: 1 for name in KEEP if name not in ("SI", "SB")}),
        2,
        14 * 10**9,
    )
    dw, ds = two["o_dw"], two["o_small"]
    if not g.aligned:
        dw = lax.psum_scatter(dw, ("dp", "expert"), scatter_dimension=0, tiled=True)
        ds = lax.psum_scatter(ds.astype(BF16), ("dp", "expert"), scatter_dimension=0, tiled=True)
        dw, ds = dw.astype(F32), ds.astype(F32)
    lw = g.LW
    grad_qkv = jnp.stack([dw[:, :lw], dw[:, 2 * lw : 3 * lw], dw[:, lw : 2 * lw]], axis=1)
    return (
        two["o_mixed"],
        two["o_gin"],
        grad_qkv,
        dw[:, 3 * lw :].T,
        ds[:, :n],
        ds[:, 120],
        ds[:, 122],
        two["o_gi"][None],
        two["o_gb"][None],
    )


def solution(mesh):
    both = ("dp", "expert")
    in_specs = (
        P(both, None, None),
        P(both, None, "head"),
        P("head", both),
        P(both, None),
        P(both),
        P(both),
        P("expert", "dp", "head"),
        P("expert", "head", "dp"),
        P(both, None, None),
        P(both, None),
        P(both, None, None),
    )
    out_specs = (
        P(both, "head", None),
        P(both, None, None),
        P(both, None, "head"),
        P("head", both),
        P(both, None),
        P(both),
        P(both),
        P("expert", "dp", "head"),
        P("expert", "head", "dp"),
    )
    return jax.shard_map(
        functools.partial(shards, mesh=mesh),
        mesh=mesh,
        in_specs=in_specs,
        out_specs=out_specs,
        check_vma=False,
    )
```

```python
import functools
import types

import jax
import jax.numpy as jnp
from jax import lax
from jax.experimental import pallas as pl
from jax.experimental.pallas import tpu as pltpu
from jax.sharding import PartitionSpec as P

HD = 64
SEQ = 196
MESH = pl.DeviceIdType.MESH
F32, BF16 = jnp.float32, jnp.bfloat16
LIMIT = 63 * 2**20


def up16(n):
    return -(-n // 16) * 16


def nn(a, b):
    return lax.dot_general(a, b, (((1,), (0,)), ((), ())), preferred_element_type=F32)


def nt(a, b):
    return lax.dot_general(a, b, (((1,), (1,)), ((), ())), preferred_element_type=F32)


def tn(a, b):
    return lax.dot_general(a, b, (((0,), (0,)), ((), ())), preferred_element_type=F32)


def loop(count, body):
    def step(i, carry):
        body(i)
        return carry

    lax.fori_loop(0, count, step, 0)


def iota(shape, dim):
    return lax.broadcasted_iota(jnp.int32, shape, dim)


def fiota(shape, dim):
    return iota(shape, dim).astype(F32)


def normalize(v):
    centered = v - jnp.mean(v, axis=1, keepdims=True)
    inverse = lax.rsqrt(jnp.mean(centered * centered, axis=1, keepdims=True) + 1e-06)
    return centered * inverse, inverse


def norm_backward(upstream, normed, inverse, gain):
    scaled = upstream * gain
    return inverse * (
        scaled
        - jnp.mean(scaled, axis=1, keepdims=True)
        - normed * jnp.mean(scaled * normed, axis=1, keepdims=True)
    )


class Sizes:
    def __init__(self, mesh, model, rows, hidden):
        self.nd, self.ne, self.nh = mesh.shape["dp"], mesh.shape["expert"], mesh.shape["head"]
        self.D, self.DH = model, model // 2
        self.M = rows
        self.CAP = rows // self.ne
        self.CP = up16(self.CAP + 2)
        self.IP = up16(SEQ)
        self.NI = rows // SEQ
        self.TP = self.NI * self.IP
        self.SL = self.ne * self.CP
        self.WIN = self.IP - 16
        self.LAG = SEQ - self.WIN
        self.F = hidden
        self.PR = model // (self.nd * self.ne)
        self.aligned = self.PR % 16 == 0
        self.SG = 1
        while self.SG * 2 * self.CP <= self.IP and self.ne % (self.SG * 2) == 0:
            self.SG *= 2
        self.R = self.SG * 2 * self.CP
        self.LW = model // self.nh
        assert self.nd == 2 and self.nh == 4 and self.NI == 4 and self.LW == 3 * HD
        assert (self.NI - 1) * self.WIN + self.IP <= rows and (self.NI - 1) * self.LAG + SEQ <= self.IP
        assert self.ne & (self.ne - 1) == 0
        assert self.ne <= 64 and 0 <= self.CAP - (self.CP - 16) <= 14


class Place:
    def __init__(self, g):
        self.ne = g.ne
        self.d = lax.axis_index("dp")
        self.e = lax.axis_index("expert")
        self.h = lax.axis_index("head")
        self.y = lax.div(self.h, 2)
        self.c = lax.rem(self.h, 2)
        self.oy, self.oc, self.od = 1 - self.y, 1 - self.c, 1 - self.d
        self.hcore = 2 * self.y + self.oc
        self.hy = 2 * self.oy + self.c
        self.hdiag = 2 * self.oy + self.oc
        self.core = (self.d, self.e, self.hcore)
        self.across = (self.d, self.e, self.hy)
        self.diag = (self.d, self.e, self.hdiag)
        self.twin = (self.od, self.e, self.h)

    def other(self, k):
        index, bit = 0, 1
        while bit < self.ne:
            index = index + lax.rem(lax.div(self.e, bit) + k // bit, 2) * bit
            bit *= 2
        return index

    def along(self, e2):
        return (self.d, e2, self.h)

    def enter(self, wide=False):
        barrier = pltpu.get_barrier_semaphore()

        def tell(device):
            pl.semaphore_signal(barrier, inc=1, device_id=device, device_id_type=MESH)

        for device in (self.core, self.across, self.diag, self.twin):
            tell(device)
        loop(self.ne - 1, lambda k: tell(self.along(self.other(k + 1))))
        if wide:
            loop(self.ne - 1, lambda k: tell((self.od, self.other(k + 1), self.h)))
        pl.semaphore_wait(barrier, 4 + (self.ne - 1) * (2 if wide else 1))


def copy(b, name, src, dst, si, ri, device):
    return pltpu.make_async_remote_copy(
        src_ref=src,
        dst_ref=dst,
        send_sem=getattr(b, name + "_s").at[si],
        recv_sem=getattr(b, name + "_r").at[ri],
        device_id=device,
        device_id_type=MESH,
    )


def send(b, name, src, dst, si, ri, device):
    copy(b, name, src, dst, si, ri, device).start()


def arrived(b, p, name, ref, ri):
    copy(b, name, ref, ref, 0, ri, p.core).wait_recv()


def left(b, p, name, ref, si):
    copy(b, name, ref, ref, si, 0, p.core).wait_send()


def fetch(b, name, src, dst, i=0):
    pltpu.make_async_copy(src, dst, getattr(b, name + "_s").at[i]).start()


def fetched(b, name, src, dst, i=0):
    pltpu.make_async_copy(src, dst, getattr(b, name + "_s").at[i]).wait()


def stow(b, *names):
    for name in names:
        fetch(b, "k" + name, getattr(b, name), getattr(b, "h" + name))


def stowed(b, *names):
    for name in names:
        fetched(b, "k" + name, getattr(b, name), getattr(b, "h" + name))


def load(b, *names):
    for name in names:
        fetch(b, "k" + name, getattr(b, "h" + name), getattr(b, name))


def loaded(b, *names):
    for name in names:
        fetched(b, "k" + name, getattr(b, "h" + name), getattr(b, name))


def shift(g, image, back=False):
    row, col = iota((g.IP, g.IP), 0), iota((g.IP, g.IP), 1)
    if back:
        hot = (row == col + g.LAG * image) & (col < SEQ)
    else:
        hot = (col == row + g.LAG * image) & (row < SEQ)
    return jnp.where(hot, 1.0, 0.0).astype(BF16)


def window(g, image):
    return pl.ds(pl.multiple_of(image * g.WIN, 16), g.IP)


def rows_out(g, p, b):
    for j in range(2):
        rows = slice(j * g.IP, (j + 1) * g.IP)
        fetch(b, "ldx", b.xin.at[p.y, window(g, 2 * p.c + j), :], b.X.at[rows, :], j)
        fetch(b, "ldu", b.uin.at[p.y, window(g, 2 * p.c + j), :], b.UPO.at[rows, :], j)
    fetch(b, "ldb", b.uin.at[p.c, :, half_of(g, p.y)], b.UB)


def rows_in(g, p, b):
    for j in range(2):
        rows = slice(j * g.IP, (j + 1) * g.IP)
        fetched(b, "ldx", b.xin.at[p.y, window(g, 2 * p.c + j), :], b.X.at[rows, :], j)
        fetched(b, "ldu", b.uin.at[p.y, window(g, 2 * p.c + j), :], b.UPO.at[rows, :], j)
        hot = shift(g, 2 * p.c + j)
        b.X[rows, :] = nn(hot, b.X[rows, :]).astype(BF16)
        b.UPO[rows, :] = nn(hot, b.UPO[rows, :]).astype(BF16)
    fetched(b, "ldb", b.uin.at[p.c, :, half_of(g, p.y)], b.UB)
    for i in range(g.NI):
        b.UPP[i * g.IP : (i + 1) * g.IP, :] = nn(
            shift(g, i), b.UB[i * g.WIN : i * g.WIN + g.IP, :]
        ).astype(BF16)


def route(g, b, c, both):
    pr_row, e0r, e1r = b.mr[c, 2:3, :], b.mr[c, 0:1, :], b.mr[c, 1:2, :]
    lane = fiota((g.IP, 128), 1)
    base = jnp.zeros((1, 128), F32)
    for i in range(g.NI):
        rows = slice(i * g.IP, (i + 1) * g.IP)
        col = b.mc[c, rows, :]
        e0c, e1c, prc = col[:, 0:1], col[:, 1:2], col[:, 2:3]
        b.L[rows, :] = jnp.where(pr_row < prc, 1.0, 0.0).astype(BF16)
        b.O[rows, :] = jnp.where((lane == e0c) | (lane == e1c + 64.0), 1.0, 0.0).astype(BF16)
        base = base + jnp.sum(jnp.where(lane == e0c + 64.0, 1.0, 0.0), axis=0, keepdims=True)
    slot_lane = fiota((g.IP, g.SL), 1)
    for i in range(g.NI if both else 0):
        rows = slice(i * g.IP, (i + 1) * g.IP)
        col = b.mc[c, rows, :]
        e0c, e1c = col[:, 0:1], col[:, 1:2]
        own = b.O[rows, :].astype(F32)
        earlier = nn(b.L[rows, :], b.O[...])
        s0 = jnp.sum(jnp.where(lane < 64.0, earlier * own, 0.0), axis=1, keepdims=True)
        s1 = jnp.sum(jnp.where(lane < 64.0, 0.0, (earlier + base) * own), axis=1, keepdims=True)
        t0 = jnp.where(s0 < g.CAP, e0c * g.CP + s0, -1.0)
        t1 = jnp.where(s1 < g.CAP, e1c * g.CP + s1, -1.0)
        b.PT[rows, :] = jnp.where((slot_lane == t0) | (slot_lane == t1), 1.0, 0.0).astype(BF16)
    sub = fiota((128, g.TP), 0)
    own = jnp.where((sub == e0r) | (sub == e1r + 64.0), 1.0, 0.0)
    base = jnp.sum(jnp.where(sub == e0r + 64.0, 1.0, 0.0), axis=1, keepdims=True)
    earlier = nt(own.astype(BF16), b.L[...])
    s0 = jnp.sum(jnp.where(sub < 64.0, earlier * own, 0.0), axis=0, keepdims=True)
    s1 = jnp.sum(jnp.where(sub < 64.0, 0.0, (earlier + base) * own), axis=0, keepdims=True)
    t0 = jnp.where(s0 < g.CAP, e0r * g.CP + s0, -1.0)
    t1 = jnp.where(s1 < g.CAP, e1r * g.CP + s1, -1.0)
    slot_sub = fiota((g.CP, g.TP), 0)

    def fill(e2):
        at = slot_sub + (e2 * g.CP).astype(F32)
        b.P[pl.ds(pl.multiple_of(e2 * g.CP, 16), g.CP), :] = jnp.where(
            (at == t0) | (at == t1), 1.0, 0.0
        ).astype(BF16)

    loop(g.ne, fill)


def pack_rows(g, e2):
    return pl.ds(pl.multiple_of(e2 * g.CP, 16), g.CP)


def piece_rows(g, d, e2):
    return pl.ds(pl.multiple_of((d * g.ne + e2) * g.PR, 16), g.PR)


def weights_out(g, p, b):
    own = piece_rows(g, p.d, p.e)
    if g.aligned:
        mine = p.d * g.ne + p.e

        def to_expert(k):
            device = p.along(p.other(k + 1))
            send(b, "wz", b.wp, b.W.at[p.h, own, :], k, p.e, device)
            send(b, "mz", b.mp, b.MI.at[own, :], k, p.e, device)

        loop(g.ne - 1, to_expert)
        send(b, "wx", b.wp, b.W.at[p.h, own, :], p.e, p.e, p.twin)
        send(b, "mx", b.mp, b.MI.at[own, :], p.e, p.e, p.twin)
        send(b, "wy", b.wp, b.W.at[p.h, own, :], mine, mine, p.across)
        send(b, "wc", b.wp, b.W.at[p.h, own, :], mine, mine, p.core)
        b.W[p.h, own, :] = b.wp[...]
        b.MI[own, :] = b.mp[...]
    else:
        send(b, "wy", b.wp, b.W.at[p.h], 0, 0, p.across)
        send(b, "wc", b.wp, b.W.at[p.h], 0, 0, p.core)
        b.W[p.h] = b.wp[...]
        b.MI[...] = b.mp[...]


def weights_on(g, p, b):
    if not g.aligned:
        return

    def relay(k):
        e2 = p.other(k + 1)
        rows = piece_rows(g, p.d, e2)
        at = p.d * g.ne + e2
        part = b.W.at[p.h, rows, :]
        arrived(b, p, "wz", part, e2)
        send(b, "wx", part, part, e2, e2, p.twin)
        send(b, "wy", part, part, at, at, p.across)
        send(b, "wc", part, part, at, at, p.core)
        part = b.MI.at[rows, :]
        arrived(b, p, "mz", part, e2)
        send(b, "mx", part, part, e2, e2, p.twin)

    loop(g.ne - 1, relay)


def odd(e2):
    return lax.rem(e2, 2) == 1


def weights_end(g, p, b):
    if not g.aligned:
        return

    def relay(k):
        e2 = p.other(k)
        rows = piece_rows(g, p.od, e2)
        at = p.od * g.ne + e2
        part = b.W.at[p.h, rows, :]
        arrived(b, p, "wx", part, e2)

        @pl.when(jnp.logical_not(odd(e2)))
        def _():
            send(b, "wy", part, part, at, at, p.across)

        send(b, "wc", part, part, at, at, p.core)
        arrived(b, p, "mx", b.MI.at[rows, :], e2)

    loop(g.ne, relay)

    def over(k):
        e2 = p.other(k)
        at = p.d * g.ne + e2
        part = b.W.at[p.hy, piece_rows(g, p.d, e2), :]
        arrived(b, p, "wy", part, at)

        @pl.when(odd(e2))
        def _():
            send(b, "wv", part, part, e2, e2, p.twin)

        send(b, "wd", part, part, at, at, p.core)

    loop(g.ne, over)


def pieces(g):
    return g.nd * g.ne if g.aligned else 1


def piece_of(g, ref, group, i):
    if not g.aligned:
        return ref.at[group]
    return ref.at[group, pl.ds(pl.multiple_of(i * g.PR, 16), g.PR), :]


def group_in(g, p, b, k):
    @pl.when(k == 1)
    def _():
        loop(pieces(g), lambda i: arrived(b, p, "wc", piece_of(g, b.W, p.hcore, i), i))

    @pl.when(k == 2)
    def _():
        if not g.aligned:
            arrived(b, p, "wy", b.W.at[p.hy], 0)
            send(b, "wd", b.W.at[p.hy], b.W.at[p.hy], 0, 0, p.core)
            return

        def on(i):
            e2 = p.other(i)
            at = p.od * g.ne + e2
            part = b.W.at[p.hy, piece_rows(g, p.od, e2), :]

            @pl.when(jnp.logical_not(odd(e2)))
            def _():
                arrived(b, p, "wy", part, at)

            @pl.when(odd(e2))
            def _():
                arrived(b, p, "wv", part, e2)

            send(b, "wd", part, part, at, at, p.core)

        loop(g.ne, on)

    @pl.when(k == 3)
    def _():
        loop(pieces(g), lambda i: arrived(b, p, "wd", piece_of(g, b.W, p.hdiag, i), i))


def masks(rows):
    lane = iota((rows, 128), 1)
    return lane < 64, lane >= 64


def attention(g, p, b):
    low, high = masks(g.IP)
    live = iota((g.IP, g.IP), 1) < SEQ
    zero = jnp.zeros((g.IP, 128), BF16)

    def group(k):
        group_in(g, p, b, k)

        @pl.when(k == 3)
        def _():
            part = b.US.at[p.e, p.c, p.y]
            send(b, "uy", part, part, p.e, p.e, p.across)
            send(b, "uc", part, part, p.e, p.e, p.core)
            loop(g.ne - 1, lambda i: cotangent_on(g, p, b, p.other(i + 1)))

        gi = 2 * lax.rem(p.y + lax.div(k, 2), 2) + lax.rem(p.c + k, 2)
        for blk in range(2):
            rows = slice(blk * g.IP, (blk + 1) * g.IP)
            b.QKV[gi, rows, :] = nn(b.ACT1[rows, :], b.W[gi, :, 0:640]).astype(BF16)
        for blk in range(2):
            rows = slice(blk * g.IP, (blk + 1) * g.IP)
            outs = []
            for j in range(3):
                qt = b.QKV[gi, rows, (j // 2) * 128 : (j // 2) * 128 + 128]
                kt = b.QKV[gi, rows, 384 + (j // 2) * 128 : 384 + (j // 2) * 128 + 128]
                vt = b.QKV[gi, rows, 128 + ((j + 1) // 2) * 128 : 256 + ((j + 1) // 2) * 128]
                scores = nt(jnp.where(high if j == 1 else low, qt, zero), kt) * (HD**-0.5)
                scores = jnp.where(live, scores, -1e30)
                scores = jnp.exp(scores - jnp.max(scores, axis=1, keepdims=True))
                probs = (scores / jnp.sum(scores, axis=1, keepdims=True)).astype(BF16)
                b.PB[gi, blk * 3 + j] = probs
                outs.append(nn(probs, vt))
            b.ATT[gi, rows, 0:128] = jnp.where(high, outs[0], 0.0).astype(BF16)
            b.ATT[gi, rows, 128:256] = jnp.where(low, outs[1], outs[2]).astype(BF16)
        for blk in range(2):
            rows = slice(blk * g.IP, (blk + 1) * g.IP)
            b.HID[rows, :] += nt(b.ATT[gi, rows, :], b.W[gi, :, 512:768])

    loop(4, group)


def rows16s(count, body):
    run = count // 32

    def step(i):
        for j in range(run):
            body(pl.ds(pl.multiple_of((i * run + j) * 16, 16), 16))

    loop(2, step)


def first_norm(g, b):
    def rows16(rows):
        x = b.X[rows, :].astype(F32)
        normed, _ = normalize(x)
        b.ACT1[rows, :] = (normed * b.GN[0:1, :]).astype(BF16)
        b.HID[rows, :] = x

    rows16s(2 * g.IP, rows16)


def second_norm(g, b):
    def rows16(rows):
        normed, _ = normalize(b.HID[rows, :])
        b.ACT2[rows, :] = (normed * b.GN[1:2, :]).astype(BF16)

    rows16s(2 * g.IP, rows16)
    lane = iota((g.IP, 128), 1)
    for blk in range(2):
        rows = slice(blk * g.IP, (blk + 1) * g.IP)
        logits = jnp.where(lane < g.ne, nn(b.ACT2[rows, :], b.RW[...]), -1e30)
        weight = jnp.exp(logits - jnp.max(logits, axis=1, keepdims=True))
        probs = weight / jnp.sum(weight, axis=1, keepdims=True)
        b.PRB[rows, :] = probs
        top = probs.astype(BF16).astype(F32)
        rest = probs - top
        b.PRH[rows, :] = (top + pltpu.roll(rest, 64, 1)).astype(BF16)


def small_weights(g, b):
    lane = iota((g.D, 128), 1)
    small = b.MI[...].astype(F32)
    b.RW[...] = jnp.where(lane < g.ne, small, 0.0).astype(BF16)
    gains = jnp.transpose(small)[120:128, :]
    b.GN[0:1, :] = gains[0:1, :] + gains[1:2, :]
    b.GN[1:2, :] = gains[2:3, :] + gains[3:4, :]


def half_of(g, i):
    return pl.ds(pl.multiple_of(i * g.DH, 128), g.DH)


def own_rows(g, c):
    return pl.ds(pl.multiple_of(c * 2 * g.IP, 16), 2 * g.IP)


def tokens_out(g, p, b):
    rows = own_rows(g, p.c)
    send(b, "ta", b.ACT2.at[:, half_of(g, p.oc)], b.TA.at[rows, :], 0, 0, p.core)
    send(b, "tp", b.PRH, b.TG.at[rows, :], 0, 0, p.core)
    b.TA[rows, :] = b.ACT2[:, half_of(g, p.c)]
    b.TG[rows, :] = b.PRH[...]


def tokens_in(g, p, b):
    arrived(b, p, "ta", b.TA.at[own_rows(g, p.oc), :], 0)
    arrived(b, p, "tp", b.TG.at[own_rows(g, p.oc), :], 0)


def cotangent_out(g, p, b):
    def pack(k):
        e2 = p.other(k)
        rows = nn(b.P[pack_rows(g, e2), :], b.UPP[...]).astype(BF16)

        @pl.when(k > 0)
        def _():
            b.PKU[e2] = rows
            send(b, "uz", b.PKU.at[e2], b.US.at[p.e, p.c, p.y], k, p.e, p.along(e2))

        @pl.when(k == 0)
        def _():
            b.US[p.e, p.c, p.y] = rows

    loop(g.ne, pack)


def cotangent_on(g, p, b, e2):
    part = b.US.at[e2, p.c, p.y]
    arrived(b, p, "uz", part, e2)
    send(b, "uy", part, part, e2, e2, p.across)
    send(b, "uc", part, part, e2, e2, p.core)


def cotangent_over(g, p, b, e2):
    part = b.US.at[e2, p.c, p.oy]
    arrived(b, p, "uy", part, e2)
    send(b, "ud", part, part, e2, e2, p.core)


def slots_out(g, p, b):
    row = iota((g.CP, g.DH), 0)
    eye = row == iota((g.CP, g.DH), 1)
    lane = iota((g.CP, 128), 1)

    def pack(k):
        e2 = p.other(k)
        hot = b.P[pack_rows(g, e2), :]
        tok = nn(hot, b.TA[...])
        gates = nn(hot, b.TG[...])
        gate = jnp.sum(
            jnp.where((lane == e2) | (lane == e2 + 64), gates, 0.0), axis=1, keepdims=True
        )
        b.GC[e2] = jnp.broadcast_to(gate, (g.CP, 128))
        across = jnp.sum(jnp.where(eye, gate, 0.0), axis=0, keepdims=True)
        top = across.astype(BF16).astype(F32)
        rows = jnp.where(row == g.CAP, top, jnp.where(row == g.CAP + 1, across - top, tok))
        rows = rows.astype(BF16)

        @pl.when(k > 0)
        def _():
            b.PKA[e2] = rows
            send(b, "xz", b.PKA.at[e2], b.XS.at[p.e, p.y, p.c], k, p.e, p.along(e2))

        @pl.when(k == 0)
        def _():
            part = b.XS.at[p.e, p.y, p.c]
            b.XS[p.e, p.y, p.c] = rows
            send(b, "xy", part, part, p.e, p.e, p.across)
            send(b, "xc", part, part, p.e, p.e, p.core)

    loop(g.ne, pack)


def slots_on(g, p, b, e2):
    part = b.XS.at[e2, p.y, p.c]
    arrived(b, p, "xz", part, e2)
    send(b, "xy", part, part, e2, e2, p.across)
    send(b, "xc", part, part, e2, e2, p.core)


def slots_over(g, p, b, e2):
    part = b.XS.at[e2, p.oy, p.c]
    arrived(b, p, "xy", part, e2)
    send(b, "xd", part, part, e2, e2, p.core)


def slots_in(g, p, b, e2):
    arrived(b, p, "xc", b.XS.at[e2, p.y, p.oc], e2)
    arrived(b, p, "xd", b.XS.at[e2, p.oy, p.oc], e2)
    arrived(b, p, "uc", b.US.at[e2, p.oc, p.y], e2)
    arrived(b, p, "ud", b.US.at[e2, p.oc, p.oy], e2)


CHUNKS = 4


def chunk(rows, i):
    size = rows // CHUNKS
    return pl.ds(i * size, size)


def experts_out(g, p, b, which):
    for i in which:
        name, src, dst = ("ei", b.wi, b.WI) if i < CHUNKS else ("eb", b.wb, b.WB)
        rows = chunk(src.shape[0], i % CHUNKS)
        send(b, name, src.at[rows, :], dst.at[p.d, rows, :], i % CHUNKS, i % CHUNKS, p.twin)


def experts_in(g, p, b):
    for i in range(CHUNKS):
        arrived(b, p, "ei", b.WI.at[p.od, chunk(g.DH, i), :], i)
    for i in range(CHUNKS):
        arrived(b, p, "eb", b.WB.at[p.od, chunk(g.F, i), :], i)


def back_core(g, p, b, part, s):
    send(b, "rc", part.at[s, :, p.oc], b.RC.at[s], s, s, p.core)


def back_over(g, p, b, part, s):
    arrived(b, p, "rc", b.RC.at[s], s)
    b.RC[s, p.oy] = (part[s, p.oy, p.c].astype(F32) + b.RC[s, p.oy].astype(F32)).astype(BF16)
    send(b, "ry", b.RC.at[s, p.oy], b.RY.at[s], s, s, p.across)


def back_on(g, p, b, part, s):
    arrived(b, p, "ry", b.RY.at[s], s)
    total = (
        part[s, p.y, p.c].astype(F32) + b.RC[s, p.y].astype(F32) + b.RY[s].astype(F32)
    ).astype(BF16)

    @pl.when(s != p.e)
    def _():
        b.RC[s, p.y] = total
        send(b, "rz", b.RC.at[s, p.y], b.RO.at[p.e], s, p.e, p.along(s))

    @pl.when(s == p.e)
    def _():
        b.RO[p.e] = total


def back_in(g, p, b):
    def rows_of(k):
        s = p.other(k + 1)
        arrived(b, p, "rz", b.RO.at[s], s)

    loop(g.ne - 1, rows_of)


def back_end(g, p, b):
    def rets(s):
        left(b, p, "rc", b.RC.at[0], s)
        left(b, p, "ry", b.RY.at[0], s)

    loop(g.ne, rets)
    loop(g.ne - 1, lambda k: left(b, p, "rz", b.RY.at[0], p.other(k + 1)))


def gelu_parts(u):
    inner = 0.7978845608028654 * (u + 0.044715 * u * u * u)
    tangent = jnp.tanh(inner)
    value = 0.5 * u * (1.0 + tangent)
    slope = 0.5 * (1.0 + tangent) + 0.5 * u * (1.0 - tangent * tangent) * 0.7978845608028654 * (
        1.0 + 3.0 * 0.044715 * u * u
    )
    return value, slope


def expert(g, b, first, between=None):
    base = g.CP - 16
    row = iota((g.CP, g.DH), 0)
    eye = row == iota((g.CP, g.DH), 1)
    for i in range(g.SG):
        for blk in range(2):
            tail = b.XS[first + i, blk, 0, base:, :].astype(F32)
            gate = tail[g.CAP - base : g.CAP - base + 1] + tail[g.CAP - base + 1 : g.CAP - base + 2]
            gate = jnp.sum(jnp.where(eye, gate, 0.0), axis=1, keepdims=True)
            at = (i * 2 + blk) * g.CP
            for q in range(2):
                b.GP[at : at + g.CP, q * g.DH : (q + 1) * g.DH] = (
                    b.US[first + i, blk, q].astype(F32) * gate
                ).astype(BF16)
    x = [b.XS[pl.ds(first, g.SG), :, q].reshape(g.R, g.DH) for q in range(2)]
    for n in range(g.F // 256):
        cols = slice(n * 256, n * 256 + 256)
        pre = nn(x[0], b.WI[0, :, cols]) + nn(x[1], b.WI[1, :, cols])
        value, slope = gelu_parts(pre)
        b.HQ[:, cols] = value.astype(BF16)
        grad = nt(b.GP[:, : g.DH], b.WB[0, cols, :]) + nt(b.GP[:, g.DH :], b.WB[1, cols, :])
        b.GR[:, cols] = (grad * slope).astype(BF16)
    shape = (g.SG, 2, g.CP, g.DH)
    dots = []
    for q in range(2):
        out = nn(b.HQ[...], b.WB[q]).astype(BF16)
        b.PO[pl.ds(first, g.SG), :, q] = out.reshape(shape)
        up = b.US[pl.ds(first, g.SG), :, q].reshape(g.R, g.DH)
        dots.append(jnp.sum(out.astype(F32) * up.astype(F32), axis=1, keepdims=True))
    dots = dots[0] + dots[1]
    for q in range(2):
        back = nt(b.GR[...], b.WI[q])
        for i in range(g.SG):
            for blk in range(2):
                at = (i * 2 + blk) * g.CP
                along = jnp.sum(jnp.where(eye, dots[at : at + g.CP], 0.0), axis=0, keepdims=True)
                if q == 1:
                    along = along - along.astype(BF16).astype(F32)
                b.PG[first + i, blk, q] = jnp.where(
                    row == g.CAP, along, back[at : at + g.CP]
                ).astype(BF16)
    if between is not None:
        between(0)
    for q in range(2):
        b.DB[q] += tn(b.HQ[...], b.GP[:, q * g.DH : (q + 1) * g.DH])
    if between is not None:
        between(1)
    for q in range(2):
        b.DI[q] += tn(x[q], b.GR[...])


def experts(g, p, b):
    b.DB[...] = jnp.zeros_like(b.DB)
    b.DI[...] = jnp.zeros_like(b.DI)
    n = g.ne
    if g.SG > 1:
        loop(n, lambda k: cotangent_over(g, p, b, p.other(k)))
        loop(n - 1, lambda k: slots_on(g, p, b, p.other(k + 1)))
        loop(n, lambda k: slots_over(g, p, b, p.other(k)))
        loop(n, lambda k: slots_in(g, p, b, p.other(k)))
        experts_in(g, p, b)
        loop(n // g.SG, lambda t: expert(g, b, t * g.SG))
        loop(n, lambda k: back_core(g, p, b, b.PG, p.other(k)))
        loop(n, lambda k: back_over(g, p, b, b.PG, p.other(k)))
        loop(n - 1, lambda k: back_on(g, p, b, b.PG, p.other(k)))
        return
    loop(n, lambda k: cotangent_over(g, p, b, p.other(k)))
    slots_over(g, p, b, p.e)
    slots_in(g, p, b, p.e)
    loop(n - 1, lambda k: slots_on(g, p, b, p.other(k + 1)))
    experts_in(g, p, b)

    def source(k):
        @pl.when(k > 0)
        def _():
            slots_over(g, p, b, p.other(k))
            slots_in(g, p, b, p.other(k))

        def between(step):
            if step == 0:
                back_core(g, p, b, b.PG, p.other(k))

                @pl.when(k > 0)
                def _():
                    back_on(g, p, b, b.PG, p.other(k - 1))
            else:
                back_over(g, p, b, b.PG, p.other(k))

        expert(g, b, p.other(k), between)

    loop(n, source)


def first_sends_end(g, p, b):
    n = g.ne
    if g.aligned:
        own = piece_rows(g, p.d, p.e)

        def z(k):
            left(b, p, "wz", b.wp, k)
            left(b, p, "mz", b.mp, k)

        loop(n - 1, z)

        def x(k):
            left(b, p, "wx", b.wp, k)
            left(b, p, "mx", b.mp, k)

        loop(n, x)

    def w(i):
        for name in ("wc", "wd"):
            left(b, p, name, piece_of(g, b.W, p.h, i), i)

    loop(pieces(g), w)
    if g.aligned:

        def across(e2):
            part = piece_of(g, b.W, p.h, 0)
            left(b, p, "wy", part, p.d * n + e2)

            @pl.when(jnp.logical_not(odd(e2)))
            def _():
                left(b, p, "wy", part, p.od * n + e2)

            @pl.when(odd(e2))
            def _():
                left(b, p, "wv", part, e2)

        loop(n, across)
    else:
        left(b, p, "wy", b.W.at[0], 0)
    left(b, p, "ta", b.TA.at[own_rows(g, 0), :], 0)
    left(b, p, "tp", b.TG.at[own_rows(g, 0), :], 0)

    def slots(k):
        left(b, p, "uz", b.PKU.at[0], k + 1)
        left(b, p, "xz", b.PKA.at[0], k + 1)

    loop(n - 1, slots)

    def on(k):
        for name in ("uy", "uc", "ud"):
            left(b, p, name, b.US.at[0, 0, 0], k)
        for name in ("xy", "xc", "xd"):
            left(b, p, name, b.XS.at[0, 0, 0], k)

    loop(n, on)
    for i in range(CHUNKS):
        left(b, p, "ei", b.wi.at[chunk(g.DH, 0), :], i)
        left(b, p, "eb", b.wb.at[chunk(g.F, 0), :], i)


KEEP = ("X", "UPO", "W", "RW", "GN", "QKV", "PB", "ATT", "HID", "PRB", "PT", "GC", "PO", "RO", "KI", "KB", "SI", "SB")


def first_kernel(g, b):
    p = Place(g)
    rows_out(g, p, b)
    p.enter()
    weights_out(g, p, b)
    experts_out(g, p, b, range(2))
    b.WI[p.d] = b.wi[...]
    b.WB[p.d] = b.wb[...]
    rows_in(g, p, b)
    route(g, b, p.c, False)
    weights_on(g, p, b)
    cotangent_out(g, p, b)
    weights_end(g, p, b)
    experts_out(g, p, b, range(2, 2 * CHUNKS))
    route(g, b, p.y, True)
    small_weights(g, b)
    first_norm(g, b)
    stow(b, "X", "UPO", "RW", "GN", "PT")
    attention(g, p, b)
    stow(b, "W", "QKV", "PB", "ATT", "HID")
    second_norm(g, b)
    stow(b, "PRB")
    tokens_out(g, p, b)
    tokens_in(g, p, b)
    slots_out(g, p, b)
    stow(b, "GC")
    experts(g, p, b)
    stow(b, "PO")
    b.KI[...] = b.DI[p.d]
    b.KB[...] = b.DB[p.d]
    b.SI[...] = b.DI[p.od].astype(BF16)
    b.SB[...] = b.DB[p.od].astype(BF16)
    stow(b, "KI", "KB", "SI", "SB")
    back_on(g, p, b, b.PG, p.other(g.ne - 1))
    back_in(g, p, b)
    stow(b, "RO")
    first_sends_end(g, p, b)
    back_end(g, p, b)
    stowed(b, *KEEP)


def grads_of_expert_out(g, p, b):
    send(b, "gi", b.hSI, b.XI, 0, 0, p.twin)


def grads_of_expert_in(g, p, b):
    loaded(b, "KI", "KB")
    arrived(b, p, "gi", b.XI, 0)
    b.o_gi[...] = b.KI[...] + b.XI[...].astype(F32)
    arrived(b, p, "gb", b.XB, 0)
    b.o_gb[...] = b.KB[...] + b.XB[...].astype(F32)


def slots_back(g, p, b, kind):
    lane = iota((g.CP, 128), 1)
    base = g.CP - 16
    eye = iota((g.CP, g.DH), 0) == iota((g.CP, g.DH), 1)

    def rows_of(s):
        rows = pack_rows(g, s)
        if kind:
            b.RG[rows, 0 : g.DH] = b.RB[s]
            dots = b.RB[s, base:, :].astype(F32)[g.CAP - base : g.CAP - base + 1]
            dots = jnp.sum(jnp.where(eye, dots, 0.0), axis=1, keepdims=True)
            b.RG[rows, g.DH :] = jnp.where(lane == s, dots, 0.0).astype(BF16)
        else:
            b.RG[rows, 0 : g.DH] = (b.RO[s].astype(F32) * b.GC[s][:, 0:1]).astype(BF16)

    loop(g.ne, rows_of)


def unpack(g, p, b, kind):
    name, width = ("ug", g.DH + 128) if kind else ("uo", g.DH)
    out, landed = (b.UG, b.TR) if kind else (b.UO, b.TO)

    def rows(c, j):
        image = pl.ds(pl.multiple_of((2 * c + j) * g.IP, 16), g.IP)
        return nn(b.PT[image, :], b.RG[:, 0:width]).astype(BF16)

    for j in range(2):
        here = slice(j * g.IP, (j + 1) * g.IP)
        out[here, :] = rows(p.oc, j)
        send(b, name, out.at[here, :], landed.at[p.c, here, :], j, j, p.core)
    for j in range(2):
        landed[p.c, j * g.IP : (j + 1) * g.IP, :] = rows(p.c, j)


def unpacked(g, p, b, kind):
    name, landed = ("ug", b.TR) if kind else ("uo", b.TO)
    for j in range(2):
        arrived(b, p, name, landed.at[p.oc, j * g.IP : (j + 1) * g.IP, :], j)


def mix(g, p, b):
    def rows16(rows):
        for q in range(2):
            cols = slice(q * g.DH, (q + 1) * g.DH)
            b.MX[rows, cols] = (b.HID[rows, cols] + b.TO[q, rows, :].astype(F32)).astype(BF16)

    rows16s(2 * g.IP, rows16)
    for j in range(2):
        part = b.MX.at[j * g.IP : (j + 1) * g.IP, :]
        here = (p.c == p.y) & (p.c == j)

        @pl.when(here)
        def _(j=j):
            b.MIX[p.y] = b.MX[j * g.IP : (j + 1) * g.IP, :]

        @pl.when(jnp.logical_not(here))
        def _(j=j, part=part):
            send(b, "mo", part, b.MIX.at[p.y], j, p.y, (p.d, p.e, 2 * p.c + j))


def mixed_in(g, p, b):
    for blk in range(2):

        @pl.when(jnp.logical_not((p.y == blk) & (p.c == p.y)))
        def _(blk=blk):
            arrived(b, p, "mo", b.MIX.at[blk], blk)

        b.o_mixed[blk] = b.MIX[blk, 0:SEQ, :]
    for j in range(2):

        @pl.when(jnp.logical_not((p.c == p.y) & (p.c == j)))
        def _(j=j):
            left(b, p, "mo", b.MIX.at[0], j)


def tokens_back(g, p, b):
    lane = iota((g.IP, 128), 1)
    b.GA[...] = jnp.zeros_like(b.GA)
    for blk in range(2):
        rows = slice(blk * g.IP, (blk + 1) * g.IP)
        gate = b.TR[0, rows, g.DH :].astype(F32) + b.TR[1, rows, g.DH :].astype(F32)
        probs = b.PRB[rows, :]
        grad = probs * (gate - jnp.sum(probs * gate, axis=1, keepdims=True))
        b.GL[rows, :] = grad.astype(BF16)
        b.GHID[rows, :] = nt(b.GL[rows, :], b.RW[...])

    def rows16(rows):
        normed, inverse = normalize(b.HID[rows, :])
        upstream = b.GHID[rows, :] + jnp.concatenate(
            [b.TR[q, rows, 0 : g.DH].astype(F32) for q in range(2)], axis=1
        )
        prod = upstream * normed
        b.GA[8:16, :] += prod[0:8, :] + prod[8:16, :]
        b.ACT2[rows, :] = (normed * b.GN[1:2, :]).astype(BF16)
        hidden = b.UPO[rows, :].astype(F32) + norm_backward(upstream, normed, inverse, b.GN[1:2, :])
        b.GHID[rows, :] = hidden
        b.GHL[rows, :] = hidden.astype(BF16)

    rows16s(2 * g.IP, rows16)


def first_norm_again(g, b):
    def rows16(rows):
        normed, _ = normalize(b.X[rows, :].astype(F32))
        b.ACT1[rows, :] = (normed * b.GN[0:1, :]).astype(BF16)

    rows16s(2 * g.IP, rows16)


def attention_back(g, p, b):
    low, high = masks(g.IP)
    zero = jnp.zeros((g.IP, 128), BF16)
    scale = HD**-0.5
    b.DA[...] = jnp.zeros_like(b.DA)

    def group(k):
        @pl.when(k == 2)
        def _():
            loop(g.ne // 2, lambda i: back_on(g, p, b, b.PO, p.other(i + 1)))

        @pl.when(k == 3)
        def _():
            loop(g.ne - g.ne // 2, lambda i: back_on(g, p, b, b.PO, p.other(i + g.ne // 2 + 1)))
            weights_back(g, p, b, 0, 1)

        yk = lax.rem(p.oy + lax.div(k, 2), 2)
        gi = 2 * yk + lax.rem(p.oc + k, 2)
        for blk in range(2):
            rows = slice(blk * g.IP, (blk + 1) * g.IP)
            grad = nn(b.GHL[rows, :], b.W[gi, :, 512:768]).astype(BF16)
            tiles = [grad[:, 0:128], grad[:, 128:256]]
            dq, dk, dv = [], [], []
            for j in range(3):
                probs = b.PB[gi, blk * 3 + j]
                gt = tiles[(j + 1) // 2]
                qt = b.QKV[gi, rows, (j // 2) * 128 : (j // 2) * 128 + 128]
                kt = b.QKV[gi, rows, 384 + (j // 2) * 128 : 384 + (j // 2) * 128 + 128]
                vt = b.QKV[gi, rows, 128 + ((j + 1) // 2) * 128 : 256 + ((j + 1) // 2) * 128]
                grad_probs = nt(jnp.where(low if j == 1 else high, gt, zero), vt)
                wide = probs.astype(F32)
                grad_scores = wide * (
                    grad_probs - jnp.sum(wide * grad_probs, axis=1, keepdims=True)
                )
                grad_scores = (grad_scores * scale).astype(BF16)
                dv.append(tn(probs, gt))
                dq.append(nn(grad_scores, kt))
                dk.append(tn(grad_scores, qt))
            b.GJ[rows, 0:128] = jnp.where(low, dq[0], dq[1]).astype(BF16)
            b.GJ[rows, 128:256] = jnp.where(low, dq[2], dv[0]).astype(BF16)
            b.GJ[rows, 256:384] = jnp.where(low, dv[1], dv[2]).astype(BF16)
            b.GJ[rows, 384:512] = jnp.where(low, dk[0], dk[1]).astype(BF16)
            b.GJ[rows, 512:640] = jnp.where(low, dk[2], 0.0).astype(BF16)
        for blk in range(2):
            rows = slice(blk * g.IP, (blk + 1) * g.IP)
            b.DA[rows, :] += nt(b.GJ[rows, :], b.W[gi, :, 0:640])
        for m in range(g.D // 256):
            cols = slice(m * 256, m * 256 + 256)
            first = tn(b.ACT1[:, cols], b.GJ[...])
            second = tn(b.GHL[:, cols], b.ATT[gi])
            b.DW[gi, cols, 0:512] = first[:, 0:512].astype(BF16)
            b.DW[gi, cols, 512:640] = (first[:, 512:] + second[:, 0:128]).astype(BF16)
            b.DW[gi, cols, 640:768] = second[:, 128:].astype(BF16)

        @pl.when(lax.rem(k, 2) == 0)
        def _():
            send(b, "dc", b.DW.at[gi], b.RDC.at[yk], yk, yk, p.core)

        @pl.when(lax.rem(k, 2) == 1)
        def _():
            arrived(b, p, "dc", b.RDC.at[yk], yk)
            if g.aligned:

                def to_twin(i):
                    e2 = p.other(i + 1)
                    rows = piece_rows(g, p.od, e2)
                    at = yk * g.ne + e2
                    b.DW[gi, rows, :] = (
                        b.DW[gi, rows, :].astype(F32) + b.RDC[yk, rows, :].astype(F32)
                    ).astype(BF16)
                    send(b, "dx", b.DW.at[gi, rows, :], b.RDX.at[yk, e2], at, at, p.twin)

                loop(g.ne, to_twin)

    loop(4, group)


def inputs_back(g, p, b):
    def rows16(rows):
        normed, inverse = normalize(b.X[rows, :].astype(F32))
        upstream = b.DA[rows, :]
        prod = upstream * normed
        b.GA[0:8, :] += prod[0:8, :] + prod[8:16, :]
        b.GIN[rows, :] = (
            b.GHID[rows, :] + norm_backward(upstream, normed, inverse, b.GN[0:1, :])
        ).astype(BF16)

    rows16s(2 * g.IP, rows16)
    for j in range(2):
        rows = slice(j * g.IP, (j + 1) * g.IP)
        image = 2 * p.c + j
        b.GIN[rows, :] = nn(shift(g, image, True), b.GIN[rows, :]).astype(BF16)
        b.EG[j, 0] = b.GIN[j * g.IP : j * g.IP + 16, :]
        b.EG[j, 1] = b.GIN[(j + 1) * g.IP - 16 : (j + 1) * g.IP, :]
        for name, device in (("i", p.across), ("j", p.core)):
            middle = b.GIN.at[j * g.IP + 16 : (j + 1) * g.IP - 16, :]
            send(b, name + "m", middle, b.o_gin.at[p.y, middle_of(g, image), :], j, j, device)
            send(b, name + "e", b.EG.at[j], b.ED.at[p.y, image], j, j, device)
        b.o_gin[p.y, middle_of(g, image), :] = b.GIN[j * g.IP + 16 : (j + 1) * g.IP - 16, :]
        b.ED[p.y, image] = b.EG[j]


def middle_of(g, image):
    return pl.ds(pl.multiple_of(image * g.WIN + 16, 16), g.WIN - 16)


def inputs_end(g, p, b):
    for j in range(2):
        image = 2 * p.c + j
        middle, edge = b.o_gin.at[p.oy, middle_of(g, image), :], b.ED.at[p.oy, image]
        arrived(b, p, "im", middle, j)
        send(b, "km", middle, middle, j, j, p.core)
        arrived(b, p, "ie", edge, j)
        send(b, "ke", edge, edge, j, j, p.core)


def inputs_last(g, p, b):
    for j in range(2):
        image = 2 * p.oc + j
        for name, yy in (("j", p.y), ("k", p.oy)):
            arrived(b, p, name + "m", b.o_gin.at[yy, middle_of(g, image), :], j)
            arrived(b, p, name + "e", b.ED.at[yy, image], j)
    for blk in range(2):
        b.o_gin[blk, 0:16, :] = b.ED[blk, 0, 0]
        for i in range(1, g.NI):
            b.o_gin[blk, i * g.WIN : i * g.WIN + 16, :] = b.ED[blk, i, 0] + b.ED[blk, i - 1, 1]
        b.o_gin[blk, g.NI * g.WIN : g.NI * g.WIN + 16, :] = b.ED[blk, g.NI - 1, 1]


def weights_back(g, p, b, first, count):
    if not g.aligned:
        if first == 0:
            b.DW[p.hy] = (b.DW[p.hy].astype(F32) + b.RDC[p.oy].astype(F32)).astype(BF16)
            send(b, "dy", b.DW.at[p.hy], b.RDY, 0, 0, p.across)
        return

    def to_across(i):
        e2 = p.other(first + i + 1)
        rows = piece_rows(g, p.d, e2)
        arrived(b, p, "dx", b.RDX.at[p.oy, e2], p.oy * g.ne + e2)
        b.RDX[p.oy, e2] = (
            b.DW[p.hy, rows, :].astype(F32)
            + b.RDC[p.oy, rows, :].astype(F32)
            + b.RDX[p.oy, e2].astype(F32)
        ).astype(BF16)
        send(b, "dy", b.RDX.at[p.oy, e2], b.RDY.at[e2], e2, e2, p.across)

    loop(count, to_across)


def weights_back_on(g, p, b):
    if not g.aligned:
        arrived(b, p, "dy", b.RDY, 0)
        total = b.DW[p.h].astype(F32) + b.RDC[p.y].astype(F32) + b.RDY[...].astype(F32)
        b.o_dw[...] = total.astype(BF16)
        return

    def piece(k):
        e2 = p.other(k + 1)
        rows = piece_rows(g, p.d, e2)
        arrived(b, p, "dx", b.RDX.at[p.y, e2], p.y * g.ne + e2)
        arrived(b, p, "dy", b.RDY.at[e2], e2)
        mine = (
            b.DW[p.h, rows, :].astype(F32)
            + b.RDC[p.y, rows, :].astype(F32)
            + b.RDX[p.y, e2].astype(F32)
            + b.RDY[e2].astype(F32)
        )

        @pl.when(k < g.ne - 1)
        def _():
            b.SDZ[e2] = mine.astype(BF16)
            send(b, "dz", b.SDZ.at[e2], b.RDZ.at[p.e], k, p.e, p.along(e2))

        @pl.when(k == g.ne - 1)
        def _():
            b.o_dw[...] = mine

    loop(g.ne, piece)


def weights_back_end(g, p, b):
    if not g.aligned:
        return

    def add(k):
        e2 = p.other(k + 1)
        arrived(b, p, "dz", b.RDZ.at[e2], e2)
        b.o_dw[...] += b.RDZ[e2].astype(F32)

    loop(g.ne - 1, add)


def small_back(g, p, b):
    sub = iota((128, g.D), 0)
    one = jnp.sum(b.GA[0:8, :], axis=0, keepdims=True)
    two = jnp.sum(b.GA[8:16, :], axis=0, keepdims=True)
    gains = jnp.where(sub == 120, one, jnp.where(sub == 122, two, 0.0))
    b.GM[...] = tn(b.ACT2[...], b.GL[...]) + jnp.transpose(gains)
    if not g.aligned:
        b.SMC[...] = b.GM[...].astype(BF16)
        return
    b.SMX[...] = b.GM[...].astype(BF16)
    mine = p.d * g.ne + p.e

    def to(k):
        for far, d2 in enumerate((p.d, p.od)):
            e2 = p.other(k)
            part = b.SMX.at[piece_rows(g, d2, e2), :]

            @pl.when((k > 0) | (far > 0))
            def _(far=far, d2=d2, e2=e2, part=part):
                send(b, "sp", part, b.RMP.at[mine], far * g.ne + k, mine, (d2, e2, p.h))

    loop(g.ne, to)


def small_back_on(g, p, b):
    if g.aligned:
        mine = p.d * g.ne + p.e
        b.RMP[mine] = b.SMX[piece_rows(g, p.d, p.e), :]

        def come(k):
            for far, d2 in enumerate((p.d, p.od)):
                at = d2 * g.ne + p.other(k)

                @pl.when((k > 0) | (far > 0))
                def _(at=at):
                    arrived(b, p, "sp", b.RMP.at[at], at)

        loop(g.ne, come)
        total = b.RMP[0].astype(F32)
        for i in range(1, g.nd * g.ne):
            total = total + b.RMP[i].astype(F32)
        b.SMC[...] = total.astype(BF16)
    for i, device in enumerate((p.core, p.across, p.diag)):
        send(b, "sh", b.SMC, b.RMH.at[p.h], i, p.h, device)
    b.RMH[p.h] = b.SMC[...]


def small_back_end(g, p, b):
    for h2 in (p.hcore, p.hy, p.hdiag):
        arrived(b, p, "sh", b.RMH.at[h2], h2)
    b.o_small[...] = (b.RMH[0].astype(F32) + b.RMH[1].astype(F32)) + (
        b.RMH[2].astype(F32) + b.RMH[3].astype(F32)
    )


def second_sends_end(g, p, b):
    n = g.ne
    left(b, p, "gi", b.XI, 0)
    left(b, p, "gb", b.XB, 0)

    back_end(g, p, b)

    def away(k):
        if g.aligned:
            left(b, p, "dz", b.SDZ.at[0], k)
            left(b, p, "sp", b.RMP.at[0], k + 1)

    loop(n - 1, away)
    for i in range(2):
        left(b, p, "dc", b.RDC.at[0], i)
        left(b, p, "ug", b.UG.at[0 : g.IP, :], i)
        left(b, p, "uo", b.UO.at[0 : g.IP, :], i)
        for name in ("i", "j", "k"):
            left(b, p, name + "m", b.o_gin.at[0, middle_of(g, 0), :], i)
            left(b, p, name + "e", b.ED.at[0, 0], i)
    if g.aligned:

        def moved(k):
            left(b, p, "sp", b.RMP.at[0], g.ne + k)
            left(b, p, "dx", b.RDX.at[0, 0], k)
            left(b, p, "dx", b.RDX.at[0, 0], g.ne + k)
            left(b, p, "dy", b.RDY.at[0], k)

        loop(n, moved)
    else:
        left(b, p, "dy", b.RDY, 0)
    for i in range(3):
        left(b, p, "sh", b.SMC, i)


def second_kernel(g, b):
    p = Place(g)
    fetch(b, "kRO", b.hRO, b.RB)
    names = ("PT", "PO", "GN", "X", "HID", "PRB", "RW", "UPO", "GC", "W", "QKV", "PB", "ATT", "KI", "KB")
    load(b, *names)
    p.enter(g.aligned)

    def outputs_out(k):
        s = p.other(k + 1)
        send(b, "rc", b.hPO.at[s, :, p.oc], b.RC.at[s], s, s, p.core)

    loop(g.ne, outputs_out)
    grads_of_expert_out(g, p, b)
    fetched(b, "kRO", b.hRO, b.RB)
    slots_back(g, p, b, 1)
    loaded(b, "PT")
    unpack(g, p, b, 1)
    loaded(b, "PO")
    loop(g.ne, lambda k: back_over(g, p, b, b.PO, p.other(k + 1)))
    loaded(b, "GN", "X")
    first_norm_again(g, b)
    unpacked(g, p, b, 1)
    loaded(b, "HID", "PRB", "RW", "UPO")
    tokens_back(g, p, b)
    loaded(b, "W", "QKV", "PB", "ATT", "GC")
    attention_back(g, p, b)
    weights_back(g, p, b, 1, 1)
    inputs_back(g, p, b)
    small_back(g, p, b)
    weights_back(g, p, b, 2, g.ne - 2)
    send(b, "gb", b.hSB, b.XB, 0, 0, p.twin)
    back_in(g, p, b)
    slots_back(g, p, b, 0)
    unpack(g, p, b, 0)
    inputs_end(g, p, b)
    unpacked(g, p, b, 0)
    mix(g, p, b)
    small_back_on(g, p, b)
    weights_back_on(g, p, b)
    mixed_in(g, p, b)
    grads_of_expert_in(g, p, b)
    inputs_last(g, p, b)
    small_back_end(g, p, b)
    weights_back_end(g, p, b)
    second_sends_end(g, p, b)


def call(body, g, inputs, far, outs, far_outs, scratch, sems, number, flops):
    names = [*inputs, *far, *outs, *far_outs, *scratch]
    single = [n for n in sems if n[0] == "k" and n[1].isupper() or n.startswith("ld")]
    names += [name + end for name in sems for end in (("_s",) if name in single else ("_s", "_r"))]

    def kernel(*refs):
        body(g, types.SimpleNamespace(**dict(zip(names, refs, strict=True))))

    vmem, anywhere = pl.BlockSpec(memory_space=pltpu.VMEM), pl.BlockSpec(memory_space=pl.ANY)
    made = pl.pallas_call(
        kernel,
        out_shape=[jax.ShapeDtypeStruct(*o) for o in [*outs.values(), *far_outs.values()]],
        in_specs=[vmem] * len(inputs) + [anywhere] * len(far),
        out_specs=[vmem] * len(outs) + [anywhere] * len(far_outs),
        scratch_shapes=[pltpu.VMEM(*s) for s in scratch.values()]
        + [pltpu.SemaphoreType.DMA((n,)) for name, n in sems.items() for _ in range(1 if name in single else 2)],
        compiler_params=pltpu.CompilerParams(
            collective_id=number, has_side_effects=True, vmem_limit_bytes=LIMIT
        ),
        cost_estimate=pl.CostEstimate(flops=flops, bytes_accessed=2**24, transcendentals=0),
    )(*inputs.values(), *far.values())
    return dict(zip([*outs, *far_outs], made, strict=True))


def shards(
    inputs, w_qkv, w_out, w_router, gain_one, gain_two, w_in, w_back, experts, priority, cotangent, *, mesh
):
    model, rows = inputs.shape[2], inputs.shape[1]
    g = Sizes(mesh, model, rows, w_in.shape[2])
    n, ip, cp, dh = g.ne, g.IP, g.CP, g.DH
    assert inputs.shape[0] == 2
    pad = ((0, 0), (0, 0), (0, ip - SEQ), (0, 0))
    part = jnp.concatenate([w_qkv[:, 0], w_qkv[:, 2], w_qkv[:, 1], w_out.T], axis=1)
    gains = jnp.stack([gain_one, gain_two], axis=1)
    top = gains.astype(BF16)
    rest = (gains - top.astype(F32)).astype(BF16)
    small = jnp.concatenate(
        [
            w_router,
            jnp.zeros((w_router.shape[0], 120 - n), BF16),
            top[:, :1],
            rest[:, :1],
            top[:, 1:],
            rest[:, 1:],
            jnp.zeros((w_router.shape[0], 4), BF16),
        ],
        axis=1,
    )
    if not g.aligned:
        part = lax.all_gather(part, ("dp", "expert"), axis=0, tiled=True)
        small = lax.all_gather(small, ("dp", "expert"), axis=0, tiled=True)
    info = jnp.concatenate([experts, priority[:, :, None]], axis=2).astype(F32)
    info = jnp.pad(info.reshape(2, g.NI, SEQ, 3), pad, constant_values=-1000.0)
    mc = jnp.pad(info.reshape(2, g.TP, 3), ((0, 0), (0, 0), (0, 5)))
    mr = jnp.swapaxes(mc, 1, 2)
    np_ = pieces(g)
    kept = dict(
        X=((2 * ip, model), BF16),
        UPO=((2 * ip, model), BF16),
        W=((4, model, model), BF16),
        RW=((model, 128), BF16),
        GN=((8, model), F32),
        QKV=((4, 2 * ip, 640), BF16),
        PB=((4, 6, ip, ip), BF16),
        ATT=((4, 2 * ip, 256), BF16),
        HID=((2 * ip, model), F32),
        PRB=((2 * ip, 128), F32),
        PT=((g.TP, g.SL), BF16),
        GC=((n, cp, 128), F32),
        PO=((n, 2, 2, cp, dh), BF16),
        RO=((n, cp, dh), BF16),
        KI=((dh, g.F), F32),
        KB=((g.F, dh), F32),
        SI=((dh, g.F), BF16),
        SB=((g.F, dh), BF16),
    )
    assert set(kept) == set(KEEP)
    one = call(
        first_kernel,
        g,
        dict(wp=part, mp=small, wi=w_in[0], wb=w_back[0], mc=mc, mr=mr),
        dict(xin=inputs, uin=cotangent),
        {},
        {"h" + name: made for name, made in kept.items()},
        dict(
            **kept,
            PG=((n, 2, 2, cp, dh), BF16),
            RC=((n, 2, cp, dh), BF16),
            RY=((n, cp, dh), BF16),
            UB=((rows, dh), BF16),
            UPP=((g.TP, dh), BF16),
            DI=((2, dh, g.F), F32),
            DB=((2, g.F, dh), F32),
            MI=((model, 128), BF16),
            L=((g.TP, g.TP), BF16),
            O=((g.TP, 128), BF16),
            P=((g.SL, g.TP), BF16),
            ACT1=((2 * ip, model), BF16),
            ACT2=((2 * ip, model), BF16),
            PRH=((2 * ip, 128), BF16),
            TA=((g.TP, dh), BF16),
            TG=((g.TP, 128), BF16),
            US=((n, 2, 2, cp, dh), BF16),
            XS=((n, 2, 2, cp, dh), BF16),
            PKA=((n, cp, dh), BF16),
            PKU=((n, cp, dh), BF16),
            WI=((2, dh, g.F), BF16),
            WB=((2, g.F, dh), BF16),
            GP=((g.R, model), BF16),
            HQ=((g.R, g.F), BF16),
            GR=((g.R, g.F), BF16),
        ),
        dict(wv=n, wz=n, mz=n, wx=n, mx=n, wy=np_, wc=np_, wd=np_, ta=1, tp=1, uz=n, uy=n, uc=n, ud=n, xz=n, xy=n, xc=n, xd=n, ei=CHUNKS, eb=CHUNKS,
             rc=n, ry=n, rz=n, ldx=2, ldu=2, ldb=1, **{"k" + name: 1 for name in KEEP}),
        1,
        14 * 10**9,
    )
    rows_out = g.PR if g.aligned else model
    extra = (
        dict(
            RDX=((2, n, g.PR, model), BF16),
            SDZ=((n, g.PR, model), BF16),
            RDZ=((n, g.PR, model), BF16),
            SMX=((model, 128), BF16),
            RMP=((g.nd * n, g.PR, 128), BF16),
        )
        if g.aligned
        else {}
    )
    two = call(
        second_kernel,
        g,
        {},
        {"h" + name: one["h" + name] for name in KEEP},
        dict(
            o_mixed=((2, SEQ, model), BF16),
            o_gin=((2, rows, model), BF16),
            o_dw=((rows_out, model), F32 if g.aligned else BF16),
            o_small=((rows_out, 128), F32),
            o_gi=((dh, g.F), F32),
            o_gb=((g.F, dh), F32),
        ),
        {},
        dict(
            **{name: made for name, made in kept.items() if name not in ("SI", "SB", "RO")},
            RO=((n, cp, dh), BF16),
            RB=((n, cp, dh), BF16),
            RC=((n, 2, cp, dh), BF16),
            RY=((n, cp, dh), BF16),
            RG=((g.SL, dh + 128), BF16),
            UG=((2 * ip, dh + 128), BF16),
            UO=((2 * ip, dh), BF16),
            TR=((2, 2 * ip, dh + 128), BF16),
            TO=((2, 2 * ip, dh), BF16),
            MX=((2 * ip, model), BF16),
            MIX=((2, ip, model), BF16),
            EG=((2, 2, 16, model), BF16),
            ED=((2, 4, 2, 16, model), BF16),
            GL=((2 * ip, 128), BF16),
            GA=((16, model), F32),
            ACT1=((2 * ip, model), BF16),
            ACT2=((2 * ip, model), BF16),
            GHID=((2 * ip, model), F32),
            GHL=((2 * ip, model), BF16),
            DA=((2 * ip, model), F32),
            GJ=((2 * ip, 640), BF16),
            DW=((4, model, model), BF16),
            RDC=((2, model, model), BF16),
            RDY=((n, g.PR, model) if g.aligned else (model, model), BF16),
            GIN=((2 * ip, model), BF16),
            GM=((model, 128), F32),
            SMC=((rows_out, 128), BF16),
            RMH=((4, rows_out, 128), BF16),
            XI=((dh, g.F), BF16),
            XB=((g.F, dh), BF16),
            **extra,
        ),
        dict(rc=n, ry=n, rz=n, ug=2, uo=2, mo=2, gi=1, gb=1, dc=2, dy=n, dx=2 * n, dz=n, sp=2 * n, sh=4, im=2, ie=2, jm=2, je=2, km=2, ke=2,
             **{"k" + name: 1 for name in KEEP if name not in ("SI", "SB")}),
        2,
        14 * 10**9,
    )
    dw, ds = two["o_dw"], two["o_small"]
    if not g.aligned:
        dw = lax.psum_scatter(dw, ("dp", "expert"), scatter_dimension=0, tiled=True)
        ds = lax.psum_scatter(ds.astype(BF16), ("dp", "expert"), scatter_dimension=0, tiled=True)
        dw, ds = dw.astype(F32), ds.astype(F32)
    lw = g.LW
    grad_qkv = jnp.stack([dw[:, :lw], dw[:, 2 * lw : 3 * lw], dw[:, lw : 2 * lw]], axis=1)
    return (
        two["o_mixed"],
        two["o_gin"],
        grad_qkv,
        dw[:, 3 * lw :].T,
        ds[:, :n],
        ds[:, 120],
        ds[:, 122],
        two["o_gi"][None],
        two["o_gb"][None],
    )


def solution(mesh):
    both = ("dp", "expert")
    in_specs = (
        P(both, None, None),
        P(both, None, "head"),
        P("head", both),
        P(both, None),
        P(both),
        P(both),
        P("expert", "dp", "head"),
        P("expert", "head", "dp"),
        P(both, None, None),
        P(both, None),
        P(both, None, None),
    )
    out_specs = (
        P(both, "head", None),
        P(both, None, None),
        P(both, None, "head"),
        P("head", both),
        P(both, None),
        P(both),
        P(both),
        P("expert", "dp", "head"),
        P("expert", "head", "dp"),
    )
    return jax.shard_map(
        functools.partial(shards, mesh=mesh),
        mesh=mesh,
        in_specs=in_specs,
        out_specs=out_specs,
        check_vma=False,
    )
```

```python
import functools
import types

import jax
import jax.numpy as jnp
from jax import lax
from jax.experimental import pallas as pl
from jax.experimental.pallas import tpu as pltpu
from jax.sharding import PartitionSpec as P

HD = 64
SEQ = 196
MESH = pl.DeviceIdType.MESH
F32, BF16 = jnp.float32, jnp.bfloat16
LIMIT = 63 * 2**20


def up16(n):
    return -(-n // 16) * 16


def nn(a, b):
    return lax.dot_general(a, b, (((1,), (0,)), ((), ())), preferred_element_type=F32)


def nt(a, b):
    return lax.dot_general(a, b, (((1,), (1,)), ((), ())), preferred_element_type=F32)


def tn(a, b):
    return lax.dot_general(a, b, (((0,), (0,)), ((), ())), preferred_element_type=F32)


def loop(count, body):
    def step(i, carry):
        body(i)
        return carry

    lax.fori_loop(0, count, step, 0)


def iota(shape, dim):
    return lax.broadcasted_iota(jnp.int32, shape, dim)


def fiota(shape, dim):
    return iota(shape, dim).astype(F32)


def normalize(v):
    centered = v - jnp.mean(v, axis=1, keepdims=True)
    inverse = lax.rsqrt(jnp.mean(centered * centered, axis=1, keepdims=True) + 1e-06)
    return centered * inverse, inverse


def norm_backward(upstream, normed, inverse, gain):
    scaled = upstream * gain
    return inverse * (
        scaled
        - jnp.mean(scaled, axis=1, keepdims=True)
        - normed * jnp.mean(scaled * normed, axis=1, keepdims=True)
    )


class Sizes:
    def __init__(self, mesh, model, rows, hidden):
        self.nd, self.ne, self.nh = mesh.shape["dp"], mesh.shape["expert"], mesh.shape["head"]
        self.D, self.DH = model, model // 2
        self.M = rows
        self.CAP = rows // self.ne
        self.CP = up16(self.CAP + 2)
        self.IP = up16(SEQ)
        self.NI = rows // SEQ
        self.TP = self.NI * self.IP
        self.SL = self.ne * self.CP
        self.WIN = self.IP - 16
        self.LAG = SEQ - self.WIN
        self.F = hidden
        self.PR = model // (self.nd * self.ne)
        self.aligned = self.PR % 16 == 0
        self.SG = 1
        while self.SG * 2 * self.CP <= self.IP and self.ne % (self.SG * 2) == 0:
            self.SG *= 2
        self.R = self.SG * 2 * self.CP
        self.LW = model // self.nh
        assert self.nd == 2 and self.nh == 4 and self.NI == 4 and self.LW == 3 * HD
        assert (self.NI - 1) * self.WIN + self.IP <= rows and (self.NI - 1) * self.LAG + SEQ <= self.IP
        assert self.ne & (self.ne - 1) == 0
        assert self.ne <= 64 and 0 <= self.CAP - (self.CP - 16) <= 14


class Place:
    def __init__(self, g):
        self.ne = g.ne
        self.d = lax.axis_index("dp")
        self.e = lax.axis_index("expert")
        self.h = lax.axis_index("head")
        self.y = lax.div(self.h, 2)
        self.c = lax.rem(self.h, 2)
        self.oy, self.oc, self.od = 1 - self.y, 1 - self.c, 1 - self.d
        self.hcore = 2 * self.y + self.oc
        self.hy = 2 * self.oy + self.c
        self.hdiag = 2 * self.oy + self.oc
        self.core = (self.d, self.e, self.hcore)
        self.across = (self.d, self.e, self.hy)
        self.diag = (self.d, self.e, self.hdiag)
        self.twin = (self.od, self.e, self.h)

    def other(self, k):
        index, bit = 0, 1
        while bit < self.ne:
            index = index + lax.rem(lax.div(self.e, bit) + k // bit, 2) * bit
            bit *= 2
        return index

    def along(self, e2):
        return (self.d, e2, self.h)

    def enter(self, wide=False):
        barrier = pltpu.get_barrier_semaphore()

        def tell(device):
            pl.semaphore_signal(barrier, inc=1, device_id=device, device_id_type=MESH)

        for device in (self.core, self.across, self.diag, self.twin):
            tell(device)
        loop(self.ne - 1, lambda k: tell(self.along(self.other(k + 1))))
        if wide:
            loop(self.ne - 1, lambda k: tell((self.od, self.other(k + 1), self.h)))
        pl.semaphore_wait(barrier, 4 + (self.ne - 1) * (2 if wide else 1))


def copy(b, name, src, dst, si, ri, device):
    return pltpu.make_async_remote_copy(
        src_ref=src,
        dst_ref=dst,
        send_sem=getattr(b, name + "_s").at[si],
        recv_sem=getattr(b, name + "_r").at[ri],
        device_id=device,
        device_id_type=MESH,
    )


def send(b, name, src, dst, si, ri, device):
    copy(b, name, src, dst, si, ri, device).start()


def arrived(b, p, name, ref, ri):
    copy(b, name, ref, ref, 0, ri, p.core).wait_recv()


def left(b, p, name, ref, si):
    copy(b, name, ref, ref, si, 0, p.core).wait_send()


def fetch(b, name, src, dst, i=0):
    pltpu.make_async_copy(src, dst, getattr(b, name + "_s").at[i]).start()


def fetched(b, name, src, dst, i=0):
    pltpu.make_async_copy(src, dst, getattr(b, name + "_s").at[i]).wait()


def stow(b, *names):
    for name in names:
        fetch(b, "k" + name, getattr(b, name), getattr(b, "h" + name))


def stowed(b, *names):
    for name in names:
        fetched(b, "k" + name, getattr(b, name), getattr(b, "h" + name))


def load(b, *names):
    for name in names:
        fetch(b, "k" + name, getattr(b, "h" + name), getattr(b, name))


def loaded(b, *names):
    for name in names:
        fetched(b, "k" + name, getattr(b, "h" + name), getattr(b, name))


def shift(g, image, back=False):
    row, col = iota((g.IP, g.IP), 0), iota((g.IP, g.IP), 1)
    if back:
        hot = (row == col + g.LAG * image) & (col < SEQ)
    else:
        hot = (col == row + g.LAG * image) & (row < SEQ)
    return jnp.where(hot, 1.0, 0.0).astype(BF16)


def window(g, image):
    return pl.ds(pl.multiple_of(image * g.WIN, 16), g.IP)


def rows_out(g, p, b):
    for j in range(2):
        rows = slice(j * g.IP, (j + 1) * g.IP)
        fetch(b, "ldx", b.xin.at[p.y, window(g, 2 * p.c + j), :], b.X.at[rows, :], j)
        fetch(b, "ldu", b.uin.at[p.y, window(g, 2 * p.c + j), :], b.UPO.at[rows, :], j)
    fetch(b, "ldb", b.uin.at[p.c, :, half_of(g, p.y)], b.UB)


def rows_in(g, p, b):
    for j in range(2):
        rows = slice(j * g.IP, (j + 1) * g.IP)
        fetched(b, "ldx", b.xin.at[p.y, window(g, 2 * p.c + j), :], b.X.at[rows, :], j)
        fetched(b, "ldu", b.uin.at[p.y, window(g, 2 * p.c + j), :], b.UPO.at[rows, :], j)
        hot = shift(g, 2 * p.c + j)
        b.X[rows, :] = nn(hot, b.X[rows, :]).astype(BF16)
        b.UPO[rows, :] = nn(hot, b.UPO[rows, :]).astype(BF16)
    fetched(b, "ldb", b.uin.at[p.c, :, half_of(g, p.y)], b.UB)
    for i in range(g.NI):
        b.UPP[i * g.IP : (i + 1) * g.IP, :] = nn(
            shift(g, i), b.UB[i * g.WIN : i * g.WIN + g.IP, :]
        ).astype(BF16)


def route(g, b, c, both):
    pr_row, e0r, e1r = b.mr[c, 2:3, :], b.mr[c, 0:1, :], b.mr[c, 1:2, :]
    lane = fiota((g.IP, 128), 1)
    base = jnp.zeros((1, 128), F32)
    for i in range(g.NI):
        rows = slice(i * g.IP, (i + 1) * g.IP)
        col = b.mc[c, rows, :]
        e0c, e1c, prc = col[:, 0:1], col[:, 1:2], col[:, 2:3]
        b.L[rows, :] = jnp.where(pr_row < prc, 1.0, 0.0).astype(BF16)
        b.O[rows, :] = jnp.where((lane == e0c) | (lane == e1c + 64.0), 1.0, 0.0).astype(BF16)
        base = base + jnp.sum(jnp.where(lane == e0c + 64.0, 1.0, 0.0), axis=0, keepdims=True)
    slot_lane = fiota((g.IP, g.SL), 1)
    for i in range(g.NI if both else 0):
        rows = slice(i * g.IP, (i + 1) * g.IP)
        col = b.mc[c, rows, :]
        e0c, e1c = col[:, 0:1], col[:, 1:2]
        own = b.O[rows, :].astype(F32)
        earlier = nn(b.L[rows, :], b.O[...])
        s0 = jnp.sum(jnp.where(lane < 64.0, earlier * own, 0.0), axis=1, keepdims=True)
        s1 = jnp.sum(jnp.where(lane < 64.0, 0.0, (earlier + base) * own), axis=1, keepdims=True)
        t0 = jnp.where(s0 < g.CAP, e0c * g.CP + s0, -1.0)
        t1 = jnp.where(s1 < g.CAP, e1c * g.CP + s1, -1.0)
        b.PT[rows, :] = jnp.where((slot_lane == t0) | (slot_lane == t1), 1.0, 0.0).astype(BF16)
    sub = fiota((128, g.TP), 0)
    own = jnp.where((sub == e0r) | (sub == e1r + 64.0), 1.0, 0.0)
    base = jnp.sum(jnp.where(sub == e0r + 64.0, 1.0, 0.0), axis=1, keepdims=True)
    earlier = nt(own.astype(BF16), b.L[...])
    s0 = jnp.sum(jnp.where(sub < 64.0, earlier * own, 0.0), axis=0, keepdims=True)
    s1 = jnp.sum(jnp.where(sub < 64.0, 0.0, (earlier + base) * own), axis=0, keepdims=True)
    t0 = jnp.where(s0 < g.CAP, e0r * g.CP + s0, -1.0)
    t1 = jnp.where(s1 < g.CAP, e1r * g.CP + s1, -1.0)
    slot_sub = fiota((g.CP, g.TP), 0)

    def fill(e2):
        at = slot_sub + (e2 * g.CP).astype(F32)
        b.P[pl.ds(pl.multiple_of(e2 * g.CP, 16), g.CP), :] = jnp.where(
            (at == t0) | (at == t1), 1.0, 0.0
        ).astype(BF16)

    loop(g.ne, fill)


def pack_rows(g, e2):
    return pl.ds(pl.multiple_of(e2 * g.CP, 16), g.CP)


def piece_rows(g, d, e2):
    return pl.ds(pl.multiple_of((d * g.ne + e2) * g.PR, 16), g.PR)


def weights_out(g, p, b):
    own = piece_rows(g, p.d, p.e)
    if g.aligned:
        mine = p.d * g.ne + p.e

        def to_expert(k):
            device = p.along(p.other(k + 1))
            send(b, "wz", b.wp, b.W.at[p.h, own, :], k, p.e, device)
            send(b, "mz", b.mp, b.MI.at[own, :], k, p.e, device)

        loop(g.ne - 1, to_expert)
        send(b, "wx", b.wp, b.W.at[p.h, own, :], p.e, p.e, p.twin)
        send(b, "mx", b.mp, b.MI.at[own, :], p.e, p.e, p.twin)
        send(b, "wy", b.wp, b.W.at[p.h, own, :], mine, mine, p.across)
        send(b, "wc", b.wp, b.W.at[p.h, own, :], mine, mine, p.core)
        b.W[p.h, own, :] = b.wp[...]
        b.MI[own, :] = b.mp[...]
    else:
        send(b, "wy", b.wp, b.W.at[p.h], 0, 0, p.across)
        send(b, "wc", b.wp, b.W.at[p.h], 0, 0, p.core)
        b.W[p.h] = b.wp[...]
        b.MI[...] = b.mp[...]


def weights_on(g, p, b):
    if not g.aligned:
        return

    def relay(k):
        e2 = p.other(k + 1)
        rows = piece_rows(g, p.d, e2)
        at = p.d * g.ne + e2
        part = b.W.at[p.h, rows, :]
        arrived(b, p, "wz", part, e2)
        send(b, "wx", part, part, e2, e2, p.twin)
        send(b, "wy", part, part, at, at, p.across)
        send(b, "wc", part, part, at, at, p.core)
        part = b.MI.at[rows, :]
        arrived(b, p, "mz", part, e2)
        send(b, "mx", part, part, e2, e2, p.twin)

    loop(g.ne - 1, relay)


def odd(e2):
    return lax.rem(e2, 2) == 1


def weights_end(g, p, b):
    if not g.aligned:
        return

    def relay(k):
        e2 = p.other(k)
        rows = piece_rows(g, p.od, e2)
        at = p.od * g.ne + e2
        part = b.W.at[p.h, rows, :]
        arrived(b, p, "wx", part, e2)

        @pl.when(jnp.logical_not(odd(e2)))
        def _():
            send(b, "wy", part, part, at, at, p.across)

        send(b, "wc", part, part, at, at, p.core)
        arrived(b, p, "mx", b.MI.at[rows, :], e2)

    loop(g.ne, relay)

    def over(k):
        e2 = p.other(k)
        at = p.d * g.ne + e2
        part = b.W.at[p.hy, piece_rows(g, p.d, e2), :]
        arrived(b, p, "wy", part, at)

        @pl.when(odd(e2))
        def _():
            send(b, "wv", part, part, e2, e2, p.twin)

        send(b, "wd", part, part, at, at, p.core)

    loop(g.ne, over)


def pieces(g):
    return g.nd * g.ne if g.aligned else 1


def piece_of(g, ref, group, i):
    if not g.aligned:
        return ref.at[group]
    return ref.at[group, pl.ds(pl.multiple_of(i * g.PR, 16), g.PR), :]


def group_in(g, p, b, k):
    @pl.when(k == 1)
    def _():
        loop(pieces(g), lambda i: arrived(b, p, "wc", piece_of(g, b.W, p.hcore, i), i))

    @pl.when(k == 2)
    def _():
        if not g.aligned:
            arrived(b, p, "wy", b.W.at[p.hy], 0)
            send(b, "wd", b.W.at[p.hy], b.W.at[p.hy], 0, 0, p.core)
            return

        def on(i):
            e2 = p.other(i)
            at = p.od * g.ne + e2
            part = b.W.at[p.hy, piece_rows(g, p.od, e2), :]

            @pl.when(jnp.logical_not(odd(e2)))
            def _():
                arrived(b, p, "wy", part, at)

            @pl.when(odd(e2))
            def _():
                arrived(b, p, "wv", part, e2)

            send(b, "wd", part, part, at, at, p.core)

        loop(g.ne, on)

    @pl.when(k == 3)
    def _():
        loop(pieces(g), lambda i: arrived(b, p, "wd", piece_of(g, b.W, p.hdiag, i), i))


def masks(rows):
    lane = iota((rows, 128), 1)
    return lane < 64, lane >= 64


def attention(g, p, b):
    low, high = masks(g.IP)
    live = iota((g.IP, g.IP), 1) < SEQ
    zero = jnp.zeros((g.IP, 128), BF16)

    def group(k):
        group_in(g, p, b, k)

        @pl.when(k == 3)
        def _():
            part = b.US.at[p.e, p.c, p.y]
            send(b, "uy", part, part, p.e, p.e, p.across)
            send(b, "uc", part, part, p.e, p.e, p.core)
            loop(g.ne - 1, lambda i: cotangent_on(g, p, b, p.other(i + 1)))

        gi = 2 * lax.rem(p.y + lax.div(k, 2), 2) + lax.rem(p.c + k, 2)
        for blk in range(2):
            rows = slice(blk * g.IP, (blk + 1) * g.IP)
            b.QKV[gi, rows, :] = nn(b.ACT1[rows, :], b.W[gi, :, 0:640]).astype(BF16)
        for blk in range(2):
            rows = slice(blk * g.IP, (blk + 1) * g.IP)
            outs = []
            for j in range(3):
                qt = b.QKV[gi, rows, (j // 2) * 128 : (j // 2) * 128 + 128]
                kt = b.QKV[gi, rows, 384 + (j // 2) * 128 : 384 + (j // 2) * 128 + 128]
                vt = b.QKV[gi, rows, 128 + ((j + 1) // 2) * 128 : 256 + ((j + 1) // 2) * 128]
                scores = nt(jnp.where(high if j == 1 else low, qt, zero), kt) * (HD**-0.5)
                scores = jnp.where(live, scores, -1e30)
                scores = jnp.exp(scores - jnp.max(scores, axis=1, keepdims=True))
                probs = (scores / jnp.sum(scores, axis=1, keepdims=True)).astype(BF16)
                b.PB[gi, blk * 3 + j] = probs
                outs.append(nn(probs, vt))
            b.ATT[gi, rows, 0:128] = jnp.where(high, outs[0], 0.0).astype(BF16)
            b.ATT[gi, rows, 128:256] = jnp.where(low, outs[1], outs[2]).astype(BF16)
        for blk in range(2):
            rows = slice(blk * g.IP, (blk + 1) * g.IP)
            b.HID[rows, :] += nt(b.ATT[gi, rows, :], b.W[gi, :, 512:768])

    loop(4, group)


def rows16s(count, body):
    run = count // 32

    def step(i):
        for j in range(run):
            body(pl.ds(pl.multiple_of((i * run + j) * 16, 16), 16))

    loop(2, step)


def first_norm(g, b):
    def rows16(rows):
        x = b.X[rows, :].astype(F32)
        normed, _ = normalize(x)
        b.ACT1[rows, :] = (normed * b.GN[0:1, :]).astype(BF16)
        b.HID[rows, :] = x

    rows16s(2 * g.IP, rows16)


def second_norm(g, b):
    def rows16(rows):
        normed, _ = normalize(b.HID[rows, :])
        b.ACT2[rows, :] = (normed * b.GN[1:2, :]).astype(BF16)

    rows16s(2 * g.IP, rows16)
    lane = iota((g.IP, 128), 1)
    for blk in range(2):
        rows = slice(blk * g.IP, (blk + 1) * g.IP)
        logits = jnp.where(lane < g.ne, nn(b.ACT2[rows, :], b.RW[...]), -1e30)
        weight = jnp.exp(logits - jnp.max(logits, axis=1, keepdims=True))
        probs = weight / jnp.sum(weight, axis=1, keepdims=True)
        b.PRB[rows, :] = probs
        top = probs.astype(BF16).astype(F32)
        rest = probs - top
        b.PRH[rows, :] = (top + pltpu.roll(rest, 64, 1)).astype(BF16)


def small_weights(g, b):
    lane = iota((g.D, 128), 1)
    small = b.MI[...].astype(F32)
    b.RW[...] = jnp.where(lane < g.ne, small, 0.0).astype(BF16)
    gains = jnp.transpose(small)[120:128, :]
    b.GN[0:1, :] = gains[0:1, :] + gains[1:2, :]
    b.GN[1:2, :] = gains[2:3, :] + gains[3:4, :]


def half_of(g, i):
    return pl.ds(pl.multiple_of(i * g.DH, 128), g.DH)


def own_rows(g, c):
    return pl.ds(pl.multiple_of(c * 2 * g.IP, 16), 2 * g.IP)


def tokens_out(g, p, b):
    rows = own_rows(g, p.c)
    send(b, "ta", b.ACT2.at[:, half_of(g, p.oc)], b.TA.at[rows, :], 0, 0, p.core)
    send(b, "tp", b.PRH, b.TG.at[rows, :], 0, 0, p.core)
    b.TA[rows, :] = b.ACT2[:, half_of(g, p.c)]
    b.TG[rows, :] = b.PRH[...]


def tokens_in(g, p, b):
    arrived(b, p, "ta", b.TA.at[own_rows(g, p.oc), :], 0)
    arrived(b, p, "tp", b.TG.at[own_rows(g, p.oc), :], 0)


def cotangent_out(g, p, b):
    def pack(k):
        e2 = p.other(k)
        rows = nn(b.P[pack_rows(g, e2), :], b.UPP[...]).astype(BF16)

        @pl.when(k > 0)
        def _():
            b.PKU[e2] = rows
            send(b, "uz", b.PKU.at[e2], b.US.at[p.e, p.c, p.y], k, p.e, p.along(e2))

        @pl.when(k == 0)
        def _():
            b.US[p.e, p.c, p.y] = rows

    loop(g.ne, pack)


def cotangent_on(g, p, b, e2):
    part = b.US.at[e2, p.c, p.y]
    arrived(b, p, "uz", part, e2)
    send(b, "uy", part, part, e2, e2, p.across)
    send(b, "uc", part, part, e2, e2, p.core)


def cotangent_over(g, p, b, e2):
    part = b.US.at[e2, p.c, p.oy]
    arrived(b, p, "uy", part, e2)
    send(b, "ud", part, part, e2, e2, p.core)


def slots_out(g, p, b):
    row = iota((g.CP, g.DH), 0)
    eye = row == iota((g.CP, g.DH), 1)
    lane = iota((g.CP, 128), 1)

    def pack(k):
        e2 = p.other(k)
        hot = b.P[pack_rows(g, e2), :]
        tok = nn(hot, b.TA[...])
        gates = nn(hot, b.TG[...])
        gate = jnp.sum(
            jnp.where((lane == e2) | (lane == e2 + 64), gates, 0.0), axis=1, keepdims=True
        )
        b.GC[e2] = jnp.broadcast_to(gate, (g.CP, 128))
        across = jnp.sum(jnp.where(eye, gate, 0.0), axis=0, keepdims=True)
        top = across.astype(BF16).astype(F32)
        rows = jnp.where(row == g.CAP, top, jnp.where(row == g.CAP + 1, across - top, tok))
        rows = rows.astype(BF16)

        @pl.when(k > 0)
        def _():
            b.PKA[e2] = rows
            send(b, "xz", b.PKA.at[e2], b.XS.at[p.e, p.y, p.c], k, p.e, p.along(e2))

        @pl.when(k == 0)
        def _():
            part = b.XS.at[p.e, p.y, p.c]
            b.XS[p.e, p.y, p.c] = rows
            send(b, "xy", part, part, p.e, p.e, p.across)
            send(b, "xc", part, part, p.e, p.e, p.core)

    loop(g.ne, pack)


def slots_on(g, p, b, e2):
    part = b.XS.at[e2, p.y, p.c]
    arrived(b, p, "xz", part, e2)
    send(b, "xy", part, part, e2, e2, p.across)
    send(b, "xc", part, part, e2, e2, p.core)


def slots_over(g, p, b, e2):
    part = b.XS.at[e2, p.oy, p.c]
    arrived(b, p, "xy", part, e2)
    send(b, "xd", part, part, e2, e2, p.core)


def slots_in(g, p, b, e2):
    arrived(b, p, "xc", b.XS.at[e2, p.y, p.oc], e2)
    arrived(b, p, "xd", b.XS.at[e2, p.oy, p.oc], e2)
    arrived(b, p, "uc", b.US.at[e2, p.oc, p.y], e2)
    arrived(b, p, "ud", b.US.at[e2, p.oc, p.oy], e2)


CHUNKS = 4


def chunk(rows, i):
    size = rows // CHUNKS
    return pl.ds(i * size, size)


def experts_out(g, p, b, which):
    for i in which:
        name, src, dst = ("ei", b.wi, b.WI) if i < CHUNKS else ("eb", b.wb, b.WB)
        rows = chunk(src.shape[0], i % CHUNKS)
        send(b, name, src.at[rows, :], dst.at[p.d, rows, :], i % CHUNKS, i % CHUNKS, p.twin)


def experts_in(g, p, b):
    for i in range(CHUNKS):
        arrived(b, p, "ei", b.WI.at[p.od, chunk(g.DH, i), :], i)
    for i in range(CHUNKS):
        arrived(b, p, "eb", b.WB.at[p.od, chunk(g.F, i), :], i)


def back_core(g, p, b, part, s):
    send(b, "rc", part.at[s, :, p.oc], b.RC.at[s], s, s, p.core)


def back_over(g, p, b, part, s):
    arrived(b, p, "rc", b.RC.at[s], s)
    b.RC[s, p.oy] = (part[s, p.oy, p.c].astype(F32) + b.RC[s, p.oy].astype(F32)).astype(BF16)
    send(b, "ry", b.RC.at[s, p.oy], b.RY.at[s], s, s, p.across)


def back_on(g, p, b, part, s):
    arrived(b, p, "ry", b.RY.at[s], s)
    total = (
        part[s, p.y, p.c].astype(F32) + b.RC[s, p.y].astype(F32) + b.RY[s].astype(F32)
    ).astype(BF16)

    @pl.when(s != p.e)
    def _():
        b.RC[s, p.y] = total
        send(b, "rz", b.RC.at[s, p.y], b.RO.at[p.e], s, p.e, p.along(s))

    @pl.when(s == p.e)
    def _():
        b.RO[p.e] = total


def back_in(g, p, b):
    def rows_of(k):
        s = p.other(k + 1)
        arrived(b, p, "rz", b.RO.at[s], s)

    loop(g.ne - 1, rows_of)


def back_end(g, p, b):
    def rets(s):
        left(b, p, "rc", b.RC.at[0], s)
        left(b, p, "ry", b.RY.at[0], s)

    loop(g.ne, rets)
    loop(g.ne - 1, lambda k: left(b, p, "rz", b.RY.at[0], p.other(k + 1)))


def gelu_parts(u):
    inner = 0.7978845608028654 * (u + 0.044715 * u * u * u)
    tangent = jnp.tanh(inner)
    value = 0.5 * u * (1.0 + tangent)
    slope = 0.5 * (1.0 + tangent) + 0.5 * u * (1.0 - tangent * tangent) * 0.7978845608028654 * (
        1.0 + 3.0 * 0.044715 * u * u
    )
    return value, slope


def expert(g, b, first, between=None):
    base = g.CP - 16
    row = iota((g.CP, g.DH), 0)
    eye = row == iota((g.CP, g.DH), 1)
    for i in range(g.SG):
        for blk in range(2):
            tail = b.XS[first + i, blk, 0, base:, :].astype(F32)
            gate = tail[g.CAP - base : g.CAP - base + 1] + tail[g.CAP - base + 1 : g.CAP - base + 2]
            gate = jnp.sum(jnp.where(eye, gate, 0.0), axis=1, keepdims=True)
            at = (i * 2 + blk) * g.CP
            for q in range(2):
                b.GP[at : at + g.CP, q * g.DH : (q + 1) * g.DH] = (
                    b.US[first + i, blk, q].astype(F32) * gate
                ).astype(BF16)
    x = [b.XS[pl.ds(first, g.SG), :, q].reshape(g.R, g.DH) for q in range(2)]
    for n in range(g.F // 256):
        cols = slice(n * 256, n * 256 + 256)
        pre = nn(x[0], b.WI[0, :, cols]) + nn(x[1], b.WI[1, :, cols])
        value, slope = gelu_parts(pre)
        b.HQ[:, cols] = value.astype(BF16)
        grad = nt(b.GP[:, : g.DH], b.WB[0, cols, :]) + nt(b.GP[:, g.DH :], b.WB[1, cols, :])
        b.GR[:, cols] = (grad * slope).astype(BF16)
    shape = (g.SG, 2, g.CP, g.DH)
    dots = []
    for q in range(2):
        out = nn(b.HQ[...], b.WB[q]).astype(BF16)
        b.PO[pl.ds(first, g.SG), :, q] = out.reshape(shape)
        up = b.US[pl.ds(first, g.SG), :, q].reshape(g.R, g.DH)
        dots.append(jnp.sum(out.astype(F32) * up.astype(F32), axis=1, keepdims=True))
    dots = dots[0] + dots[1]
    for q in range(2):
        back = nt(b.GR[...], b.WI[q])
        for i in range(g.SG):
            for blk in range(2):
                at = (i * 2 + blk) * g.CP
                along = jnp.sum(jnp.where(eye, dots[at : at + g.CP], 0.0), axis=0, keepdims=True)
                if q == 1:
                    along = along - along.astype(BF16).astype(F32)
                b.PG[first + i, blk, q] = jnp.where(
                    row == g.CAP, along, back[at : at + g.CP]
                ).astype(BF16)
    if between is not None:
        between(0)
    for q in range(2):
        b.DB[q] += tn(b.HQ[...], b.GP[:, q * g.DH : (q + 1) * g.DH])
    if between is not None:
        between(1)
    for q in range(2):
        b.DI[q] += tn(x[q], b.GR[...])


def experts(g, p, b):
    b.DB[...] = jnp.zeros_like(b.DB)
    b.DI[...] = jnp.zeros_like(b.DI)
    n = g.ne
    if g.SG > 1:
        loop(n, lambda k: cotangent_over(g, p, b, p.other(k)))
        loop(n - 1, lambda k: slots_on(g, p, b, p.other(k + 1)))
        loop(n, lambda k: slots_over(g, p, b, p.other(k)))
        loop(n, lambda k: slots_in(g, p, b, p.other(k)))
        experts_in(g, p, b)
        loop(n // g.SG, lambda t: expert(g, b, t * g.SG))
        loop(n, lambda k: back_core(g, p, b, b.PG, p.other(k)))
        loop(n, lambda k: back_over(g, p, b, b.PG, p.other(k)))
        loop(n - 1, lambda k: back_on(g, p, b, b.PG, p.other(k)))
        return
    loop(n, lambda k: cotangent_over(g, p, b, p.other(k)))
    slots_over(g, p, b, p.e)
    slots_in(g, p, b, p.e)
    loop(n - 1, lambda k: slots_on(g, p, b, p.other(k + 1)))
    experts_in(g, p, b)

    def source(k):
        @pl.when(k > 0)
        def _():
            slots_over(g, p, b, p.other(k))
            slots_in(g, p, b, p.other(k))

        def between(step):
            if step == 0:
                back_core(g, p, b, b.PG, p.other(k))

                @pl.when(k > 0)
                def _():
                    back_on(g, p, b, b.PG, p.other(k - 1))
            else:
                back_over(g, p, b, b.PG, p.other(k))

        expert(g, b, p.other(k), between)

    loop(n, source)


def first_sends_end(g, p, b):
    n = g.ne
    if g.aligned:
        own = piece_rows(g, p.d, p.e)

        def z(k):
            left(b, p, "wz", b.wp, k)
            left(b, p, "mz", b.mp, k)

        loop(n - 1, z)

        def x(k):
            left(b, p, "wx", b.wp, k)
            left(b, p, "mx", b.mp, k)

        loop(n, x)

    def w(i):
        for name in ("wc", "wd"):
            left(b, p, name, piece_of(g, b.W, p.h, i), i)

    loop(pieces(g), w)
    if g.aligned:

        def across(e2):
            part = piece_of(g, b.W, p.h, 0)
            left(b, p, "wy", part, p.d * n + e2)

            @pl.when(jnp.logical_not(odd(e2)))
            def _():
                left(b, p, "wy", part, p.od * n + e2)

            @pl.when(odd(e2))
            def _():
                left(b, p, "wv", part, e2)

        loop(n, across)
    else:
        left(b, p, "wy", b.W.at[0], 0)
    left(b, p, "ta", b.TA.at[own_rows(g, 0), :], 0)
    left(b, p, "tp", b.TG.at[own_rows(g, 0), :], 0)

    def slots(k):
        left(b, p, "uz", b.PKU.at[0], k + 1)
        left(b, p, "xz", b.PKA.at[0], k + 1)

    loop(n - 1, slots)

    def on(k):
        for name in ("uy", "uc", "ud"):
            left(b, p, name, b.US.at[0, 0, 0], k)
        for name in ("xy", "xc", "xd"):
            left(b, p, name, b.XS.at[0, 0, 0], k)

    loop(n, on)
    for i in range(CHUNKS):
        left(b, p, "ei", b.wi.at[chunk(g.DH, 0), :], i)
        left(b, p, "eb", b.wb.at[chunk(g.F, 0), :], i)


KEEP = ("X", "UPO", "W", "RW", "GN", "QKV", "PB", "ATT", "HID", "PRB", "PT", "GC", "PO", "RO", "KI", "KB", "SI", "SB")


def first_kernel(g, b):
    p = Place(g)
    rows_out(g, p, b)
    p.enter()
    weights_out(g, p, b)
    b.WI[p.d] = b.wi[...]
    b.WB[p.d] = b.wb[...]
    rows_in(g, p, b)
    route(g, b, p.c, False)
    weights_on(g, p, b)
    cotangent_out(g, p, b)
    weights_end(g, p, b)
    experts_out(g, p, b, range(2 * CHUNKS))
    route(g, b, p.y, True)
    small_weights(g, b)
    first_norm(g, b)
    stow(b, "X", "UPO", "RW", "GN", "PT")
    attention(g, p, b)
    stow(b, "W", "QKV", "PB", "ATT", "HID")
    second_norm(g, b)
    stow(b, "PRB")
    tokens_out(g, p, b)
    tokens_in(g, p, b)
    slots_out(g, p, b)
    stow(b, "GC")
    experts(g, p, b)
    stow(b, "PO")
    b.KI[...] = b.DI[p.d]
    b.KB[...] = b.DB[p.d]
    b.SI[...] = b.DI[p.od].astype(BF16)
    b.SB[...] = b.DB[p.od].astype(BF16)
    stow(b, "KI", "KB", "SI", "SB")
    back_on(g, p, b, b.PG, p.other(g.ne - 1))
    back_in(g, p, b)
    stow(b, "RO")
    first_sends_end(g, p, b)
    back_end(g, p, b)
    stowed(b, *KEEP)


def grads_of_expert_out(g, p, b):
    send(b, "gi", b.hSI, b.XI, 0, 0, p.twin)


def grads_of_expert_in(g, p, b):
    loaded(b, "KI", "KB")
    arrived(b, p, "gi", b.XI, 0)
    b.o_gi[...] = b.KI[...] + b.XI[...].astype(F32)
    arrived(b, p, "gb", b.XB, 0)
    b.o_gb[...] = b.KB[...] + b.XB[...].astype(F32)


def slots_back(g, p, b, kind):
    lane = iota((g.CP, 128), 1)
    base = g.CP - 16
    eye = iota((g.CP, g.DH), 0) == iota((g.CP, g.DH), 1)

    def rows_of(s):
        rows = pack_rows(g, s)
        if kind:
            b.RG[rows, 0 : g.DH] = b.RB[s]
            dots = b.RB[s, base:, :].astype(F32)[g.CAP - base : g.CAP - base + 1]
            dots = jnp.sum(jnp.where(eye, dots, 0.0), axis=1, keepdims=True)
            b.RG[rows, g.DH :] = jnp.where(lane == s, dots, 0.0).astype(BF16)
        else:
            b.RG[rows, 0 : g.DH] = (b.RO[s].astype(F32) * b.GC[s][:, 0:1]).astype(BF16)

    loop(g.ne, rows_of)


def unpack(g, p, b, kind):
    name, width = ("ug", g.DH + 128) if kind else ("uo", g.DH)
    out, landed = (b.UG, b.TR) if kind else (b.UO, b.TO)

    def rows(c, j):
        image = pl.ds(pl.multiple_of((2 * c + j) * g.IP, 16), g.IP)
        return nn(b.PT[image, :], b.RG[:, 0:width]).astype(BF16)

    for j in range(2):
        here = slice(j * g.IP, (j + 1) * g.IP)
        out[here, :] = rows(p.oc, j)
        send(b, name, out.at[here, :], landed.at[p.c, here, :], j, j, p.core)
    for j in range(2):
        landed[p.c, j * g.IP : (j + 1) * g.IP, :] = rows(p.c, j)


def unpacked(g, p, b, kind):
    name, landed = ("ug", b.TR) if kind else ("uo", b.TO)
    for j in range(2):
        arrived(b, p, name, landed.at[p.oc, j * g.IP : (j + 1) * g.IP, :], j)


def mix(g, p, b):
    def rows16(rows):
        for q in range(2):
            cols = slice(q * g.DH, (q + 1) * g.DH)
            b.MX[rows, cols] = (b.HID[rows, cols] + b.TO[q, rows, :].astype(F32)).astype(BF16)

    rows16s(2 * g.IP, rows16)
    for j in range(2):
        part = b.MX.at[j * g.IP : (j + 1) * g.IP, :]
        here = (p.c == p.y) & (p.c == j)

        @pl.when(here)
        def _(j=j):
            b.MIX[p.y] = b.MX[j * g.IP : (j + 1) * g.IP, :]

        @pl.when(jnp.logical_not(here))
        def _(j=j, part=part):
            send(b, "mo", part, b.MIX.at[p.y], j, p.y, (p.d, p.e, 2 * p.c + j))


def mixed_in(g, p, b):
    for blk in range(2):

        @pl.when(jnp.logical_not((p.y == blk) & (p.c == p.y)))
        def _(blk=blk):
            arrived(b, p, "mo", b.MIX.at[blk], blk)

        b.o_mixed[blk] = b.MIX[blk, 0:SEQ, :]
    for j in range(2):

        @pl.when(jnp.logical_not((p.c == p.y) & (p.c == j)))
        def _(j=j):
            left(b, p, "mo", b.MIX.at[0], j)


def tokens_back(g, p, b):
    lane = iota((g.IP, 128), 1)
    b.GA[...] = jnp.zeros_like(b.GA)
    for blk in range(2):
        rows = slice(blk * g.IP, (blk + 1) * g.IP)
        gate = b.TR[0, rows, g.DH :].astype(F32) + b.TR[1, rows, g.DH :].astype(F32)
        probs = b.PRB[rows, :]
        grad = probs * (gate - jnp.sum(probs * gate, axis=1, keepdims=True))
        b.GL[rows, :] = grad.astype(BF16)
        b.GHID[rows, :] = nt(b.GL[rows, :], b.RW[...])

    def rows16(rows):
        normed, inverse = normalize(b.HID[rows, :])
        upstream = b.GHID[rows, :] + jnp.concatenate(
            [b.TR[q, rows, 0 : g.DH].astype(F32) for q in range(2)], axis=1
        )
        prod = upstream * normed
        b.GA[8:16, :] += prod[0:8, :] + prod[8:16, :]
        b.ACT2[rows, :] = (normed * b.GN[1:2, :]).astype(BF16)
        hidden = b.UPO[rows, :].astype(F32) + norm_backward(upstream, normed, inverse, b.GN[1:2, :])
        b.GHID[rows, :] = hidden
        b.GHL[rows, :] = hidden.astype(BF16)

    rows16s(2 * g.IP, rows16)


def first_norm_again(g, b):
    def rows16(rows):
        normed, _ = normalize(b.X[rows, :].astype(F32))
        b.ACT1[rows, :] = (normed * b.GN[0:1, :]).astype(BF16)

    rows16s(2 * g.IP, rows16)


def attention_back(g, p, b):
    low, high = masks(g.IP)
    zero = jnp.zeros((g.IP, 128), BF16)
    scale = HD**-0.5
    b.DA[...] = jnp.zeros_like(b.DA)

    def group(k):
        @pl.when(k == 2)
        def _():
            loop(g.ne // 2, lambda i: back_on(g, p, b, b.PO, p.other(i + 1)))

        @pl.when(k == 3)
        def _():
            loop(g.ne - g.ne // 2, lambda i: back_on(g, p, b, b.PO, p.other(i + g.ne // 2 + 1)))
            weights_back(g, p, b, 0, 1)

        yk = lax.rem(p.oy + lax.div(k, 2), 2)
        gi = 2 * yk + lax.rem(p.oc + k, 2)
        for blk in range(2):
            rows = slice(blk * g.IP, (blk + 1) * g.IP)
            grad = nn(b.GHL[rows, :], b.W[gi, :, 512:768]).astype(BF16)
            tiles = [grad[:, 0:128], grad[:, 128:256]]
            dq, dk, dv = [], [], []
            for j in range(3):
                probs = b.PB[gi, blk * 3 + j]
                gt = tiles[(j + 1) // 2]
                qt = b.QKV[gi, rows, (j // 2) * 128 : (j // 2) * 128 + 128]
                kt = b.QKV[gi, rows, 384 + (j // 2) * 128 : 384 + (j // 2) * 128 + 128]
                vt = b.QKV[gi, rows, 128 + ((j + 1) // 2) * 128 : 256 + ((j + 1) // 2) * 128]
                grad_probs = nt(jnp.where(low if j == 1 else high, gt, zero), vt)
                wide = probs.astype(F32)
                grad_scores = wide * (
                    grad_probs - jnp.sum(wide * grad_probs, axis=1, keepdims=True)
                )
                grad_scores = (grad_scores * scale).astype(BF16)
                dv.append(tn(probs, gt))
                dq.append(nn(grad_scores, kt))
                dk.append(tn(grad_scores, qt))
            b.GJ[rows, 0:128] = jnp.where(low, dq[0], dq[1]).astype(BF16)
            b.GJ[rows, 128:256] = jnp.where(low, dq[2], dv[0]).astype(BF16)
            b.GJ[rows, 256:384] = jnp.where(low, dv[1], dv[2]).astype(BF16)
            b.GJ[rows, 384:512] = jnp.where(low, dk[0], dk[1]).astype(BF16)
            b.GJ[rows, 512:640] = jnp.where(low, dk[2], 0.0).astype(BF16)
        for blk in range(2):
            rows = slice(blk * g.IP, (blk + 1) * g.IP)
            b.DA[rows, :] += nt(b.GJ[rows, :], b.W[gi, :, 0:640])
        for m in range(g.D // 256):
            cols = slice(m * 256, m * 256 + 256)
            first = tn(b.ACT1[:, cols], b.GJ[...])
            second = tn(b.GHL[:, cols], b.ATT[gi])
            b.DW[gi, cols, 0:512] = first[:, 0:512].astype(BF16)
            b.DW[gi, cols, 512:640] = (first[:, 512:] + second[:, 0:128]).astype(BF16)
            b.DW[gi, cols, 640:768] = second[:, 128:].astype(BF16)

        @pl.when(lax.rem(k, 2) == 0)
        def _():
            send(b, "dc", b.DW.at[gi], b.RDC.at[yk], yk, yk, p.core)

        @pl.when(lax.rem(k, 2) == 1)
        def _():
            arrived(b, p, "dc", b.RDC.at[yk], yk)
            if g.aligned:

                def to_twin(i):
                    e2 = p.other(i + 1)
                    rows = piece_rows(g, p.od, e2)
                    at = yk * g.ne + e2
                    b.DW[gi, rows, :] = (
                        b.DW[gi, rows, :].astype(F32) + b.RDC[yk, rows, :].astype(F32)
                    ).astype(BF16)
                    send(b, "dx", b.DW.at[gi, rows, :], b.RDX.at[yk, e2], at, at, p.twin)

                loop(g.ne, to_twin)

    loop(4, group)


def inputs_back(g, p, b):
    def rows16(rows):
        normed, inverse = normalize(b.X[rows, :].astype(F32))
        upstream = b.DA[rows, :]
        prod = upstream * normed
        b.GA[0:8, :] += prod[0:8, :] + prod[8:16, :]
        b.GIN[rows, :] = (
            b.GHID[rows, :] + norm_backward(upstream, normed, inverse, b.GN[0:1, :])
        ).astype(BF16)

    rows16s(2 * g.IP, rows16)
    for j in range(2):
        rows = slice(j * g.IP, (j + 1) * g.IP)
        image = 2 * p.c + j
        b.GIN[rows, :] = nn(shift(g, image, True), b.GIN[rows, :]).astype(BF16)
        b.EG[j, 0] = b.GIN[j * g.IP : j * g.IP + 16, :]
        b.EG[j, 1] = b.GIN[(j + 1) * g.IP - 16 : (j + 1) * g.IP, :]
        for name, device in (("i", p.across), ("j", p.core)):
            middle = b.GIN.at[j * g.IP + 16 : (j + 1) * g.IP - 16, :]
            send(b, name + "m", middle, b.o_gin.at[p.y, middle_of(g, image), :], j, j, device)
            send(b, name + "e", b.EG.at[j], b.ED.at[p.y, image], j, j, device)
        b.o_gin[p.y, middle_of(g, image), :] = b.GIN[j * g.IP + 16 : (j + 1) * g.IP - 16, :]
        b.ED[p.y, image] = b.EG[j]


def middle_of(g, image):
    return pl.ds(pl.multiple_of(image * g.WIN + 16, 16), g.WIN - 16)


def inputs_end(g, p, b):
    for j in range(2):
        image = 2 * p.c + j
        middle, edge = b.o_gin.at[p.oy, middle_of(g, image), :], b.ED.at[p.oy, image]
        arrived(b, p, "im", middle, j)
        send(b, "km", middle, middle, j, j, p.core)
        arrived(b, p, "ie", edge, j)
        send(b, "ke", edge, edge, j, j, p.core)


def inputs_last(g, p, b):
    for j in range(2):
        image = 2 * p.oc + j
        for name, yy in (("j", p.y), ("k", p.oy)):
            arrived(b, p, name + "m", b.o_gin.at[yy, middle_of(g, image), :], j)
            arrived(b, p, name + "e", b.ED.at[yy, image], j)
    for blk in range(2):
        b.o_gin[blk, 0:16, :] = b.ED[blk, 0, 0]
        for i in range(1, g.NI):
            b.o_gin[blk, i * g.WIN : i * g.WIN + 16, :] = b.ED[blk, i, 0] + b.ED[blk, i - 1, 1]
        b.o_gin[blk, g.NI * g.WIN : g.NI * g.WIN + 16, :] = b.ED[blk, g.NI - 1, 1]


def weights_back(g, p, b, first, count):
    if not g.aligned:
        if first == 0:
            b.DW[p.hy] = (b.DW[p.hy].astype(F32) + b.RDC[p.oy].astype(F32)).astype(BF16)
            send(b, "dy", b.DW.at[p.hy], b.RDY, 0, 0, p.across)
        return

    def to_across(i):
        e2 = p.other(first + i + 1)
        rows = piece_rows(g, p.d, e2)
        arrived(b, p, "dx", b.RDX.at[p.oy, e2], p.oy * g.ne + e2)
        b.RDX[p.oy, e2] = (
            b.DW[p.hy, rows, :].astype(F32)
            + b.RDC[p.oy, rows, :].astype(F32)
            + b.RDX[p.oy, e2].astype(F32)
        ).astype(BF16)
        send(b, "dy", b.RDX.at[p.oy, e2], b.RDY.at[e2], e2, e2, p.across)

    loop(count, to_across)


def weights_back_on(g, p, b):
    if not g.aligned:
        arrived(b, p, "dy", b.RDY, 0)
        total = b.DW[p.h].astype(F32) + b.RDC[p.y].astype(F32) + b.RDY[...].astype(F32)
        b.o_dw[...] = total.astype(BF16)
        return

    def piece(k):
        e2 = p.other(k + 1)
        rows = piece_rows(g, p.d, e2)
        arrived(b, p, "dx", b.RDX.at[p.y, e2], p.y * g.ne + e2)
        arrived(b, p, "dy", b.RDY.at[e2], e2)
        mine = (
            b.DW[p.h, rows, :].astype(F32)
            + b.RDC[p.y, rows, :].astype(F32)
            + b.RDX[p.y, e2].astype(F32)
            + b.RDY[e2].astype(F32)
        )

        @pl.when(k < g.ne - 1)
        def _():
            b.SDZ[e2] = mine.astype(BF16)
            send(b, "dz", b.SDZ.at[e2], b.RDZ.at[p.e], k, p.e, p.along(e2))

        @pl.when(k == g.ne - 1)
        def _():
            b.o_dw[...] = mine

    loop(g.ne, piece)


def weights_back_end(g, p, b):
    if not g.aligned:
        return

    def add(k):
        e2 = p.other(k + 1)
        arrived(b, p, "dz", b.RDZ.at[e2], e2)
        b.o_dw[...] += b.RDZ[e2].astype(F32)

    loop(g.ne - 1, add)


def small_back(g, p, b):
    sub = iota((128, g.D), 0)
    one = jnp.sum(b.GA[0:8, :], axis=0, keepdims=True)
    two = jnp.sum(b.GA[8:16, :], axis=0, keepdims=True)
    gains = jnp.where(sub == 120, one, jnp.where(sub == 122, two, 0.0))
    b.GM[...] = tn(b.ACT2[...], b.GL[...]) + jnp.transpose(gains)
    if not g.aligned:
        b.SMC[...] = b.GM[...].astype(BF16)
        return
    b.SMX[...] = b.GM[...].astype(BF16)
    mine = p.d * g.ne + p.e

    def to(k):
        for far, d2 in enumerate((p.d, p.od)):
            e2 = p.other(k)
            part = b.SMX.at[piece_rows(g, d2, e2), :]

            @pl.when((k > 0) | (far > 0))
            def _(far=far, d2=d2, e2=e2, part=part):
                send(b, "sp", part, b.RMP.at[mine], far * g.ne + k, mine, (d2, e2, p.h))

    loop(g.ne, to)


def small_back_on(g, p, b):
    if g.aligned:
        mine = p.d * g.ne + p.e
        b.RMP[mine] = b.SMX[piece_rows(g, p.d, p.e), :]

        def come(k):
            for far, d2 in enumerate((p.d, p.od)):
                at = d2 * g.ne + p.other(k)

                @pl.when((k > 0) | (far > 0))
                def _(at=at):
                    arrived(b, p, "sp", b.RMP.at[at], at)

        loop(g.ne, come)
        total = b.RMP[0].astype(F32)
        for i in range(1, g.nd * g.ne):
            total = total + b.RMP[i].astype(F32)
        b.SMC[...] = total.astype(BF16)
    for i, device in enumerate((p.core, p.across, p.diag)):
        send(b, "sh", b.SMC, b.RMH.at[p.h], i, p.h, device)
    b.RMH[p.h] = b.SMC[...]


def small_back_end(g, p, b):
    for h2 in (p.hcore, p.hy, p.hdiag):
        arrived(b, p, "sh", b.RMH.at[h2], h2)
    b.o_small[...] = (b.RMH[0].astype(F32) + b.RMH[1].astype(F32)) + (
        b.RMH[2].astype(F32) + b.RMH[3].astype(F32)
    )


def second_sends_end(g, p, b):
    n = g.ne
    left(b, p, "gi", b.XI, 0)
    left(b, p, "gb", b.XB, 0)

    back_end(g, p, b)

    def away(k):
        if g.aligned:
            left(b, p, "dz", b.SDZ.at[0], k)
            left(b, p, "sp", b.RMP.at[0], k + 1)

    loop(n - 1, away)
    for i in range(2):
        left(b, p, "dc", b.RDC.at[0], i)
        left(b, p, "ug", b.UG.at[0 : g.IP, :], i)
        left(b, p, "uo", b.UO.at[0 : g.IP, :], i)
        for name in ("i", "j", "k"):
            left(b, p, name + "m", b.o_gin.at[0, middle_of(g, 0), :], i)
            left(b, p, name + "e", b.ED.at[0, 0], i)
    if g.aligned:

        def moved(k):
            left(b, p, "sp", b.RMP.at[0], g.ne + k)
            left(b, p, "dx", b.RDX.at[0, 0], k)
            left(b, p, "dx", b.RDX.at[0, 0], g.ne + k)
            left(b, p, "dy", b.RDY.at[0], k)

        loop(n, moved)
    else:
        left(b, p, "dy", b.RDY, 0)
    for i in range(3):
        left(b, p, "sh", b.SMC, i)


def second_kernel(g, b):
    p = Place(g)
    fetch(b, "kRO", b.hRO, b.RB)
    names = ("PT", "PO", "GN", "X", "HID", "PRB", "RW", "UPO", "GC", "W", "QKV", "PB", "ATT", "KI", "KB")
    load(b, *names)
    p.enter(g.aligned)

    def outputs_out(k):
        s = p.other(k + 1)
        send(b, "rc", b.hPO.at[s, :, p.oc], b.RC.at[s], s, s, p.core)

    loop(g.ne, outputs_out)
    grads_of_expert_out(g, p, b)
    fetched(b, "kRO", b.hRO, b.RB)
    slots_back(g, p, b, 1)
    loaded(b, "PT")
    unpack(g, p, b, 1)
    loaded(b, "PO")
    loop(g.ne, lambda k: back_over(g, p, b, b.PO, p.other(k + 1)))
    loaded(b, "GN", "X")
    first_norm_again(g, b)
    unpacked(g, p, b, 1)
    loaded(b, "HID", "PRB", "RW", "UPO")
    tokens_back(g, p, b)
    loaded(b, "W", "QKV", "PB", "ATT", "GC")
    attention_back(g, p, b)
    weights_back(g, p, b, 1, 1)
    inputs_back(g, p, b)
    small_back(g, p, b)
    weights_back(g, p, b, 2, g.ne - 2)
    send(b, "gb", b.hSB, b.XB, 0, 0, p.twin)
    back_in(g, p, b)
    slots_back(g, p, b, 0)
    unpack(g, p, b, 0)
    inputs_end(g, p, b)
    unpacked(g, p, b, 0)
    mix(g, p, b)
    small_back_on(g, p, b)
    weights_back_on(g, p, b)
    mixed_in(g, p, b)
    grads_of_expert_in(g, p, b)
    inputs_last(g, p, b)
    small_back_end(g, p, b)
    weights_back_end(g, p, b)
    second_sends_end(g, p, b)


def call(body, g, inputs, far, outs, far_outs, scratch, sems, number, flops):
    names = [*inputs, *far, *outs, *far_outs, *scratch]
    single = [n for n in sems if n[0] == "k" and n[1].isupper() or n.startswith("ld")]
    names += [name + end for name in sems for end in (("_s",) if name in single else ("_s", "_r"))]

    def kernel(*refs):
        body(g, types.SimpleNamespace(**dict(zip(names, refs, strict=True))))

    vmem, anywhere = pl.BlockSpec(memory_space=pltpu.VMEM), pl.BlockSpec(memory_space=pl.ANY)
    made = pl.pallas_call(
        kernel,
        out_shape=[jax.ShapeDtypeStruct(*o) for o in [*outs.values(), *far_outs.values()]],
        in_specs=[vmem] * len(inputs) + [anywhere] * len(far),
        out_specs=[vmem] * len(outs) + [anywhere] * len(far_outs),
        scratch_shapes=[pltpu.VMEM(*s) for s in scratch.values()]
        + [pltpu.SemaphoreType.DMA((n,)) for name, n in sems.items() for _ in range(1 if name in single else 2)],
        compiler_params=pltpu.CompilerParams(
            collective_id=number, has_side_effects=True, vmem_limit_bytes=LIMIT
        ),
        cost_estimate=pl.CostEstimate(flops=flops, bytes_accessed=2**24, transcendentals=0),
    )(*inputs.values(), *far.values())
    return dict(zip([*outs, *far_outs], made, strict=True))


def shards(
    inputs, w_qkv, w_out, w_router, gain_one, gain_two, w_in, w_back, experts, priority, cotangent, *, mesh
):
    model, rows = inputs.shape[2], inputs.shape[1]
    g = Sizes(mesh, model, rows, w_in.shape[2])
    n, ip, cp, dh = g.ne, g.IP, g.CP, g.DH
    assert inputs.shape[0] == 2
    pad = ((0, 0), (0, 0), (0, ip - SEQ), (0, 0))
    part = jnp.concatenate([w_qkv[:, 0], w_qkv[:, 2], w_qkv[:, 1], w_out.T], axis=1)
    gains = jnp.stack([gain_one, gain_two], axis=1)
    top = gains.astype(BF16)
    rest = (gains - top.astype(F32)).astype(BF16)
    small = jnp.concatenate(
        [
            w_router,
            jnp.zeros((w_router.shape[0], 120 - n), BF16),
            top[:, :1],
            rest[:, :1],
            top[:, 1:],
            rest[:, 1:],
            jnp.zeros((w_router.shape[0], 4), BF16),
        ],
        axis=1,
    )
    if not g.aligned:
        part = lax.all_gather(part, ("dp", "expert"), axis=0, tiled=True)
        small = lax.all_gather(small, ("dp", "expert"), axis=0, tiled=True)
    info = jnp.concatenate([experts, priority[:, :, None]], axis=2).astype(F32)
    info = jnp.pad(info.reshape(2, g.NI, SEQ, 3), pad, constant_values=-1000.0)
    mc = jnp.pad(info.reshape(2, g.TP, 3), ((0, 0), (0, 0), (0, 5)))
    mr = jnp.swapaxes(mc, 1, 2)
    np_ = pieces(g)
    kept = dict(
        X=((2 * ip, model), BF16),
        UPO=((2 * ip, model), BF16),
        W=((4, model, model), BF16),
        RW=((model, 128), BF16),
        GN=((8, model), F32),
        QKV=((4, 2 * ip, 640), BF16),
        PB=((4, 6, ip, ip), BF16),
        ATT=((4, 2 * ip, 256), BF16),
        HID=((2 * ip, model), F32),
        PRB=((2 * ip, 128), F32),
        PT=((g.TP, g.SL), BF16),
        GC=((n, cp, 128), F32),
        PO=((n, 2, 2, cp, dh), BF16),
        RO=((n, cp, dh), BF16),
        KI=((dh, g.F), F32),
        KB=((g.F, dh), F32),
        SI=((dh, g.F), BF16),
        SB=((g.F, dh), BF16),
    )
    assert set(kept) == set(KEEP)
    one = call(
        first_kernel,
        g,
        dict(wp=part, mp=small, wi=w_in[0], wb=w_back[0], mc=mc, mr=mr),
        dict(xin=inputs, uin=cotangent),
        {},
        {"h" + name: made for name, made in kept.items()},
        dict(
            **kept,
            PG=((n, 2, 2, cp, dh), BF16),
            RC=((n, 2, cp, dh), BF16),
            RY=((n, cp, dh), BF16),
            UB=((rows, dh), BF16),
            UPP=((g.TP, dh), BF16),
            DI=((2, dh, g.F), F32),
            DB=((2, g.F, dh), F32),
            MI=((model, 128), BF16),
            L=((g.TP, g.TP), BF16),
            O=((g.TP, 128), BF16),
            P=((g.SL, g.TP), BF16),
            ACT1=((2 * ip, model), BF16),
            ACT2=((2 * ip, model), BF16),
            PRH=((2 * ip, 128), BF16),
            TA=((g.TP, dh), BF16),
            TG=((g.TP, 128), BF16),
            US=((n, 2, 2, cp, dh), BF16),
            XS=((n, 2, 2, cp, dh), BF16),
            PKA=((n, cp, dh), BF16),
            PKU=((n, cp, dh), BF16),
            WI=((2, dh, g.F), BF16),
            WB=((2, g.F, dh), BF16),
            GP=((g.R, model), BF16),
            HQ=((g.R, g.F), BF16),
            GR=((g.R, g.F), BF16),
        ),
        dict(wv=n, wz=n, mz=n, wx=n, mx=n, wy=np_, wc=np_, wd=np_, ta=1, tp=1, uz=n, uy=n, uc=n, ud=n, xz=n, xy=n, xc=n, xd=n, ei=CHUNKS, eb=CHUNKS,
             rc=n, ry=n, rz=n, ldx=2, ldu=2, ldb=1, **{"k" + name: 1 for name in KEEP}),
        1,
        14 * 10**9,
    )
    rows_out = g.PR if g.aligned else model
    extra = (
        dict(
            RDX=((2, n, g.PR, model), BF16),
            SDZ=((n, g.PR, model), BF16),
            RDZ=((n, g.PR, model), BF16),
            SMX=((model, 128), BF16),
            RMP=((g.nd * n, g.PR, 128), BF16),
        )
        if g.aligned
        else {}
    )
    two = call(
        second_kernel,
        g,
        {},
        {"h" + name: one["h" + name] for name in KEEP},
        dict(
            o_mixed=((2, SEQ, model), BF16),
            o_gin=((2, rows, model), BF16),
            o_dw=((rows_out, model), F32 if g.aligned else BF16),
            o_small=((rows_out, 128), F32),
            o_gi=((dh, g.F), F32),
            o_gb=((g.F, dh), F32),
        ),
        {},
        dict(
            **{name: made for name, made in kept.items() if name not in ("SI", "SB", "RO")},
            RO=((n, cp, dh), BF16),
            RB=((n, cp, dh), BF16),
            RC=((n, 2, cp, dh), BF16),
            RY=((n, cp, dh), BF16),
            RG=((g.SL, dh + 128), BF16),
            UG=((2 * ip, dh + 128), BF16),
            UO=((2 * ip, dh), BF16),
            TR=((2, 2 * ip, dh + 128), BF16),
            TO=((2, 2 * ip, dh), BF16),
            MX=((2 * ip, model), BF16),
            MIX=((2, ip, model), BF16),
            EG=((2, 2, 16, model), BF16),
            ED=((2, 4, 2, 16, model), BF16),
            GL=((2 * ip, 128), BF16),
            GA=((16, model), F32),
            ACT1=((2 * ip, model), BF16),
            ACT2=((2 * ip, model), BF16),
            GHID=((2 * ip, model), F32),
            GHL=((2 * ip, model), BF16),
            DA=((2 * ip, model), F32),
            GJ=((2 * ip, 640), BF16),
            DW=((4, model, model), BF16),
            RDC=((2, model, model), BF16),
            RDY=((n, g.PR, model) if g.aligned else (model, model), BF16),
            GIN=((2 * ip, model), BF16),
            GM=((model, 128), F32),
            SMC=((rows_out, 128), BF16),
            RMH=((4, rows_out, 128), BF16),
            XI=((dh, g.F), BF16),
            XB=((g.F, dh), BF16),
            **extra,
        ),
        dict(rc=n, ry=n, rz=n, ug=2, uo=2, mo=2, gi=1, gb=1, dc=2, dy=n, dx=2 * n, dz=n, sp=2 * n, sh=4, im=2, ie=2, jm=2, je=2, km=2, ke=2,
             **{"k" + name: 1 for name in KEEP if name not in ("SI", "SB")}),
        2,
        14 * 10**9,
    )
    dw, ds = two["o_dw"], two["o_small"]
    if not g.aligned:
        dw = lax.psum_scatter(dw, ("dp", "expert"), scatter_dimension=0, tiled=True)
        ds = lax.psum_scatter(ds.astype(BF16), ("dp", "expert"), scatter_dimension=0, tiled=True)
        dw, ds = dw.astype(F32), ds.astype(F32)
    lw = g.LW
    grad_qkv = jnp.stack([dw[:, :lw], dw[:, 2 * lw : 3 * lw], dw[:, lw : 2 * lw]], axis=1)
    return (
        two["o_mixed"],
        two["o_gin"],
        grad_qkv,
        dw[:, 3 * lw :].T,
        ds[:, :n],
        ds[:, 120],
        ds[:, 122],
        two["o_gi"][None],
        two["o_gb"][None],
    )


def solution(mesh):
    both = ("dp", "expert")
    in_specs = (
        P(both, None, None),
        P(both, None, "head"),
        P("head", both),
        P(both, None),
        P(both),
        P(both),
        P("expert", "dp", "head"),
        P("expert", "head", "dp"),
        P(both, None, None),
        P(both, None),
        P(both, None, None),
    )
    out_specs = (
        P(both, "head", None),
        P(both, None, None),
        P(both, None, "head"),
        P("head", both),
        P(both, None),
        P(both),
        P(both),
        P("expert", "dp", "head"),
        P("expert", "head", "dp"),
    )
    return jax.shard_map(
        functools.partial(shards, mesh=mesh),
        mesh=mesh,
        in_specs=in_specs,
        out_specs=out_specs,
        check_vma=False,
    )
```
